512 devices in a mesh: dp: 32 (over x, z_lo, core), tensor: 16 (over z_hi, y).
Axes of the slice: x: 4, y: 8, z: 8 (z_hi: 2, z_lo: 4; z = z_hi * 4 + z_lo), core: 2. Of those that a mesh axis runs over, the one named last changes fastest.
Arguments:
- x_inner: bfloat16 [32, 256, 16384], P('dp', None, 'tensor'), may hold values from -6 to 6
- proj_dt: bfloat16 [32, 256, 512], P('dp', 'tensor'), may hold values from -6 to 6
- proj_bc: bfloat16 [32, 256, 32], P('dp', 'tensor'), may hold values from -6 to 6
- grad_y: bfloat16 [32, 256, 16384], P('dp', None, 'tensor'), may hold values from -6 to 6
- w_xdt: bfloat16 [512, 16384], P(None, 'tensor'), may hold values from -0.046875 to 0.046875
- w_xbc: bfloat16 [32, 16384], P(None, 'tensor'), may hold values from -0.046875 to 0.046875
- w_dt: bfloat16 [512, 16384], P(None, 'tensor'), may hold values from -0.25 to 0.25
- dt_bias: float32 [16384], P('tensor'), may hold values from -6 to -2.5
- a_log: float32 [16, 16384], P(None, 'tensor'), may hold values from -0.7 to 2.8
- d_skip: float32 [16384], P('tensor'), may hold values from 0.5 to 1.5
- dt_gain: float32 [512], replicated, may hold values from 0.25 to 1.75
- bc_gain: float32 [32], replicated, may hold values from 0.25 to 1.75
Outputs:
- grad_x: bfloat16 [32, 256, 16384], P('dp', None, 'tensor')
- grad_w_xdt: float32 [512, 16384], P('dp', 'tensor')
- grad_w_dt: float32 [512, 16384], P('dp', 'tensor')
- grad_w_xbc: float32 [32, 16384], P(None, 'tensor')
- grad_a_log: float32 [16, 16384], P(None, 'tensor')
- grad_dt_bias: float32 [16384], P('tensor')
- grad_d_skip: float32 [16384], P('tensor')
- grad_dt_gain: float32 [512], replicated
- grad_bc_gain: float32 [32], replicated
The draws below stay inside these ranges and needn't reach their ends.
All inputs are finite; a program needn't handle non-finite values.
Results may differ from the reference program's by a relative error of at most 0.0059.
Values may be sent and summed in bfloat16 or wider, within the bound.
No kernel may reach another device: no remote copies, remote signals or barrier semaphores. Data moves between devices by JAX's collectives and lax.ppermute only.
A program may use at most 128 MiB of HBM per device.

```python
import math
import jax
import jax.numpy as jnp
from jax import lax

INNER = 16384
STATE = 16
RANK = 512
SEQ_LEN = 256
BATCH = 32


def block_levels(stream_key, dims, shards, smallest, high):
    level = 1.0
    for dim, shards_of in shards:
        heights = jax.random.uniform(jax.random.fold_in(jax.random.fold_in(stream_key, 6), dim), (shards_of,), jnp.float32, smallest / len(shards), high / len(shards))
        level = level * jnp.repeat(jnp.exp(heights), dims[dim] // shards_of).reshape((-1,) + (1,) * (len(dims) - 1 - dim))
    return level


def normal_values(own_key, shape, spread, reach, split=(), dtype=jnp.bfloat16):
    loudness = block_levels(own_key, shape, split, -0.22, 0.18) if split else 1.0
    drawn = jax.random.normal(own_key, shape, jnp.float32) * spread * loudness
    return jnp.minimum(jnp.maximum(drawn, -reach), reach).astype(dtype)


def setup_inputs(seed: int = 0) -> dict:
    keys = jax.random.split(jax.random.key(seed), 13)
    return {
        "x_inner": normal_values(keys[0], (BATCH, SEQ_LEN, INNER), 1.0, 6.0, ((0, 32), (2, 16))),
        "proj_dt": normal_values(keys[1], (BATCH, SEQ_LEN, RANK), 1.0, 6.0, ((0, 32), (1, 16))),
        "proj_bc": normal_values(keys[2], (BATCH, SEQ_LEN, 2 * STATE), 1.0, 6.0, ((0, 32), (1, 16))),
        "grad_y": normal_values(keys[3], (BATCH, SEQ_LEN, INNER), 1.0, 6.0, ((0, 32), (2, 16))),
        "w_xdt": normal_values(keys[4], (RANK, INNER), INNER ** -0.5, 0.046875, ((1, 16),)),
        "w_xbc": normal_values(keys[5], (2 * STATE, INNER), INNER ** -0.5, 0.046875, ((1, 16),)),
        "w_dt": normal_values(keys[6], (RANK, INNER), RANK ** -0.5, 0.25, ((1, 16),)),
        "dt_bias": jnp.clip(-6.0 + 3.5 * jax.random.uniform(keys[7], (INNER,), jnp.float32) ** block_levels(keys[7], (INNER,), ((0, 16),), -0.2, 0.2), -6.0, -2.5),
        "a_log": jnp.clip(-0.7 + 3.5 * jax.random.uniform(keys[8], (STATE, INNER), jnp.float32) ** block_levels(keys[8], (STATE, INNER), ((1, 16),), -0.2, 0.2), -0.7, 2.8),
        "d_skip": jnp.clip(0.5 + 1.0 * jax.random.uniform(keys[9], (INNER,), jnp.float32) ** block_levels(keys[9], (INNER,), ((0, 16),), -0.2, 0.2), 0.5, 1.5),
        "dt_gain": jnp.clip(1.0 + 0.15 * jax.random.normal(keys[10], (RANK,), jnp.float32), 0.25, 1.75),
        "bc_gain": jnp.clip(1.0 + 0.15 * jax.random.normal(keys[11], (2 * STATE,), jnp.float32), 0.25, 1.75),
    }


norm_eps = 1e-06
state_floor = 0.25
contract_rows = (((0,), (0,)), ((), ()))
contract_cols = (((1,), (1,)), ((), ()))

def unit_rows(dt_part, bc_part):
    dt_square = lax.optimization_barrier(jnp.mean(dt_part * dt_part, axis=-1, keepdims=True))
    dt_unit = dt_part * lax.rsqrt(dt_square + norm_eps)
    split_at = bc_part.shape[-1] // 2
    b_part = bc_part[..., :split_at]
    c_part = bc_part[..., split_at:]
    b_square = lax.optimization_barrier(jnp.mean(b_part * b_part, axis=-1, keepdims=True))
    c_square = lax.optimization_barrier(jnp.mean(c_part * c_part, axis=-1, keepdims=True))
    b_unit = b_part * lax.rsqrt(jnp.maximum(b_square, state_floor))
    c_unit = c_part * lax.rsqrt(jnp.maximum(c_square, state_floor))
    return (dt_unit, jnp.concatenate([b_unit, c_unit], axis=-1))

def scan_states(dt_rows, b_rows, c_rows, x_rows, a_mat):

    def scan_step(carry_state, inputs):
        dt_now, b_now, c_now, x_now = inputs
        decay_now = jnp.exp(dt_now[None, :] * a_mat)
        carry_state = decay_now * carry_state + (dt_now * x_now)[None, :] * b_now[:, None]
        return (carry_state, lax.optimization_barrier(jnp.sum(c_now[:, None] * carry_state, axis=0)))
    start_state = jnp.zeros(a_mat.shape, jnp.float32)
    last_state, outputs = lax.scan(jax.checkpoint(scan_step), start_state, (dt_rows, b_rows, c_rows, x_rows))
    return outputs

def one_sequence(x_seq, dt_seq, bc_seq, gy_seq, w_xdt, w_xbc, w_dt, dt_bias, a_log, d_skip, dt_gain, bc_gain):
    (dt_unit, bc_unit), unit_back = jax.vjp(unit_rows, dt_seq.astype(jnp.float32), bc_seq.astype(jnp.float32))
    dt_low = (dt_unit * dt_gain).astype(jnp.bfloat16)
    bc_normed = bc_unit * bc_gain
    split_at = bc_normed.shape[-1] // 2
    pre_act = jnp.dot(dt_low, w_dt, preferred_element_type=jnp.float32) + dt_bias
    dt_rows = jax.nn.softplus(pre_act)
    a_mat = -jnp.exp(a_log)
    x_float = x_seq.astype(jnp.float32)
    gy_float = gy_seq.astype(jnp.float32)
    scan_out, scan_back = jax.vjp(scan_states, dt_rows, bc_normed[:, :split_at], bc_normed[:, split_at:], x_float, a_mat)
    dt_grad, b_grad, c_grad, x_grad, a_grad = scan_back(gy_float)
    pre_float = dt_grad * jax.nn.sigmoid(pre_act)
    pre_grad = pre_float.astype(jnp.bfloat16)
    dt_normed_grad = lax.dot_general(pre_grad, w_dt, contract_cols, preferred_element_type=jnp.float32)
    bc_normed_grad = jnp.concatenate([b_grad, c_grad], axis=-1)
    proj_dt_grad, proj_bc_grad = unit_back((dt_normed_grad * dt_gain, bc_normed_grad * bc_gain))
    proj_dt_low = proj_dt_grad.astype(jnp.bfloat16)
    proj_bc_low = proj_bc_grad.astype(jnp.bfloat16)
    summed = x_grad + d_skip * gy_float
    summed = summed + jnp.dot(proj_dt_low, w_xdt, preferred_element_type=jnp.float32)
    summed = summed + jnp.dot(proj_bc_low, w_xbc, preferred_element_type=jnp.float32)
    grad_x = summed.astype(jnp.bfloat16)
    w_dt_term = lax.dot_general(dt_low, pre_grad, contract_rows, preferred_element_type=jnp.float32)
    w_xdt_term = lax.dot_general(proj_dt_low, x_seq, contract_rows, preferred_element_type=jnp.float32)
    w_xbc_term = lax.dot_general(proj_bc_low, x_seq, contract_rows, preferred_element_type=jnp.float32)
    a_term = a_grad * a_mat
    bias_term = lax.optimization_barrier(jnp.sum(pre_float, axis=0))
    skip_term = lax.optimization_barrier(jnp.sum(gy_float * x_float, axis=0))
    dt_gain_term = lax.optimization_barrier(jnp.sum(dt_normed_grad * dt_unit, axis=0))
    bc_gain_term = lax.optimization_barrier(jnp.sum(bc_normed_grad * bc_unit, axis=0))
    return (grad_x, (w_xdt_term, w_dt_term, w_xbc_term, a_term, bias_term, skip_term, dt_gain_term, bc_gain_term))

def reference(x_inner, proj_dt, proj_bc, grad_y, w_xdt, w_xbc, w_dt, dt_bias, a_log, d_skip, dt_gain, bc_gain):
    grad_scale = 1.0 / math.sqrt(BATCH * SEQ_LEN)

    def per_sequence(totals, inputs):
        x_seq, dt_seq, bc_seq, gy_seq = inputs
        grad_x, terms = one_sequence(x_seq, dt_seq, bc_seq, gy_seq, w_xdt, w_xbc, w_dt, dt_bias, a_log, d_skip, dt_gain, bc_gain)
        updated = tuple((totals[index] + grad_scale * terms[index] for index in range(8)))
        return (updated, grad_x)
    start_totals = (jnp.zeros(w_xdt.shape, jnp.float32), jnp.zeros(w_dt.shape, jnp.float32), jnp.zeros(w_xbc.shape, jnp.float32), jnp.zeros(a_log.shape, jnp.float32), jnp.zeros(dt_bias.shape, jnp.float32), jnp.zeros(d_skip.shape, jnp.float32), jnp.zeros(dt_gain.shape, jnp.float32), jnp.zeros(bc_gain.shape, jnp.float32))
    totals, grad_x = lax.scan(per_sequence, start_totals, (x_inner, proj_dt, proj_bc, grad_y))
    return (grad_x, totals[0], totals[1], totals[2], totals[3], totals[4], totals[5], totals[6], totals[7])
```

```python
import functools
import math

import jax
import jax.numpy as jnp
from jax import lax
from jax.experimental import pallas as pl
from jax.experimental.pallas import tpu as pltpu
from jax.sharding import PartitionSpec as P

norm_eps = 1e-06
state_floor = 0.25
log2_e = 1.4426950408889634
lane = 128
f32 = jnp.float32
bf16 = jnp.bfloat16
contract_rows = (((0,), (0,)), ((), ()))
contract_cols = (((1,), (1,)), ((), ()))
in_vmem = pl.BlockSpec(memory_space=pltpu.VMEM)


def inverse_norms(proj, rank, state):
    dt_part = proj[:, :rank]
    b_part = proj[:, rank : rank + state]
    c_part = proj[:, rank + state : rank + 2 * state]
    dt_square = jnp.mean(dt_part * dt_part, axis=1, keepdims=True)
    b_square = jnp.mean(b_part * b_part, axis=1, keepdims=True)
    c_square = jnp.mean(c_part * c_part, axis=1, keepdims=True)
    return (
        (dt_part, lax.rsqrt(dt_square + norm_eps)),
        (b_part, lax.rsqrt(jnp.maximum(b_square, state_floor)), b_square),
        (c_part, lax.rsqrt(jnp.maximum(c_square, state_floor)), c_square),
    )


def scan_kernel(
    proj_ref,
    x_ref,
    gy_ref,
    w_ref,
    bias_ref,
    alog_ref,
    skip_ref,
    dt_gain_ref,
    bc_gain_ref,
    normed_ref,
    w_part_ref,
    xg_ref,
    misc_ref,
    dt_s,
    gy_s,
    src_s,
    sig_s,
    a2_s,
    low_s,
    bcb_s,
    u_s,
    b_acc,
    c_acc,
    s1_s,
    s2_s,
    *,
    wide_lanes,
    scale,
):
    tokens, width = x_ref.shape
    state = alog_ref.shape[0]
    rank = w_ref.shape[0]
    dt_norm, b_norm, c_norm = inverse_norms(proj_ref[...].astype(f32), rank, state)
    low_s[...] = (dt_norm[0] * dt_norm[1] * dt_gain_ref[...]).astype(bf16)
    b_rows = b_norm[0] * b_norm[1] * bc_gain_ref[:, :state]
    c_rows = c_norm[0] * c_norm[1] * bc_gain_ref[:, state:]
    bcb_s[:, :state] = jnp.broadcast_to(b_rows[:, :, None], (tokens, state, lane))
    bcb_s[:, state:] = jnp.broadcast_to(c_rows[:, :, None], (tokens, state, lane))
    pre = jnp.dot(low_s[...], w_ref[...], preferred_element_type=f32) + bias_ref[...]
    small = jnp.exp(-jnp.abs(pre))
    dt_rows = jnp.maximum(pre, 0.0) + jnp.log1p(small)
    sig_s[...] = jnp.where(pre >= 0, 1.0, small) / (1.0 + small)
    x_float = x_ref[...].astype(f32)
    gy_float = gy_ref[...].astype(f32)
    dt_s[...] = dt_rows
    gy_s[...] = gy_float
    src_s[...] = dt_rows * x_float
    a_mat = -jnp.exp(alog_ref[...])
    a2_s[...] = a_mat * log2_e
    b_acc[...] = jnp.zeros_like(b_acc)
    c_acc[...] = jnp.zeros_like(c_acc)
    reps = wide_lanes // lane

    def widen(part):
        return jnp.concatenate([part] * reps, axis=1)

    def fold(part):
        total = part[:, :lane]
        for rep in range(1, reps):
            total = total + part[:, rep * lane : (rep + 1) * lane]
        return total

    for group in range(width // wide_lanes):
        cols = slice(group * wide_lanes, (group + 1) * wide_lanes)

        def forward(block, held):
            a2 = a2_s[:, cols]
            for offset in range(8):
                t = block * 8 + offset
                decayed = jnp.exp2(dt_s[pl.ds(t, 1), cols] * a2) * held
                u_s[pl.ds(t, 1), :, cols] = decayed[None]
                c_acc[pl.ds(t, 1)] += fold(decayed * gy_s[pl.ds(t, 1), cols])[None]
                held = decayed + src_s[pl.ds(t, 1), cols] * widen(bcb_s[t, :state])
            return held

        zeros = jnp.zeros((state, wide_lanes), f32)
        lax.fori_loop(0, tokens // 8, forward, zeros)

        def backward(step, carry):
            later, a_total = carry
            block = tokens // 8 - 1 - step
            a2 = a2_s[:, cols]
            for offset in range(7, -1, -1):
                t = block * 8 + offset
                dt_now = dt_s[pl.ds(t, 1), cols]
                adjoint = widen(bcb_s[t, state:]) * gy_s[pl.ds(t, 1), cols] + later
                through = adjoint * u_s[t, :, cols]
                s1_s[pl.ds(t, 1), cols] = jnp.sum(
                    adjoint * widen(bcb_s[t, :state]), axis=0, keepdims=True
                )
                s2_s[pl.ds(t, 1), cols] = jnp.sum(through * a2, axis=0, keepdims=True)
                b_acc[pl.ds(t, 1)] += fold(adjoint * src_s[pl.ds(t, 1), cols])[None]
                a_total = a_total + dt_now * through
                later = jnp.exp2(dt_now * a2) * adjoint
            return later, a_total

        _, a_total = lax.fori_loop(0, tokens // 8, backward, (zeros, zeros))
        misc_ref[:state, cols] = (scale / log2_e) * (a_total * a2_s[:, cols])

    s1 = s1_s[...]
    xg_ref[...] = dt_s[...] * s1 + skip_ref[...] * gy_s[...]
    dt_grad = x_ref[...].astype(f32) * s1 + s2_s[...] * (1.0 / log2_e)
    pre_float = dt_grad * sig_s[...]
    pre_grad = pre_float.astype(bf16)
    misc_ref[state : state + 1, :] = scale * jnp.sum(pre_float, axis=0, keepdims=True)
    misc_ref[state + 1 : state + 2, :] = scale * jnp.sum(
        gy_s[...] * x_ref[...].astype(f32), axis=0, keepdims=True
    )
    normed_ref[:, :rank] = lax.dot_general(
        pre_grad, w_ref[...], contract_cols, preferred_element_type=f32
    ).astype(bf16)
    w_part_ref[...] = (
        scale
        * lax.dot_general(low_s[...], pre_grad, contract_rows, preferred_element_type=f32)
    ).astype(bf16)
    source_sum = jnp.sum(src_s[...] * gy_s[...], axis=1, keepdims=True)
    b_grad = jnp.sum(b_acc[...], axis=2)
    c_grad = jnp.sum(c_acc[...], axis=2) + b_rows * source_sum
    normed_ref[:, rank : rank + state] = b_grad.astype(bf16)
    normed_ref[:, rank + state : rank + 2 * state] = c_grad.astype(bf16)
    normed_ref[:, rank + 2 * state :] = jnp.zeros_like(normed_ref[:, rank + 2 * state :])


def norm_kernel(parts_ref, proj_ref, dt_gain_ref, bc_gain_ref, out_ref, pack_s, *, state):
    rank = dt_gain_ref.shape[1]
    grads = jnp.sum(parts_ref[...].astype(f32), axis=0)
    dt_norm, b_norm, c_norm = inverse_norms(proj_ref[...].astype(f32), rank, state)
    dt_grad = grads[:, :rank]
    dt_unit = dt_norm[0] * dt_norm[1]
    dt_cot = dt_grad * dt_gain_ref[...]
    dt_mean = jnp.mean(dt_cot * dt_unit, axis=1, keepdims=True)
    pack_s[...] = jnp.zeros_like(pack_s)
    pack_s[:, :rank] = dt_norm[1] * (dt_cot - dt_unit * dt_mean)
    gain_rows = []
    dt_gain_part = jnp.sum(dt_grad * dt_unit, axis=0, keepdims=True)
    for piece in range(rank // lane):
        gain_rows.append(dt_gain_part[:, piece * lane : (piece + 1) * lane])
    last = rank + lane
    for index, part in enumerate((b_norm, c_norm)):
        start = rank + index * state
        grad = grads[:, start : start + state]
        unit = part[0] * part[1]
        cot = grad * bc_gain_ref[:, index * state : (index + 1) * state]
        mean = jnp.mean(cot * unit, axis=1, keepdims=True)
        inner = jnp.where(part[2] > state_floor, mean, 0.0)
        inner = jnp.where(part[2] == state_floor, 0.5 * mean, inner)
        pack_s[:, start : start + state] = part[1] * (cot - unit * inner)
        gain_part = jnp.sum(grad * unit, axis=0, keepdims=True)
        pack_s[4:5, last + index * state : last + (index + 1) * state] = gain_part
    for piece, row in enumerate(gain_rows):
        pack_s[piece : piece + 1, last : last + lane] = row
    gains = pack_s[0:8, last : last + lane]
    high = gains.astype(bf16)
    pack_s[8:16, last : last + lane] = gains - high.astype(f32)
    packed = pack_s[...].astype(bf16)
    for peer in range(out_ref.shape[0]):
        out_ref[peer] = packed


def project_kernel(
    low_ref,
    xg_ref,
    x_ref,
    w_xdt_ref,
    w_xbc_ref,
    w_part_ref,
    misc_ref,
    grad_x_ref,
    out_ref,
    all_s,
    *,
    scale,
):
    rank, width = w_xdt_ref.shape
    bc_width = w_xbc_ref.shape[0]
    own = low_ref.shape[0] // 16
    dt_low = low_ref[:, :rank]
    bc_low = low_ref[:, rank : rank + bc_width]
    summed = xg_ref[...] + jnp.dot(dt_low, w_xdt_ref[...], preferred_element_type=f32)
    summed = summed + jnp.dot(bc_low, w_xbc_ref[...], preferred_element_type=f32)
    grad_x_ref[...] = summed.astype(bf16)
    out_ref[:, :width] = (
        scale
        * lax.dot_general(dt_low, x_ref[...], contract_rows, preferred_element_type=f32)
    ).astype(bf16)
    out_ref[:, width : 2 * width] = w_part_ref[...]
    state = bc_width // 2
    all_s[...] = jnp.zeros_like(all_s)
    all_s[: state + 2, :] = misc_ref[: state + 2, :]
    all_s[state + 8 : state + 8 + bc_width, :] = scale * lax.dot_general(
        bc_low, x_ref[...], contract_rows, preferred_element_type=f32
    )
    gains = low_ref[:, rank + lane : rank + 2 * lane].astype(f32)
    total = jnp.zeros((8, lane), f32)
    for peer in range(16):
        first = peer * own
        total = total + (gains[first : first + 8] + gains[first + 8 : first + 16])
    for piece in range(rank // lane + 1):
        row = state + 8 + bc_width
        all_s[row : row + 1, piece * lane : (piece + 1) * lane] = (
            scale * total[piece : piece + 1]
        )
    for piece in range(width // lane):
        out_ref[piece * 64 : (piece + 1) * 64, 2 * width :] = all_s[
            :, piece * lane : (piece + 1) * lane
        ].astype(bf16)


def total_kernel(parts_ref, xdt_ref, dt_ref, own_ref):
    width = xdt_ref.shape[1]
    total = jnp.sum(parts_ref[...].astype(f32), axis=0)
    xdt_ref[...] = total[:, :width]
    dt_ref[...] = total[:, width : 2 * width]
    for peer in range(own_ref.shape[0]):
        own_ref[peer] = total[:, 2 * width :]


def call(kernel, name, outs, scratch, limit_mib, *args):
    return pl.pallas_call(
        kernel,
        out_shape=tuple(jax.ShapeDtypeStruct(shape, dtype) for shape, dtype in outs),
        in_specs=[in_vmem] * len(args),
        out_specs=tuple([in_vmem] * len(outs)),
        scratch_shapes=[pltpu.VMEM(shape, dtype) for shape, dtype in scratch],
        compiler_params=pltpu.CompilerParams(vmem_limit_bytes=limit_mib * 2**20),
        name=name,
    )(*args)


def send_to_all(block, axis):
    return lax.all_to_all(block, axis, 0, 0)


def body(
    x_inner, proj_dt, proj_bc, grad_y, w_xdt, w_xbc, w_dt, dt_bias, a_log, d_skip, dt_gain, bc_gain
):
    x_rows = x_inner[0]
    gy_rows = grad_y[0]
    tokens, width = x_rows.shape
    rank = proj_dt.shape[2]
    bc_width = proj_bc.shape[2]
    state = bc_width // 2
    own = proj_dt.shape[1]
    dp = lax.axis_size("dp")
    tensor = lax.axis_size("tensor")
    scale = 1.0 / math.sqrt(dp * tokens)
    bias_row = dt_bias.reshape(1, width)
    skip_row = d_skip.reshape(1, width)
    dt_gain_row = dt_gain.reshape(1, rank)
    bc_gain_row = bc_gain.reshape(1, bc_width)

    columns = rank + lane
    own_proj = jnp.concatenate(
        [proj_dt[0], proj_bc[0], jnp.zeros((own, lane - bc_width), bf16)], axis=1
    )
    full_proj = send_to_all(
        jnp.broadcast_to(own_proj[None], (tensor, own, columns)), "tensor"
    ).reshape(tokens, columns)

    rows = ((tokens, width), f32)
    normed_part, w_part, xg, misc = call(
        functools.partial(scan_kernel, wide_lanes=min(512, width), scale=scale),
        "scan",
        [
            ((tokens, columns), bf16),
            ((rank, width), bf16),
            ((tokens, width), f32),
            ((state + 8, width), f32),
        ],
        [
            rows,
            rows,
            rows,
            rows,
            ((state, width), f32),
            ((tokens, rank), bf16),
            ((tokens, 2 * state, lane), f32),
            ((tokens, state, width), f32),
            ((tokens, state, lane), f32),
            ((tokens, state, lane), f32),
            rows,
            rows,
        ],
        56,
        full_proj,
        x_rows,
        gy_rows,
        w_dt,
        bias_row,
        a_log,
        skip_row,
        dt_gain_row,
        bc_gain_row,
    )
    normed_parts = send_to_all(normed_part.reshape(tensor, own, columns), "tensor")
    packed_columns = columns + lane
    (own_low,) = call(
        functools.partial(norm_kernel, state=state),
        "norm",
        [((tensor, own, packed_columns), bf16)],
        [((own, packed_columns), f32)],
        16,
        normed_parts,
        own_proj,
        dt_gain_row,
        bc_gain_row,
    )
    low = send_to_all(own_low, "tensor").reshape(tokens, packed_columns)
    grad_x, parts = call(
        functools.partial(project_kernel, scale=scale),
        "project",
        [((tokens, width), bf16), ((rank, 2 * width + lane), bf16)],
        [((64, width), f32)],
        32,
        low,
        xg,
        x_rows,
        w_xdt,
        w_xbc,
        w_part,
        misc,
    )
    per_device = rank // dp
    all_parts = send_to_all(parts.reshape(dp, per_device, 2 * width + lane), "dp")
    grad_w_xdt, grad_w_dt, own_total = call(
        total_kernel,
        "total",
        [
            ((per_device, width), f32),
            ((per_device, width), f32),
            ((dp, per_device, lane), f32),
        ],
        [],
        32,
        all_parts,
    )
    totals = send_to_all(own_total, "dp").reshape(width // lane, 64, lane)
    totals = totals.transpose(1, 0, 2).reshape(64, width)
    gain_row = state + 8 + bc_width
    return (
        grad_x[None],
        grad_w_xdt,
        grad_w_dt,
        totals[state + 8 : state + 8 + bc_width],
        totals[:state],
        totals[state],
        totals[state + 1],
        totals[gain_row, :rank],
        totals[gain_row, rank : rank + bc_width],
    )


def solution(mesh):
    return jax.shard_map(
        body,
        mesh=mesh,
        in_specs=(
            P("dp", None, "tensor"),
            P("dp", "tensor", None),
            P("dp", "tensor", None),
            P("dp", None, "tensor"),
            P(None, "tensor"),
            P(None, "tensor"),
            P(None, "tensor"),
            P("tensor"),
            P(None, "tensor"),
            P("tensor"),
            P(),
            P(),
        ),
        out_specs=(
            P("dp", None, "tensor"),
            P("dp", "tensor"),
            P("dp", "tensor"),
            P(None, "tensor"),
            P(None, "tensor"),
            P("tensor"),
            P("tensor"),
            P(),
            P(),
        ),
        check_vma=False,
    )
```

```python
import functools
import math

import jax
import jax.numpy as jnp
from jax import lax
from jax.experimental import pallas as pl
from jax.experimental.pallas import tpu as pltpu
from jax.sharding import PartitionSpec as P

norm_eps = 1e-06
state_floor = 0.25
log2_e = 1.4426950408889634
lane = 128
f32 = jnp.float32
bf16 = jnp.bfloat16
contract_rows = (((0,), (0,)), ((), ()))
contract_cols = (((1,), (1,)), ((), ()))
in_vmem = pl.BlockSpec(memory_space=pltpu.VMEM)


def inverse_norms(proj, rank, state):
    dt_part = proj[:, :rank]
    b_part = proj[:, rank : rank + state]
    c_part = proj[:, rank + state : rank + 2 * state]
    dt_square = jnp.mean(dt_part * dt_part, axis=1, keepdims=True)
    b_square = jnp.mean(b_part * b_part, axis=1, keepdims=True)
    c_square = jnp.mean(c_part * c_part, axis=1, keepdims=True)
    return (
        (dt_part, lax.rsqrt(dt_square + norm_eps)),
        (b_part, lax.rsqrt(jnp.maximum(b_square, state_floor)), b_square),
        (c_part, lax.rsqrt(jnp.maximum(c_square, state_floor)), c_square),
    )


def scan_kernel(
    proj_ref,
    x_ref,
    gy_ref,
    w_ref,
    bias_ref,
    alog_ref,
    skip_ref,
    dt_gain_ref,
    bc_gain_ref,
    normed_ref,
    w_part_ref,
    xg_ref,
    misc_ref,
    dt_s,
    gy_s,
    src_s,
    sig_s,
    a2_s,
    low_s,
    bcb_s,
    u_s,
    b_acc,
    c_acc,
    s1_s,
    s2_s,
    *,
    wide_lanes,
    scale,
):
    tokens, width = x_ref.shape
    state = alog_ref.shape[0]
    rank = w_ref.shape[0]
    dt_norm, b_norm, c_norm = inverse_norms(proj_ref[...].astype(f32), rank, state)
    low_s[...] = (dt_norm[0] * dt_norm[1] * dt_gain_ref[...]).astype(bf16)
    b_rows = b_norm[0] * b_norm[1] * bc_gain_ref[:, :state]
    c_rows = c_norm[0] * c_norm[1] * bc_gain_ref[:, state:]
    bcb_s[:, :state] = jnp.broadcast_to(b_rows[:, :, None], (tokens, state, lane))
    bcb_s[:, state:] = jnp.broadcast_to(c_rows[:, :, None], (tokens, state, lane))
    pre = jnp.dot(low_s[...], w_ref[...], preferred_element_type=f32) + bias_ref[...]
    small = jnp.exp(-jnp.abs(pre))
    dt_rows = jnp.maximum(pre, 0.0) + jnp.log1p(small)
    sig_s[...] = jnp.where(pre >= 0, 1.0, small) / (1.0 + small)
    x_float = x_ref[...].astype(f32)
    gy_float = gy_ref[...].astype(f32)
    dt_s[...] = dt_rows
    gy_s[...] = gy_float
    src_s[...] = dt_rows * x_float
    a_mat = -jnp.exp(alog_ref[...])
    a2_s[...] = a_mat * log2_e
    b_acc[...] = jnp.zeros_like(b_acc)
    c_acc[...] = jnp.zeros_like(c_acc)
    reps = wide_lanes // lane

    def widen(part):
        return jnp.concatenate([part] * reps, axis=1)

    def fold(part):
        total = part[:, :lane]
        for rep in range(1, reps):
            total = total + part[:, rep * lane : (rep + 1) * lane]
        return total

    for group in range(width // wide_lanes):
        cols = slice(group * wide_lanes, (group + 1) * wide_lanes)

        def forward(block, held):
            a2 = a2_s[:, cols]
            for offset in range(8):
                t = block * 8 + offset
                decayed = jnp.exp2(dt_s[pl.ds(t, 1), cols] * a2) * held
                u_s[pl.ds(t, 1), :, cols] = decayed[None]
                c_acc[pl.ds(t, 1)] += fold(decayed * gy_s[pl.ds(t, 1), cols])[None]
                held = decayed + src_s[pl.ds(t, 1), cols] * widen(bcb_s[t, :state])
            return held

        zeros = jnp.zeros((state, wide_lanes), f32)
        lax.fori_loop(0, tokens // 8, forward, zeros)

        def backward(step, carry):
            later, a_total = carry
            block = tokens // 8 - 1 - step
            a2 = a2_s[:, cols]
            for offset in range(7, -1, -1):
                t = block * 8 + offset
                dt_now = dt_s[pl.ds(t, 1), cols]
                adjoint = widen(bcb_s[t, state:]) * gy_s[pl.ds(t, 1), cols] + later
                through = adjoint * u_s[t, :, cols]
                s1_s[pl.ds(t, 1), cols] = jnp.sum(
                    adjoint * widen(bcb_s[t, :state]), axis=0, keepdims=True
                )
                s2_s[pl.ds(t, 1), cols] = jnp.sum(through * a2, axis=0, keepdims=True)
                b_acc[pl.ds(t, 1)] += fold(adjoint * src_s[pl.ds(t, 1), cols])[None]
                a_total = a_total + dt_now * through
                later = jnp.exp2(dt_now * a2) * adjoint
            return later, a_total

        _, a_total = lax.fori_loop(0, tokens // 8, backward, (zeros, zeros))
        misc_ref[:state, cols] = (scale / log2_e) * (a_total * a2_s[:, cols])

    s1 = s1_s[...]
    xg_ref[...] = dt_s[...] * s1 + skip_ref[...] * gy_s[...]
    dt_grad = x_ref[...].astype(f32) * s1 + s2_s[...] * (1.0 / log2_e)
    pre_float = dt_grad * sig_s[...]
    pre_grad = pre_float.astype(bf16)
    misc_ref[state : state + 1, :] = scale * jnp.sum(pre_float, axis=0, keepdims=True)
    misc_ref[state + 1 : state + 2, :] = scale * jnp.sum(
        gy_s[...] * x_ref[...].astype(f32), axis=0, keepdims=True
    )
    normed_ref[:, :rank] = lax.dot_general(
        pre_grad, w_ref[...], contract_cols, preferred_element_type=f32
    ).astype(bf16)
    w_part_ref[...] = (
        scale
        * lax.dot_general(low_s[...], pre_grad, contract_rows, preferred_element_type=f32)
    ).astype(bf16)
    source_sum = jnp.sum(src_s[...] * gy_s[...], axis=1, keepdims=True)
    b_grad = jnp.sum(b_acc[...], axis=2)
    c_grad = jnp.sum(c_acc[...], axis=2) + b_rows * source_sum
    normed_ref[:, rank : rank + state] = b_grad.astype(bf16)
    normed_ref[:, rank + state : rank + 2 * state] = c_grad.astype(bf16)
    normed_ref[:, rank + 2 * state :] = jnp.zeros_like(normed_ref[:, rank + 2 * state :])


def norm_kernel(parts_ref, proj_ref, dt_gain_ref, bc_gain_ref, out_ref, pack_s, *, state):
    rank = dt_gain_ref.shape[1]
    grads = jnp.sum(parts_ref[...].astype(f32), axis=0)
    dt_norm, b_norm, c_norm = inverse_norms(proj_ref[...].astype(f32), rank, state)
    dt_grad = grads[:, :rank]
    dt_unit = dt_norm[0] * dt_norm[1]
    dt_cot = dt_grad * dt_gain_ref[...]
    dt_mean = jnp.mean(dt_cot * dt_unit, axis=1, keepdims=True)
    pack_s[...] = jnp.zeros_like(pack_s)
    pack_s[:, :rank] = dt_norm[1] * (dt_cot - dt_unit * dt_mean)
    gain_rows = []
    dt_gain_part = jnp.sum(dt_grad * dt_unit, axis=0, keepdims=True)
    for piece in range(rank // lane):
        gain_rows.append(dt_gain_part[:, piece * lane : (piece + 1) * lane])
    last = rank + lane
    for index, part in enumerate((b_norm, c_norm)):
        start = rank + index * state
        grad = grads[:, start : start + state]
        unit = part[0] * part[1]
        cot = grad * bc_gain_ref[:, index * state : (index + 1) * state]
        mean = jnp.mean(cot * unit, axis=1, keepdims=True)
        inner = jnp.where(part[2] > state_floor, mean, 0.0)
        inner = jnp.where(part[2] == state_floor, 0.5 * mean, inner)
        pack_s[:, start : start + state] = part[1] * (cot - unit * inner)
        gain_part = jnp.sum(grad * unit, axis=0, keepdims=True)
        pack_s[4:5, last + index * state : last + (index + 1) * state] = gain_part
    for piece, row in enumerate(gain_rows):
        pack_s[piece : piece + 1, last : last + lane] = row
    gains = pack_s[0:8, last : last + lane]
    high = gains.astype(bf16)
    pack_s[8:16, last : last + lane] = gains - high.astype(f32)
    packed = pack_s[...].astype(bf16)
    for peer in range(out_ref.shape[0]):
        out_ref[peer] = packed


def project_kernel(
    core_ref,
    low_ref,
    xg_ref,
    x_ref,
    w_xdt_ref,
    w_xbc_ref,
    w_part_ref,
    misc_ref,
    grad_x_ref,
    keep_ref,
    send_ref,
    out_ref,
    all_s,
    *,
    scale,
):
    rank, width = w_xdt_ref.shape
    bc_width = w_xbc_ref.shape[0]
    own = low_ref.shape[0] // 16
    dt_low = low_ref[:, :rank]
    bc_low = low_ref[:, rank : rank + bc_width]
    summed = xg_ref[...] + jnp.dot(dt_low, w_xdt_ref[...], preferred_element_type=f32)
    summed = summed + jnp.dot(bc_low, w_xbc_ref[...], preferred_element_type=f32)
    grad_x_ref[...] = summed.astype(bf16)
    out_ref[:, :width] = (
        scale
        * lax.dot_general(dt_low, x_ref[...], contract_rows, preferred_element_type=f32)
    ).astype(bf16)
    out_ref[:, width : 2 * width] = w_part_ref[...]
    state = bc_width // 2
    all_s[...] = jnp.zeros_like(all_s)
    all_s[: state + 2, :] = misc_ref[: state + 2, :]
    all_s[state + 8 : state + 8 + bc_width, :] = scale * lax.dot_general(
        bc_low, x_ref[...], contract_rows, preferred_element_type=f32
    )
    gains = low_ref[:, rank + lane : rank + 2 * lane].astype(f32)
    total = jnp.zeros((8, lane), f32)
    for peer in range(16):
        first = peer * own
        total = total + (gains[first : first + 8] + gains[first + 8 : first + 16])
    for piece in range(rank // lane + 1):
        row = state + 8 + bc_width
        all_s[row : row + 1, piece * lane : (piece + 1) * lane] = (
            scale * total[piece : piece + 1]
        )
    for piece in range(width // lane):
        out_ref[piece * 64 : (piece + 1) * 64, 2 * width :] = all_s[
            :, piece * lane : (piece + 1) * lane
        ].astype(bf16)
    first_core = core_ref[0] == 0
    for pair in range(keep_ref.shape[0]):
        even = out_ref[32 * pair : 32 * pair + 16, :]
        odd = out_ref[32 * pair + 16 : 32 * pair + 32, :]
        keep_ref[pair] = jnp.where(first_core, even, odd)
        send_ref[pair] = jnp.where(first_core, odd, even)


def total_kernel(parts_ref, xdt_ref, dt_ref, own_ref):
    width = xdt_ref.shape[1]
    total = parts_ref[0].astype(f32)
    for peer in range(1, parts_ref.shape[0]):
        total = total + parts_ref[peer].astype(f32)
    xdt_ref[...] = total[:, :width]
    dt_ref[...] = total[:, width : 2 * width]
    for peer in range(own_ref.shape[0]):
        own_ref[peer] = total[:, 2 * width :]


def spread_kernel(
    parts_ref, xbc_ref, alog_ref, bias_ref, skip_ref, dt_gain_ref, bc_gain_ref, all_s, *, order
):
    state = alog_ref.shape[0]
    bc_width = xbc_ref.shape[0]
    rank = dt_gain_ref.shape[1]
    for block, (peer, place) in enumerate(order):
        row, piece = 16 * (block % 4), lane * (block // 4)
        all_s[row : row + 16, piece : piece + lane] = parts_ref[
            peer, :, place * lane : (place + 1) * lane
        ]
    alog_ref[...] = all_s[:state, :]
    bias_ref[...] = all_s[state : state + 1, :]
    skip_ref[...] = all_s[state + 1 : state + 2, :]
    xbc_ref[...] = all_s[state + 8 : state + 8 + bc_width, :]
    gain_row = state + 8 + bc_width
    dt_gain_ref[...] = all_s[gain_row : gain_row + 1, :rank]
    bc_gain_ref[...] = all_s[gain_row : gain_row + 1, rank : rank + bc_width]


def call(kernel, name, outs, scratch, limit_mib, *args):
    in_smem = pl.BlockSpec(memory_space=pltpu.SMEM)
    return pl.pallas_call(
        kernel,
        out_shape=tuple(jax.ShapeDtypeStruct(shape, dtype) for shape, dtype in outs),
        in_specs=[in_smem if arg.dtype == jnp.int32 else in_vmem for arg in args],
        out_specs=tuple([in_vmem] * len(outs)),
        scratch_shapes=[pltpu.VMEM(shape, dtype) for shape, dtype in scratch],
        compiler_params=pltpu.CompilerParams(vmem_limit_bytes=limit_mib * 2**20),
        name=name,
    )(*args)


def send_to_all(block, axis, groups=None):
    return lax.all_to_all(block, axis, 0, 0, axis_index_groups=groups)


def sum_low(parts):
    return jnp.sum(parts.astype(f32), axis=0).astype(bf16)


def body(
    x_inner, proj_dt, proj_bc, grad_y, w_xdt, w_xbc, w_dt, dt_bias, a_log, d_skip, dt_gain, bc_gain
):
    x_rows = x_inner[0]
    gy_rows = grad_y[0]
    tokens, width = x_rows.shape
    rank = proj_dt.shape[2]
    bc_width = proj_bc.shape[2]
    state = bc_width // 2
    own = proj_dt.shape[1]
    dp = lax.axis_size("dp")
    tensor = lax.axis_size("tensor")
    scale = 1.0 / math.sqrt(dp * tokens)
    bias_row = dt_bias.reshape(1, width)
    skip_row = d_skip.reshape(1, width)
    dt_gain_row = dt_gain.reshape(1, rank)
    bc_gain_row = bc_gain.reshape(1, bc_width)

    columns = rank + lane
    own_proj = jnp.concatenate(
        [proj_dt[0], proj_bc[0], jnp.zeros((own, lane - bc_width), bf16)], axis=1
    )
    full_proj = send_to_all(
        jnp.broadcast_to(own_proj[None], (tensor, own, columns)), "tensor"
    ).reshape(tokens, columns)

    rows = ((tokens, width), f32)
    normed_part, w_part, xg, misc = call(
        functools.partial(scan_kernel, wide_lanes=min(512, width), scale=scale),
        "scan",
        [
            ((tokens, columns), bf16),
            ((rank, width), bf16),
            ((tokens, width), f32),
            ((state + 8, width), f32),
        ],
        [
            rows,
            rows,
            rows,
            rows,
            ((state, width), f32),
            ((tokens, rank), bf16),
            ((tokens, 2 * state, lane), f32),
            ((tokens, state, width), f32),
            ((tokens, state, lane), f32),
            ((tokens, state, lane), f32),
            rows,
            rows,
        ],
        56,
        full_proj,
        x_rows,
        gy_rows,
        w_dt,
        bias_row,
        a_log,
        skip_row,
        dt_gain_row,
        bc_gain_row,
    )
    normed_parts = send_to_all(normed_part.reshape(tensor, own, columns), "tensor")
    packed_columns = columns + lane
    (own_low,) = call(
        functools.partial(norm_kernel, state=state),
        "norm",
        [((tensor, own, packed_columns), bf16)],
        [((own, packed_columns), f32)],
        16,
        normed_parts,
        own_proj,
        dt_gain_row,
        bc_gain_row,
    )
    low = send_to_all(own_low, "tensor").reshape(tokens, packed_columns)
    cores, z_size = 2, 4
    x_size = dp // (cores * z_size)
    core = (lax.axis_index("dp") % cores).astype(jnp.int32).reshape(1)
    per_device = rank // dp
    row_width = 2 * width + lane
    half = ((x_size * z_size, per_device, row_width), bf16)
    grad_x, kept, sent = call(
        functools.partial(project_kernel, scale=scale),
        "project",
        [((tokens, width), bf16), half, half],
        [((rank, row_width), bf16), ((64, width), f32)],
        32,
        core,
        low,
        xg,
        x_rows,
        w_xdt,
        w_xbc,
        w_part,
        misc,
    )
    other_core = [(index, index ^ 1) for index in range(dp)]
    kept = (kept.astype(f32) + lax.ppermute(sent, "dp", other_core).astype(f32)).astype(bf16)
    z_stride, x_stride = cores, cores * z_size
    along_x = [[x * x_stride + rest for x in range(x_size)] for rest in range(x_stride)]
    along_z = [
        [x * x_stride + z * z_stride + c for z in range(z_size)]
        for x in range(x_size)
        for c in range(cores)
    ]
    along_xc = [
        [x * x_stride + z * z_stride + c for x in range(x_size) for c in range(cores)]
        for z in range(z_size)
    ]
    by_x = sum_low(
        send_to_all(kept.reshape(x_size, z_size, per_device, row_width), "dp", along_x)
    )
    by_z = by_x[:, :, 2 * width :].transpose(1, 0, 2).reshape(1, per_device, z_size * lane)
    by_z = jnp.broadcast_to(by_z, (z_size, per_device, z_size * lane))
    by_z = jnp.concatenate([by_x[:, :, : 2 * width], by_z], axis=2)
    all_parts = send_to_all(by_z, "dp", along_z)
    shared = x_size * cores
    grad_w_xdt, grad_w_dt, own_total = call(
        total_kernel,
        "total",
        [
            ((per_device, width), f32),
            ((per_device, width), f32),
            ((shared, per_device, z_size * lane), f32),
        ],
        [],
        32,
        all_parts,
    )
    totals = send_to_all(own_total, "dp", along_xc)
    order = tuple(
        (x * cores + c, z) for x in range(x_size) for z in range(z_size) for c in range(cores)
    )
    grad_w_xbc, grad_a_log, bias_total, skip_total, dt_gain_total, bc_gain_total = call(
        functools.partial(spread_kernel, order=order),
        "spread",
        [
            ((bc_width, width), f32),
            ((state, width), f32),
            ((1, width), f32),
            ((1, width), f32),
            ((1, rank), f32),
            ((1, bc_width), f32),
        ],
        [((64, width), f32)],
        16,
        totals,
    )
    return (
        grad_x[None],
        grad_w_xdt,
        grad_w_dt,
        grad_w_xbc,
        grad_a_log,
        bias_total.reshape(width),
        skip_total.reshape(width),
        dt_gain_total.reshape(rank),
        bc_gain_total.reshape(bc_width),
    )


def solution(mesh):
    return jax.shard_map(
        body,
        mesh=mesh,
        in_specs=(
            P("dp", None, "tensor"),
            P("dp", "tensor", None),
            P("dp", "tensor", None),
            P("dp", None, "tensor"),
            P(None, "tensor"),
            P(None, "tensor"),
            P(None, "tensor"),
            P("tensor"),
            P(None, "tensor"),
            P("tensor"),
            P(),
            P(),
        ),
        out_specs=(
            P("dp", None, "tensor"),
            P("dp", "tensor"),
            P("dp", "tensor"),
            P(None, "tensor"),
            P(None, "tensor"),
            P("tensor"),
            P("tensor"),
            P(),
            P(),
        ),
        check_vma=False,
    )
```

```python
import functools
import math

import jax
import jax.numpy as jnp
from jax import lax
from jax.experimental import pallas as pl
from jax.experimental.pallas import tpu as pltpu
from jax.sharding import PartitionSpec as P

norm_eps = 1e-06
state_floor = 0.25
log2_e = 1.4426950408889634
lane = 128
f32 = jnp.float32
bf16 = jnp.bfloat16
contract_rows = (((0,), (0,)), ((), ()))
contract_cols = (((1,), (1,)), ((), ()))
in_vmem = pl.BlockSpec(memory_space=pltpu.VMEM)


def inverse_norms(proj, rank, state):
    dt_part = proj[:, :rank]
    b_part = proj[:, rank : rank + state]
    c_part = proj[:, rank + state : rank + 2 * state]
    dt_square = jnp.mean(dt_part * dt_part, axis=1, keepdims=True)
    b_square = jnp.mean(b_part * b_part, axis=1, keepdims=True)
    c_square = jnp.mean(c_part * c_part, axis=1, keepdims=True)
    return (
        (dt_part, lax.rsqrt(dt_square + norm_eps)),
        (b_part, lax.rsqrt(jnp.maximum(b_square, state_floor)), b_square),
        (c_part, lax.rsqrt(jnp.maximum(c_square, state_floor)), c_square),
    )


def scan_kernel(
    proj_ref,
    x_ref,
    gy_ref,
    w_ref,
    bias_ref,
    alog_ref,
    skip_ref,
    dt_gain_ref,
    bc_gain_ref,
    normed_ref,
    w_part_ref,
    xg_ref,
    misc_ref,
    dt_s,
    gy_s,
    src_s,
    sig_s,
    a2_s,
    low_s,
    bcb_s,
    u_s,
    b_acc,
    c_acc,
    s1_s,
    s2_s,
    *,
    wide_lanes,
    scale,
):
    tokens, width = x_ref.shape
    state = alog_ref.shape[0]
    rank = w_ref.shape[0]
    dt_norm, b_norm, c_norm = inverse_norms(proj_ref[...].astype(f32), rank, state)
    low_s[...] = (dt_norm[0] * dt_norm[1] * dt_gain_ref[...]).astype(bf16)
    b_rows = b_norm[0] * b_norm[1] * bc_gain_ref[:, :state]
    c_rows = c_norm[0] * c_norm[1] * bc_gain_ref[:, state:]
    bcb_s[:, :state] = jnp.broadcast_to(b_rows[:, :, None], (tokens, state, lane))
    bcb_s[:, state:] = jnp.broadcast_to(c_rows[:, :, None], (tokens, state, lane))
    pre = jnp.dot(low_s[...], w_ref[...], preferred_element_type=f32) + bias_ref[...]
    small = jnp.exp(-jnp.abs(pre))
    dt_rows = jnp.maximum(pre, 0.0) + jnp.log1p(small)
    sig_s[...] = jnp.where(pre >= 0, 1.0, small) / (1.0 + small)
    x_float = x_ref[...].astype(f32)
    gy_float = gy_ref[...].astype(f32)
    dt_s[...] = dt_rows
    gy_s[...] = gy_float
    src_s[...] = dt_rows * x_float
    a_mat = -jnp.exp(alog_ref[...])
    a2_s[...] = a_mat * log2_e
    b_acc[...] = jnp.zeros_like(b_acc)
    c_acc[...] = jnp.zeros_like(c_acc)
    reps = wide_lanes // lane

    def widen(part):
        return jnp.concatenate([part] * reps, axis=1)

    def fold(part):
        total = part[:, :lane]
        for rep in range(1, reps):
            total = total + part[:, rep * lane : (rep + 1) * lane]
        return total

    def fold_states(part):
        total = part[:8]
        for rep in range(1, state // 8):
            total = total + part[rep * 8 : (rep + 1) * 8]
        return total

    row_ids = lax.broadcasted_iota(jnp.int32, (8, wide_lanes), 0)

    def join_rows(early, late, level):
        mine = (row_ids & level) == 0
        kept = jnp.where(mine, early, late)
        moved = jnp.where(mine, late, early)
        return kept + pltpu.roll(moved, 8 - level, 0)

    for group in range(width // wide_lanes):
        cols = slice(group * wide_lanes, (group + 1) * wide_lanes)

        def forward(block, held):
            a2 = a2_s[:, cols]
            for offset in range(8):
                t = block * 8 + offset
                decayed = jnp.exp2(dt_s[pl.ds(t, 1), cols] * a2) * held
                u_s[pl.ds(t, 1), :, cols] = decayed[None]
                c_acc[pl.ds(t, 1)] += fold(decayed * gy_s[pl.ds(t, 1), cols])[None]
                held = decayed + src_s[pl.ds(t, 1), cols] * widen(bcb_s[t, :state])
            return held

        zeros = jnp.zeros((state, wide_lanes), f32)
        lax.fori_loop(0, tokens // 8, forward, zeros)

        def backward(step, carry):
            later, a_total = carry
            block = tokens // 8 - 1 - step
            a2 = a2_s[:, cols]
            waiting = {}
            for offset in range(7, -1, -1):
                t = block * 8 + offset
                dt_now = dt_s[pl.ds(t, 1), cols]
                adjoint = widen(bcb_s[t, state:]) * gy_s[pl.ds(t, 1), cols] + later
                through = adjoint * u_s[t, :, cols]
                first = fold_states(adjoint * widen(bcb_s[t, :state]))
                second = fold_states(through * a2)
                level = 1
                while level in waiting:
                    later_first, later_second = waiting.pop(level)
                    first = join_rows(first, later_first, level)
                    second = join_rows(second, later_second, level)
                    level *= 2
                waiting[level] = (first, second)
                b_acc[pl.ds(t, 1)] += fold(adjoint * src_s[pl.ds(t, 1), cols])[None]
                a_total = a_total + dt_now * through
                later = jnp.exp2(dt_now * a2) * adjoint
            s1_s[pl.ds(block * 8, 8), cols], s2_s[pl.ds(block * 8, 8), cols] = waiting[8]
            return later, a_total

        _, a_total = lax.fori_loop(0, tokens // 8, backward, (zeros, zeros))
        misc_ref[:state, cols] = (scale / log2_e) * (a_total * a2_s[:, cols])

    s1 = s1_s[...]
    xg_ref[...] = dt_s[...] * s1 + skip_ref[...] * gy_s[...]
    dt_grad = x_ref[...].astype(f32) * s1 + s2_s[...] * (1.0 / log2_e)
    pre_float = dt_grad * sig_s[...]
    pre_grad = pre_float.astype(bf16)
    misc_ref[state : state + 1, :] = scale * jnp.sum(pre_float, axis=0, keepdims=True)
    misc_ref[state + 1 : state + 2, :] = scale * jnp.sum(
        gy_s[...] * x_ref[...].astype(f32), axis=0, keepdims=True
    )
    dt_normed = lax.dot_general(
        pre_grad, w_ref[...], contract_cols, preferred_element_type=f32
    ).astype(bf16)
    w_part_ref[...] = (
        scale
        * lax.dot_general(low_s[...], pre_grad, contract_rows, preferred_element_type=f32)
    ).astype(bf16)
    source_sum = jnp.sum(src_s[...] * gy_s[...], axis=1, keepdims=True)
    b_grad = jnp.sum(b_acc[...], axis=2)
    c_grad = jnp.sum(c_acc[...], axis=2) + b_rows * source_sum
    b_grad = b_grad.astype(bf16)
    c_grad = c_grad.astype(bf16)
    z_size, y_size, own = normed_ref.shape[1], normed_ref.shape[0], normed_ref.shape[2]
    for y in range(y_size):
        for z in range(z_size):
            rows = slice((z * y_size + y) * own, (z * y_size + y + 1) * own)
            normed_ref[y, z, :, :rank] = dt_normed[rows]
            normed_ref[y, z, :, rank : rank + state] = b_grad[rows]
            normed_ref[y, z, :, rank + state : rank + 2 * state] = c_grad[rows]
            normed_ref[y, z, :, rank + 2 * state :] = jnp.zeros(
                (own, lane - 2 * state), bf16
            )


def sum_kernel(parts_ref, out_ref):
    total = parts_ref[0].astype(f32)
    for peer in range(1, parts_ref.shape[0]):
        total = total + parts_ref[peer].astype(f32)
    out_ref[...] = total


def norm_kernel(
    y_ref, mine_ref, other_ref, proj_ref, dt_gain_ref, bc_gain_ref, out_ref, pack_s, *, state
):
    rank = dt_gain_ref.shape[1]
    rows = mine_ref.shape[0]
    grads = mine_ref[...] + other_ref[...]
    proj = jnp.concatenate([proj_ref[z, y_ref[0]] for z in range(proj_ref.shape[0])], axis=0)
    dt_norm, b_norm, c_norm = inverse_norms(proj.astype(f32), rank, state)
    dt_grad = grads[:, :rank]
    dt_unit = dt_norm[0] * dt_norm[1]
    dt_cot = dt_grad * dt_gain_ref[...]
    dt_mean = jnp.mean(dt_cot * dt_unit, axis=1, keepdims=True)
    pack_s[:, rank:] = jnp.zeros((rows, lane), f32)
    pack_s[:, :rank] = dt_norm[1] * (dt_cot - dt_unit * dt_mean)
    dt_gain_part = jnp.sum(dt_grad * dt_unit, axis=0, keepdims=True)
    last = rank + lane // 2
    for piece in range(rank // (lane // 2)):
        pack_s[piece : piece + 1, last:] = dt_gain_part[
            :, piece * (lane // 2) : (piece + 1) * (lane // 2)
        ]
    gain_row = rank // (lane // 2)
    for index, part in enumerate((b_norm, c_norm)):
        start = rank + index * state
        grad = grads[:, start : start + state]
        unit = part[0] * part[1]
        cot = grad * bc_gain_ref[:, index * state : (index + 1) * state]
        mean = jnp.mean(cot * unit, axis=1, keepdims=True)
        inner = jnp.where(part[2] > state_floor, mean, 0.0)
        inner = jnp.where(part[2] == state_floor, 0.5 * mean, inner)
        pack_s[:, start : start + state] = part[1] * (cot - unit * inner)
        pack_s[gain_row : gain_row + 1, last + index * state : last + (index + 1) * state] = (
            jnp.sum(grad * unit, axis=0, keepdims=True)
        )
    gains = pack_s[: rows // 2, last:]
    pack_s[rows // 2 :, last:] = gains - gains.astype(bf16).astype(f32)
    packed = pack_s[...].astype(bf16)
    for peer in range(out_ref.shape[0]):
        out_ref[peer] = packed


def project_kernel(
    core_ref,
    low_ref,
    xg_ref,
    x_ref,
    w_xdt_ref,
    w_xbc_ref,
    w_part_ref,
    misc_ref,
    grad_x_ref,
    keep_ref,
    send_ref,
    out_ref,
    all_s,
    low_s,
    *,
    scale,
):
    rank, width = w_xdt_ref.shape
    bc_width = w_xbc_ref.shape[0]
    y_size, z_size, own, _ = low_ref.shape
    for y in range(y_size):
        for z in range(z_size):
            start = (z * y_size + y) * own
            low_s[start : start + own, :] = low_ref[y, z]
    dt_low = low_s[:, :rank]
    bc_low = low_s[:, rank : rank + bc_width]
    summed = xg_ref[...] + jnp.dot(dt_low, w_xdt_ref[...], preferred_element_type=f32)
    summed = summed + jnp.dot(bc_low, w_xbc_ref[...], preferred_element_type=f32)
    grad_x_ref[...] = summed.astype(bf16)
    out_ref[:, :width] = (
        scale
        * lax.dot_general(dt_low, x_ref[...], contract_rows, preferred_element_type=f32)
    ).astype(bf16)
    out_ref[:, width : 2 * width] = w_part_ref[...]
    state = bc_width // 2
    all_s[...] = jnp.zeros_like(all_s)
    all_s[: state + 2, :] = misc_ref[: state + 2, :]
    all_s[state + 8 : state + 8 + bc_width, :] = scale * lax.dot_general(
        bc_low, x_ref[...], contract_rows, preferred_element_type=f32
    )
    gains = jnp.zeros((own, lane), f32)
    for y in range(y_size):
        for z in range(z_size):
            gains = gains + low_ref[y, z, :, rank:].astype(f32)
    gains = scale * gains[:, lane // 2 :]
    gain_row = state + 8 + bc_width
    for piece in range(rank // (lane // 2)):
        all_s[gain_row : gain_row + 1, piece * (lane // 2) : (piece + 1) * (lane // 2)] = gains[
            piece : piece + 1
        ]
    piece = rank // (lane // 2)
    all_s[gain_row : gain_row + 1, rank : rank + bc_width] = gains[piece : piece + 1, :bc_width]
    for piece in range(width // lane):
        out_ref[piece * 64 : (piece + 1) * 64, 2 * width :] = all_s[
            :, piece * lane : (piece + 1) * lane
        ].astype(bf16)
    first_core = core_ref[0] == 0
    for pair in range(keep_ref.shape[0]):
        even = out_ref[32 * pair : 32 * pair + 16, :]
        odd = out_ref[32 * pair + 16 : 32 * pair + 32, :]
        keep_ref[pair] = jnp.where(first_core, even, odd)
        send_ref[pair] = jnp.where(first_core, odd, even)


def total_kernel(parts_ref, xdt_ref, dt_ref, own_ref):
    width = xdt_ref.shape[1]
    total = parts_ref[0].astype(f32)
    for peer in range(1, parts_ref.shape[0]):
        total = total + parts_ref[peer].astype(f32)
    xdt_ref[...] = total[:, :width]
    dt_ref[...] = total[:, width : 2 * width]
    for peer in range(own_ref.shape[0]):
        own_ref[peer] = total[:, 2 * width :]


def spread_kernel(
    parts_ref, xbc_ref, alog_ref, bias_ref, skip_ref, dt_gain_ref, bc_gain_ref, all_s, *, order
):
    state = alog_ref.shape[0]
    bc_width = xbc_ref.shape[0]
    rank = dt_gain_ref.shape[1]
    for block, (peer, place) in enumerate(order):
        row, piece = 16 * (block % 4), lane * (block // 4)
        all_s[row : row + 16, piece : piece + lane] = parts_ref[
            peer, :, place * lane : (place + 1) * lane
        ]
    alog_ref[...] = all_s[:state, :]
    bias_ref[...] = all_s[state : state + 1, :]
    skip_ref[...] = all_s[state + 1 : state + 2, :]
    xbc_ref[...] = all_s[state + 8 : state + 8 + bc_width, :]
    gain_row = state + 8 + bc_width
    dt_gain_ref[...] = all_s[gain_row : gain_row + 1, :rank]
    bc_gain_ref[...] = all_s[gain_row : gain_row + 1, rank : rank + bc_width]


def call(kernel, name, outs, scratch, limit_mib, *args):
    in_smem = pl.BlockSpec(memory_space=pltpu.SMEM)
    return pl.pallas_call(
        kernel,
        out_shape=tuple(jax.ShapeDtypeStruct(shape, dtype) for shape, dtype in outs),
        in_specs=[in_smem if arg.dtype == jnp.int32 else in_vmem for arg in args],
        out_specs=tuple([in_vmem] * len(outs)),
        scratch_shapes=[pltpu.VMEM(shape, dtype) for shape, dtype in scratch],
        compiler_params=pltpu.CompilerParams(vmem_limit_bytes=limit_mib * 2**20),
        name=name,
    )(*args)


def send_to_all(block, axis, groups=None):
    return lax.all_to_all(block, axis, 0, 0, axis_index_groups=groups)


def sum_low(parts):
    return jnp.sum(parts.astype(f32), axis=0).astype(bf16)


def body(
    x_inner, proj_dt, proj_bc, grad_y, w_xdt, w_xbc, w_dt, dt_bias, a_log, d_skip, dt_gain, bc_gain
):
    x_rows = x_inner[0]
    gy_rows = grad_y[0]
    tokens, width = x_rows.shape
    rank = proj_dt.shape[2]
    bc_width = proj_bc.shape[2]
    state = bc_width // 2
    own = proj_dt.shape[1]
    dp = lax.axis_size("dp")
    tensor = lax.axis_size("tensor")
    scale = 1.0 / math.sqrt(dp * tokens)
    bias_row = dt_bias.reshape(1, width)
    skip_row = d_skip.reshape(1, width)
    dt_gain_row = dt_gain.reshape(1, rank)
    bc_gain_row = bc_gain.reshape(1, bc_width)

    columns = rank + lane
    own_proj = jnp.concatenate(
        [proj_dt[0], proj_bc[0], jnp.zeros((own, lane - bc_width), bf16)], axis=1
    )
    full_proj = send_to_all(
        jnp.broadcast_to(own_proj[None], (tensor, own, columns)), "tensor"
    ).reshape(tokens, columns)

    z_pair = 2
    y_size = tensor // z_pair
    along_y = [[z * y_size + y for y in range(y_size)] for z in range(z_pair)]
    rows = ((tokens, width), f32)
    by_token = (y_size, z_pair, own, columns)
    normed_part, w_part, xg, misc = call(
        functools.partial(scan_kernel, wide_lanes=min(512, width), scale=scale),
        "scan",
        [
            (by_token, bf16),
            ((rank, width), bf16),
            ((tokens, width), f32),
            ((state + 8, width), f32),
        ],
        [
            rows,
            rows,
            rows,
            rows,
            ((state, width), f32),
            ((tokens, rank), bf16),
            ((tokens, 2 * state, lane), f32),
            ((tokens, state, width), f32),
            ((tokens, state, lane), f32),
            ((tokens, state, lane), f32),
            rows,
            rows,
        ],
        42,
        full_proj,
        x_rows,
        gy_rows,
        w_dt,
        bias_row,
        a_log,
        skip_row,
        dt_gain_row,
        bc_gain_row,
    )
    shared_rows = z_pair * own
    normed_parts = send_to_all(
        normed_part.reshape(y_size, shared_rows, columns), "tensor", along_y
    )
    (mine,) = call(
        sum_kernel, "join", [((shared_rows, columns), f32)], [], 4, normed_parts
    )
    other = lax.ppermute(
        mine, "tensor", [(index, (index + y_size) % tensor) for index in range(tensor)]
    )
    y_index = (lax.axis_index("tensor") % y_size).astype(jnp.int32).reshape(1)
    (own_low,) = call(
        functools.partial(norm_kernel, state=state),
        "norm",
        [((y_size, shared_rows, columns), bf16)],
        [((shared_rows, columns), f32)],
        4,
        y_index,
        mine,
        other,
        full_proj.reshape(z_pair, y_size, own, columns),
        dt_gain_row,
        bc_gain_row,
    )
    low = send_to_all(own_low, "tensor", along_y).reshape(by_token)
    cores, z_size = 2, 4
    x_size = dp // (cores * z_size)
    core = (lax.axis_index("dp") % cores).astype(jnp.int32).reshape(1)
    per_device = rank // dp
    row_width = 2 * width + lane
    half = ((x_size * z_size, per_device, row_width), bf16)
    grad_x, kept, sent = call(
        functools.partial(project_kernel, scale=scale),
        "project",
        [((tokens, width), bf16), half, half],
        [
            ((rank, row_width), bf16),
            ((64, width), f32),
            ((tokens, columns), bf16),
        ],
        16,
        core,
        low,
        xg,
        x_rows,
        w_xdt,
        w_xbc,
        w_part,
        misc,
    )
    other_core = [(index, index ^ 1) for index in range(dp)]
    kept = (kept.astype(f32) + lax.ppermute(sent, "dp", other_core).astype(f32)).astype(bf16)
    z_stride, x_stride = cores, cores * z_size
    along_x = [[x * x_stride + rest for x in range(x_size)] for rest in range(x_stride)]
    along_z = [
        [x * x_stride + z * z_stride + c for z in range(z_size)]
        for x in range(x_size)
        for c in range(cores)
    ]
    along_xc = [
        [x * x_stride + z * z_stride + c for x in range(x_size) for c in range(cores)]
        for z in range(z_size)
    ]
    by_x = sum_low(
        send_to_all(kept.reshape(x_size, z_size, per_device, row_width), "dp", along_x)
    )
    by_z = by_x[:, :, 2 * width :].transpose(1, 0, 2).reshape(1, per_device, z_size * lane)
    by_z = jnp.broadcast_to(by_z, (z_size, per_device, z_size * lane))
    by_z = jnp.concatenate([by_x[:, :, : 2 * width], by_z], axis=2)
    all_parts = send_to_all(by_z, "dp", along_z)
    shared = x_size * cores
    grad_w_xdt, grad_w_dt, own_total = call(
        total_kernel,
        "total",
        [
            ((per_device, width), f32),
            ((per_device, width), f32),
            ((shared, per_device, z_size * lane), f32),
        ],
        [],
        4,
        all_parts,
    )
    totals = send_to_all(own_total, "dp", along_xc)
    order = tuple(
        (x * cores + c, z) for x in range(x_size) for z in range(z_size) for c in range(cores)
    )
    grad_w_xbc, grad_a_log, bias_total, skip_total, dt_gain_total, bc_gain_total = call(
        functools.partial(spread_kernel, order=order),
        "spread",
        [
            ((bc_width, width), f32),
            ((state, width), f32),
            ((1, width), f32),
            ((1, width), f32),
            ((1, rank), f32),
            ((1, bc_width), f32),
        ],
        [((64, width), f32)],
        4,
        totals,
    )
    return (
        grad_x[None],
        grad_w_xdt,
        grad_w_dt,
        grad_w_xbc,
        grad_a_log,
        bias_total.reshape(width),
        skip_total.reshape(width),
        dt_gain_total.reshape(rank),
        bc_gain_total.reshape(bc_width),
    )


def solution(mesh):
    return jax.shard_map(
        body,
        mesh=mesh,
        in_specs=(
            P("dp", None, "tensor"),
            P("dp", "tensor", None),
            P("dp", "tensor", None),
            P("dp", None, "tensor"),
            P(None, "tensor"),
            P(None, "tensor"),
            P(None, "tensor"),
            P("tensor"),
            P(None, "tensor"),
            P("tensor"),
            P(),
            P(),
        ),
        out_specs=(
            P("dp", None, "tensor"),
            P("dp", "tensor"),
            P("dp", "tensor"),
            P(None, "tensor"),
            P(None, "tensor"),
            P("tensor"),
            P("tensor"),
            P(),
            P(),
        ),
        check_vma=False,
    )
```

```python
import functools
import math

import jax
import jax.numpy as jnp
from jax import lax
from jax.experimental import pallas as pl
from jax.experimental.pallas import tpu as pltpu
from jax.sharding import PartitionSpec as P

norm_eps = 1e-06
state_floor = 0.25
log2_e = 1.4426950408889634
lane = 128
f32 = jnp.float32
bf16 = jnp.bfloat16
contract_rows = (((0,), (0,)), ((), ()))
contract_cols = (((1,), (1,)), ((), ()))
in_vmem = pl.BlockSpec(memory_space=pltpu.VMEM)


def inverse_norms(proj, rank, state):
    dt_part = proj[:, :rank]
    b_part = proj[:, rank : rank + state]
    c_part = proj[:, rank + state : rank + 2 * state]
    dt_square = jnp.mean(dt_part * dt_part, axis=1, keepdims=True)
    b_square = jnp.mean(b_part * b_part, axis=1, keepdims=True)
    c_square = jnp.mean(c_part * c_part, axis=1, keepdims=True)
    return (
        (dt_part, lax.rsqrt(dt_square + norm_eps)),
        (b_part, lax.rsqrt(jnp.maximum(b_square, state_floor)), b_square),
        (c_part, lax.rsqrt(jnp.maximum(c_square, state_floor)), c_square),
    )


def split_cores(core_ref, whole, keep_ref, send_ref):
    first_core = core_ref[0] == 0
    for pair in range(keep_ref.shape[0]):
        even = whole[32 * pair : 32 * pair + 16]
        odd = whole[32 * pair + 16 : 32 * pair + 32]
        keep_ref[pair] = jnp.where(first_core, even, odd)
        send_ref[pair] = jnp.where(first_core, odd, even)


def scan_kernel(
    core_ref,
    proj_ref,
    x_ref,
    gy_ref,
    w_ref,
    bias_ref,
    alog_ref,
    skip_ref,
    dt_gain_ref,
    bc_gain_ref,
    normed_ref,
    w_keep_ref,
    w_send_ref,
    xg_ref,
    misc_ref,
    dt_s,
    gy_s,
    src_s,
    sig_s,
    a2_s,
    low_s,
    bcb_s,
    u_s,
    b_acc,
    c_acc,
    s1_s,
    s2_s,
    *,
    wide_lanes,
    scale,
):
    tokens, width = x_ref.shape
    state = alog_ref.shape[0]
    rank = w_ref.shape[0]
    dt_norm, b_norm, c_norm = inverse_norms(proj_ref[...].astype(f32), rank, state)
    low_s[...] = (dt_norm[0] * dt_norm[1] * dt_gain_ref[...]).astype(bf16)
    b_rows = b_norm[0] * b_norm[1] * bc_gain_ref[:, :state]
    c_rows = c_norm[0] * c_norm[1] * bc_gain_ref[:, state:]
    bcb_s[:, :state] = jnp.broadcast_to(b_rows[:, :, None], (tokens, state, lane))
    bcb_s[:, state:] = jnp.broadcast_to(c_rows[:, :, None], (tokens, state, lane))
    pre = jnp.dot(low_s[...], w_ref[...], preferred_element_type=f32) + bias_ref[...]
    small = jnp.exp(-jnp.abs(pre))
    dt_rows = jnp.maximum(pre, 0.0) + jnp.log1p(small)
    sig_s[...] = jnp.where(pre >= 0, 1.0, small) / (1.0 + small)
    x_float = x_ref[...].astype(f32)
    gy_float = gy_ref[...].astype(f32)
    dt_s[...] = dt_rows
    gy_s[...] = gy_float
    src_s[...] = dt_rows * x_float
    a_mat = -jnp.exp(alog_ref[...])
    a2_s[...] = a_mat * log2_e
    b_acc[...] = jnp.zeros_like(b_acc)
    c_acc[...] = jnp.zeros_like(c_acc)
    reps = wide_lanes // lane

    def widen(part):
        return jnp.concatenate([part] * reps, axis=1)

    def fold(part):
        total = part[:, :lane]
        for rep in range(1, reps):
            total = total + part[:, rep * lane : (rep + 1) * lane]
        return total

    def fold_states(part):
        total = part[:8]
        for rep in range(1, state // 8):
            total = total + part[rep * 8 : (rep + 1) * 8]
        return total

    row_ids = lax.broadcasted_iota(jnp.int32, (8, wide_lanes), 0)

    def join_rows(early, late, level):
        mine = (row_ids & level) == 0
        kept = jnp.where(mine, early, late)
        moved = jnp.where(mine, late, early)
        return kept + pltpu.roll(moved, 8 - level, 0)

    for group in range(width // wide_lanes):
        cols = slice(group * wide_lanes, (group + 1) * wide_lanes)

        def forward(block, held):
            a2 = a2_s[:, cols]
            for offset in range(8):
                t = block * 8 + offset
                decayed = jnp.exp2(dt_s[pl.ds(t, 1), cols] * a2) * held
                u_s[pl.ds(t, 1), :, cols] = decayed[None]
                c_acc[pl.ds(t, 1)] += fold(decayed * gy_s[pl.ds(t, 1), cols])[None]
                held = decayed + src_s[pl.ds(t, 1), cols] * widen(bcb_s[t, :state])
            return held

        zeros = jnp.zeros((state, wide_lanes), f32)
        lax.fori_loop(0, tokens // 8, forward, zeros)

        def backward(step, carry):
            later, a_total = carry
            block = tokens // 8 - 1 - step
            a2 = a2_s[:, cols]
            waiting = {}
            for offset in range(7, -1, -1):
                t = block * 8 + offset
                dt_now = dt_s[pl.ds(t, 1), cols]
                adjoint = widen(bcb_s[t, state:]) * gy_s[pl.ds(t, 1), cols] + later
                through = adjoint * u_s[t, :, cols]
                first = fold_states(adjoint * widen(bcb_s[t, :state]))
                second = fold_states(through * a2)
                level = 1
                while level in waiting:
                    later_first, later_second = waiting.pop(level)
                    first = join_rows(first, later_first, level)
                    second = join_rows(second, later_second, level)
                    level *= 2
                waiting[level] = (first, second)
                b_acc[pl.ds(t, 1)] += fold(adjoint * src_s[pl.ds(t, 1), cols])[None]
                a_total = a_total + dt_now * through
                later = jnp.exp2(dt_now * a2) * adjoint
            s1_s[pl.ds(block * 8, 8), cols], s2_s[pl.ds(block * 8, 8), cols] = waiting[8]
            return later, a_total

        _, a_total = lax.fori_loop(0, tokens // 8, backward, (zeros, zeros))
        misc_ref[:state, cols] = (scale / log2_e) * (a_total * a2_s[:, cols])

    s1 = s1_s[...]
    xg_ref[...] = dt_s[...] * s1 + skip_ref[...] * gy_s[...]
    dt_grad = x_ref[...].astype(f32) * s1 + s2_s[...] * (1.0 / log2_e)
    pre_float = dt_grad * sig_s[...]
    pre_grad = pre_float.astype(bf16)
    misc_ref[state : state + 1, :] = scale * jnp.sum(pre_float, axis=0, keepdims=True)
    misc_ref[state + 1 : state + 2, :] = scale * jnp.sum(
        gy_s[...] * x_ref[...].astype(f32), axis=0, keepdims=True
    )
    dt_normed = lax.dot_general(
        pre_grad, w_ref[...], contract_cols, preferred_element_type=f32
    ).astype(bf16)
    w_part = scale * lax.dot_general(
        low_s[...], pre_grad, contract_rows, preferred_element_type=f32
    )
    split_cores(core_ref, w_part.astype(bf16), w_keep_ref, w_send_ref)
    source_sum = jnp.sum(src_s[...] * gy_s[...], axis=1, keepdims=True)
    b_grad = jnp.sum(b_acc[...], axis=2)
    c_grad = jnp.sum(c_acc[...], axis=2) + b_rows * source_sum
    b_grad = b_grad.astype(bf16)
    c_grad = c_grad.astype(bf16)
    z_size, y_size, own = normed_ref.shape[1], normed_ref.shape[0], normed_ref.shape[2]
    for y in range(y_size):
        for z in range(z_size):
            rows = slice((z * y_size + y) * own, (z * y_size + y + 1) * own)
            normed_ref[y, z, :, :rank] = dt_normed[rows]
            normed_ref[y, z, :, rank : rank + state] = b_grad[rows]
            normed_ref[y, z, :, rank + state : rank + 2 * state] = c_grad[rows]
            normed_ref[y, z, :, rank + 2 * state :] = jnp.zeros(
                (own, lane - 2 * state), bf16
            )


def sum_kernel(parts_ref, out_ref):
    total = parts_ref[0].astype(f32)
    for peer in range(1, parts_ref.shape[0]):
        total = total + parts_ref[peer].astype(f32)
    out_ref[...] = total


def norm_kernel(
    y_ref, mine_ref, other_ref, proj_ref, dt_gain_ref, bc_gain_ref, out_ref, pack_s, *, state
):
    rank = dt_gain_ref.shape[1]
    rows = mine_ref.shape[0]
    grads = mine_ref[...] + other_ref[...]
    proj = jnp.concatenate([proj_ref[z, y_ref[0]] for z in range(proj_ref.shape[0])], axis=0)
    dt_norm, b_norm, c_norm = inverse_norms(proj.astype(f32), rank, state)
    dt_grad = grads[:, :rank]
    dt_unit = dt_norm[0] * dt_norm[1]
    dt_cot = dt_grad * dt_gain_ref[...]
    dt_mean = jnp.mean(dt_cot * dt_unit, axis=1, keepdims=True)
    pack_s[:, rank:] = jnp.zeros((rows, lane), f32)
    pack_s[:, :rank] = dt_norm[1] * (dt_cot - dt_unit * dt_mean)
    dt_gain_part = jnp.sum(dt_grad * dt_unit, axis=0, keepdims=True)
    last = rank + lane // 2
    for piece in range(rank // (lane // 2)):
        pack_s[piece : piece + 1, last:] = dt_gain_part[
            :, piece * (lane // 2) : (piece + 1) * (lane // 2)
        ]
    gain_row = rank // (lane // 2)
    for index, part in enumerate((b_norm, c_norm)):
        start = rank + index * state
        grad = grads[:, start : start + state]
        unit = part[0] * part[1]
        cot = grad * bc_gain_ref[:, index * state : (index + 1) * state]
        mean = jnp.mean(cot * unit, axis=1, keepdims=True)
        inner = jnp.where(part[2] > state_floor, mean, 0.0)
        inner = jnp.where(part[2] == state_floor, 0.5 * mean, inner)
        pack_s[:, start : start + state] = part[1] * (cot - unit * inner)
        pack_s[gain_row : gain_row + 1, last + index * state : last + (index + 1) * state] = (
            jnp.sum(grad * unit, axis=0, keepdims=True)
        )
    gains = pack_s[: rows // 2, last:]
    pack_s[rows // 2 :, last:] = gains - gains.astype(bf16).astype(f32)
    packed = pack_s[...].astype(bf16)
    for peer in range(out_ref.shape[0]):
        out_ref[peer] = packed


def project_kernel(
    core_ref,
    low_ref,
    xg_ref,
    x_ref,
    w_xdt_ref,
    w_xbc_ref,
    misc_ref,
    grad_x_ref,
    keep_ref,
    send_ref,
    out_s,
    all_s,
    low_s,
    *,
    scale,
):
    rank, width = w_xdt_ref.shape
    bc_width = w_xbc_ref.shape[0]
    y_size, z_size, own, _ = low_ref.shape
    for y in range(y_size):
        for z in range(z_size):
            start = (z * y_size + y) * own
            low_s[start : start + own, :] = low_ref[y, z]
    dt_low = low_s[:, :rank]
    bc_low = low_s[:, rank : rank + bc_width]
    summed = xg_ref[...] + jnp.dot(dt_low, w_xdt_ref[...], preferred_element_type=f32)
    summed = summed + jnp.dot(bc_low, w_xbc_ref[...], preferred_element_type=f32)
    grad_x_ref[...] = summed.astype(bf16)
    out_s[:, :width] = (
        scale
        * lax.dot_general(dt_low, x_ref[...], contract_rows, preferred_element_type=f32)
    ).astype(bf16)
    state = bc_width // 2
    all_s[...] = jnp.zeros_like(all_s)
    all_s[: state + 2, :] = misc_ref[: state + 2, :]
    all_s[state + 8 : state + 8 + bc_width, :] = scale * lax.dot_general(
        bc_low, x_ref[...], contract_rows, preferred_element_type=f32
    )
    gains = jnp.zeros((own, lane), f32)
    for y in range(y_size):
        for z in range(z_size):
            gains = gains + low_ref[y, z, :, rank:].astype(f32)
    gains = scale * gains[:, lane // 2 :]
    gain_row = state + 8 + bc_width
    for piece in range(rank // (lane // 2)):
        all_s[gain_row : gain_row + 1, piece * (lane // 2) : (piece + 1) * (lane // 2)] = gains[
            piece : piece + 1
        ]
    piece = rank // (lane // 2)
    all_s[gain_row : gain_row + 1, rank : rank + bc_width] = gains[piece : piece + 1, :bc_width]
    for piece in range(width // lane):
        out_s[piece * 64 : (piece + 1) * 64, width:] = all_s[
            :, piece * lane : (piece + 1) * lane
        ].astype(bf16)
    split_cores(core_ref, out_s, keep_ref, send_ref)


def total_kernel(parts_ref, xdt_ref, dt_ref, own_ref):
    width = xdt_ref.shape[1]
    total = parts_ref[0].astype(f32)
    for peer in range(1, parts_ref.shape[0]):
        total = total + parts_ref[peer].astype(f32)
    xdt_ref[...] = total[:, :width]
    dt_ref[...] = total[:, width : 2 * width]
    for peer in range(own_ref.shape[0]):
        own_ref[peer] = total[:, 2 * width :]


def spread_kernel(
    parts_ref, xbc_ref, alog_ref, bias_ref, skip_ref, dt_gain_ref, bc_gain_ref, all_s, *, order
):
    state = alog_ref.shape[0]
    bc_width = xbc_ref.shape[0]
    rank = dt_gain_ref.shape[1]
    for block, (peer, place) in enumerate(order):
        row, piece = 16 * (block % 4), lane * (block // 4)
        all_s[row : row + 16, piece : piece + lane] = parts_ref[
            peer, :, place * lane : (place + 1) * lane
        ]
    alog_ref[...] = all_s[:state, :]
    bias_ref[...] = all_s[state : state + 1, :]
    skip_ref[...] = all_s[state + 1 : state + 2, :]
    xbc_ref[...] = all_s[state + 8 : state + 8 + bc_width, :]
    gain_row = state + 8 + bc_width
    dt_gain_ref[...] = all_s[gain_row : gain_row + 1, :rank]
    bc_gain_ref[...] = all_s[gain_row : gain_row + 1, rank : rank + bc_width]


def call(kernel, name, outs, scratch, limit_mib, *args):
    in_smem = pl.BlockSpec(memory_space=pltpu.SMEM)
    return pl.pallas_call(
        kernel,
        out_shape=tuple(jax.ShapeDtypeStruct(shape, dtype) for shape, dtype in outs),
        in_specs=[in_smem if arg.dtype == jnp.int32 else in_vmem for arg in args],
        out_specs=tuple([in_vmem] * len(outs)),
        scratch_shapes=[pltpu.VMEM(shape, dtype) for shape, dtype in scratch],
        compiler_params=pltpu.CompilerParams(vmem_limit_bytes=limit_mib * 2**20),
        name=name,
    )(*args)


def send_to_all(block, axis, groups=None):
    return lax.all_to_all(block, axis, 0, 0, axis_index_groups=groups)


def sum_low(parts):
    return jnp.sum(parts.astype(f32), axis=0).astype(bf16)


def body(
    x_inner, proj_dt, proj_bc, grad_y, w_xdt, w_xbc, w_dt, dt_bias, a_log, d_skip, dt_gain, bc_gain
):
    x_rows = x_inner[0]
    gy_rows = grad_y[0]
    tokens, width = x_rows.shape
    rank = proj_dt.shape[2]
    bc_width = proj_bc.shape[2]
    state = bc_width // 2
    own = proj_dt.shape[1]
    dp = lax.axis_size("dp")
    tensor = lax.axis_size("tensor")
    scale = 1.0 / math.sqrt(dp * tokens)
    bias_row = dt_bias.reshape(1, width)
    skip_row = d_skip.reshape(1, width)
    dt_gain_row = dt_gain.reshape(1, rank)
    bc_gain_row = bc_gain.reshape(1, bc_width)

    columns = rank + lane
    own_proj = jnp.concatenate(
        [proj_dt[0], proj_bc[0], jnp.zeros((own, lane - bc_width), bf16)], axis=1
    )
    full_proj = send_to_all(
        jnp.broadcast_to(own_proj[None], (tensor, own, columns)), "tensor"
    ).reshape(tokens, columns)

    cores, z_size, z_pair = 2, 4, 2
    x_size = dp // (cores * z_size)
    y_size = tensor // z_pair
    per_device = rank // dp
    core = (lax.axis_index("dp") % cores).astype(jnp.int32).reshape(1)
    other_core = [(index, index ^ 1) for index in range(dp)]
    z_stride, x_stride = cores, cores * z_size
    along_x = [[x * x_stride + rest for x in range(x_size)] for rest in range(x_stride)]
    along_z = [
        [x * x_stride + z * z_stride + c for z in range(z_size)]
        for x in range(x_size)
        for c in range(cores)
    ]
    along_xc = [
        [x * x_stride + z * z_stride + c for x in range(x_size) for c in range(cores)]
        for z in range(z_size)
    ]
    along_y = [[z * y_size + y for y in range(y_size)] for z in range(z_pair)]

    def swap_cores(sent):
        return lax.ppermute(sent, "dp", other_core)

    def sum_over_x(kept, other):
        both = (kept.astype(f32) + other.astype(f32)).astype(bf16)
        blocks = both.reshape((x_size, z_size) + both.shape[1:])
        return sum_low(send_to_all(blocks, "dp", along_x))

    rows = ((tokens, width), f32)
    by_token = (y_size, z_pair, own, columns)
    half = (x_size * z_size, per_device)
    normed_part, w_kept, w_sent, xg, misc = call(
        functools.partial(scan_kernel, wide_lanes=min(512, width), scale=scale),
        "scan",
        [
            (by_token, bf16),
            (half + (width,), bf16),
            (half + (width,), bf16),
            ((tokens, width), f32),
            ((state + 8, width), f32),
        ],
        [
            rows,
            rows,
            rows,
            rows,
            ((state, width), f32),
            ((tokens, rank), bf16),
            ((tokens, 2 * state, lane), f32),
            ((tokens, state, width), f32),
            ((tokens, state, lane), f32),
            ((tokens, state, lane), f32),
            rows,
            rows,
        ],
        60,
        core,
        full_proj,
        x_rows,
        gy_rows,
        w_dt,
        bias_row,
        a_log,
        skip_row,
        dt_gain_row,
        bc_gain_row,
    )
    shared_rows = z_pair * own
    normed_parts = send_to_all(
        normed_part.reshape(y_size, shared_rows, columns), "tensor", along_y
    )
    (mine,) = call(
        sum_kernel, "join", [((shared_rows, columns), f32)], [], 4, normed_parts
    )
    mine, w_other = lax.optimization_barrier((mine, swap_cores(w_sent)))
    w_by_x = sum_over_x(w_kept, w_other)
    other = lax.ppermute(
        mine, "tensor", [(index, (index + y_size) % tensor) for index in range(tensor)]
    )
    other, w_by_x = lax.optimization_barrier((other, w_by_x))
    y_index = (lax.axis_index("tensor") % y_size).astype(jnp.int32).reshape(1)
    (own_low,) = call(
        functools.partial(norm_kernel, state=state),
        "norm",
        [((y_size, shared_rows, columns), bf16)],
        [((shared_rows, columns), f32)],
        4,
        y_index,
        mine,
        other,
        full_proj.reshape(z_pair, y_size, own, columns),
        dt_gain_row,
        bc_gain_row,
    )
    low = send_to_all(own_low, "tensor", along_y).reshape(by_token)
    half_row = (half + (width + lane,), bf16)
    grad_x, kept, sent = call(
        functools.partial(project_kernel, scale=scale),
        "project",
        [((tokens, width), bf16), half_row, half_row],
        [
            ((rank, width + lane), bf16),
            ((64, width), f32),
            ((tokens, columns), bf16),
        ],
        60,
        core,
        low,
        xg,
        x_rows,
        w_xdt,
        w_xbc,
        misc,
    )
    by_x = sum_over_x(kept, swap_cores(sent))
    by_z = by_x[:, :, width:].transpose(1, 0, 2).reshape(1, per_device, z_size * lane)
    by_z = jnp.broadcast_to(by_z, (z_size, per_device, z_size * lane))
    by_z = jnp.concatenate([by_x[:, :, :width], w_by_x, by_z], axis=2)
    all_parts = send_to_all(by_z, "dp", along_z)
    shared = x_size * cores
    grad_w_xdt, grad_w_dt, own_total = call(
        total_kernel,
        "total",
        [
            ((per_device, width), f32),
            ((per_device, width), f32),
            ((shared, per_device, z_size * lane), f32),
        ],
        [],
        4,
        all_parts,
    )
    totals = send_to_all(own_total, "dp", along_xc)
    order = tuple(
        (x * cores + c, z) for x in range(x_size) for z in range(z_size) for c in range(cores)
    )
    grad_w_xbc, grad_a_log, bias_total, skip_total, dt_gain_total, bc_gain_total = call(
        functools.partial(spread_kernel, order=order),
        "spread",
        [
            ((bc_width, width), f32),
            ((state, width), f32),
            ((1, width), f32),
            ((1, width), f32),
            ((1, rank), f32),
            ((1, bc_width), f32),
        ],
        [((64, width), f32)],
        4,
        totals,
    )
    return (
        grad_x[None],
        grad_w_xdt,
        grad_w_dt,
        grad_w_xbc,
        grad_a_log,
        bias_total.reshape(width),
        skip_total.reshape(width),
        dt_gain_total.reshape(rank),
        bc_gain_total.reshape(bc_width),
    )


def solution(mesh):
    return jax.shard_map(
        body,
        mesh=mesh,
        in_specs=(
            P("dp", None, "tensor"),
            P("dp", "tensor", None),
            P("dp", "tensor", None),
            P("dp", None, "tensor"),
            P(None, "tensor"),
            P(None, "tensor"),
            P(None, "tensor"),
            P("tensor"),
            P(None, "tensor"),
            P("tensor"),
            P(),
            P(),
        ),
        out_specs=(
            P("dp", None, "tensor"),
            P("dp", "tensor"),
            P("dp", "tensor"),
            P(None, "tensor"),
            P(None, "tensor"),
            P("tensor"),
            P("tensor"),
            P(),
            P(),
        ),
        check_vma=False,
    )
```

```python
import functools
import math

import jax
import jax.numpy as jnp
from jax import lax
from jax.experimental import pallas as pl
from jax.experimental.pallas import tpu as pltpu
from jax.sharding import PartitionSpec as P

norm_eps = 1e-06
state_floor = 0.25
log2_e = 1.4426950408889634
lane = 128
f32 = jnp.float32
bf16 = jnp.bfloat16
contract_rows = (((0,), (0,)), ((), ()))
contract_cols = (((1,), (1,)), ((), ()))
in_vmem = pl.BlockSpec(memory_space=pltpu.VMEM)


def inverse_norms(proj, rank, state):
    dt_part = proj[:, :rank]
    b_part = proj[:, rank : rank + state]
    c_part = proj[:, rank + state : rank + 2 * state]
    dt_square = jnp.mean(dt_part * dt_part, axis=1, keepdims=True)
    b_square = jnp.mean(b_part * b_part, axis=1, keepdims=True)
    c_square = jnp.mean(c_part * c_part, axis=1, keepdims=True)
    return (
        (dt_part, lax.rsqrt(dt_square + norm_eps)),
        (b_part, lax.rsqrt(jnp.maximum(b_square, state_floor)), b_square),
        (c_part, lax.rsqrt(jnp.maximum(c_square, state_floor)), c_square),
    )


def pack_kernel(dt_ref, bc_ref, out_ref):
    rank, bc_width = dt_ref.shape[1], bc_ref.shape[1]
    spare = out_ref.shape[2] - rank - bc_width
    for peer in range(out_ref.shape[0]):
        out_ref[peer, :, :rank] = dt_ref[...]
        out_ref[peer, :, rank : rank + bc_width] = bc_ref[...]
        out_ref[peer, :, rank + bc_width :] = jnp.zeros((dt_ref.shape[0], spare), bf16)


def split_cores(core_ref, whole, keep_ref, send_ref):
    first_core = core_ref[0] == 0
    for pair in range(keep_ref.shape[0]):
        even = whole[32 * pair : 32 * pair + 16]
        odd = whole[32 * pair + 16 : 32 * pair + 32]
        keep_ref[pair] = jnp.where(first_core, even, odd)
        send_ref[pair] = jnp.where(first_core, odd, even)


def scan_kernel(
    core_ref,
    proj_ref,
    x_ref,
    gy_ref,
    w_ref,
    bias_ref,
    alog_ref,
    skip_ref,
    dt_gain_ref,
    bc_gain_ref,
    normed_ref,
    w_keep_ref,
    w_send_ref,
    xg_ref,
    misc_ref,
    dt_s,
    gy_s,
    src_s,
    sig_s,
    a2_s,
    low_s,
    bcb_s,
    u_s,
    b_acc,
    c_acc,
    s1_s,
    s2_s,
    *,
    wide_lanes,
    scale,
):
    tokens, width = x_ref.shape
    state = alog_ref.shape[0]
    rank = w_ref.shape[0]
    dt_norm, b_norm, c_norm = inverse_norms(proj_ref[...].astype(f32), rank, state)
    low_s[...] = (dt_norm[0] * dt_norm[1] * dt_gain_ref[...]).astype(bf16)
    b_rows = b_norm[0] * b_norm[1] * bc_gain_ref[:, :state]
    c_rows = c_norm[0] * c_norm[1] * bc_gain_ref[:, state:]
    bcb_s[:, :state] = jnp.broadcast_to(b_rows[:, :, None], (tokens, state, lane))
    bcb_s[:, state:] = jnp.broadcast_to(c_rows[:, :, None], (tokens, state, lane))
    pre = jnp.dot(low_s[...], w_ref[...], preferred_element_type=f32) + bias_ref[...]
    small = jnp.exp(-jnp.abs(pre))
    dt_rows = jnp.maximum(pre, 0.0) + jnp.log1p(small)
    sig_s[...] = jnp.where(pre >= 0, 1.0, small) / (1.0 + small)
    x_float = x_ref[...].astype(f32)
    gy_float = gy_ref[...].astype(f32)
    dt_s[...] = dt_rows
    gy_s[...] = gy_float
    src_s[...] = dt_rows * x_float
    a_mat = -jnp.exp(alog_ref[...])
    a2_s[...] = a_mat * log2_e
    b_acc[...] = jnp.zeros_like(b_acc)
    c_acc[...] = jnp.zeros_like(c_acc)
    reps = wide_lanes // lane

    def widen(part):
        return jnp.concatenate([part] * reps, axis=1)

    def fold(part):
        total = part[:, :lane]
        for rep in range(1, reps):
            total = total + part[:, rep * lane : (rep + 1) * lane]
        return total

    def fold_states(part):
        total = part[:8]
        for rep in range(1, state // 8):
            total = total + part[rep * 8 : (rep + 1) * 8]
        return total

    row_ids = lax.broadcasted_iota(jnp.int32, (8, wide_lanes), 0)

    def join_rows(early, late, level):
        mine = (row_ids & level) == 0
        kept = jnp.where(mine, early, late)
        moved = jnp.where(mine, late, early)
        return kept + pltpu.roll(moved, 8 - level, 0)

    for group in range(width // wide_lanes):
        cols = slice(group * wide_lanes, (group + 1) * wide_lanes)

        def forward(block, held):
            a2 = a2_s[:, cols]
            for offset in range(8):
                t = block * 8 + offset
                decayed = jnp.exp2(dt_s[pl.ds(t, 1), cols] * a2) * held
                u_s[pl.ds(t, 1), :, cols] = decayed[None]
                c_acc[pl.ds(t, 1)] += fold(decayed * gy_s[pl.ds(t, 1), cols])[None]
                held = decayed + src_s[pl.ds(t, 1), cols] * widen(bcb_s[t, :state])
            return held

        zeros = jnp.zeros((state, wide_lanes), f32)
        lax.fori_loop(0, tokens // 8, forward, zeros)

        def backward(step, carry):
            later, a_total = carry
            block = tokens // 8 - 1 - step
            a2 = a2_s[:, cols]
            waiting = {}
            for offset in range(7, -1, -1):
                t = block * 8 + offset
                dt_now = dt_s[pl.ds(t, 1), cols]
                adjoint = widen(bcb_s[t, state:]) * gy_s[pl.ds(t, 1), cols] + later
                through = adjoint * u_s[t, :, cols]
                first = fold_states(adjoint * widen(bcb_s[t, :state]))
                second = fold_states(through * a2)
                level = 1
                while level in waiting:
                    later_first, later_second = waiting.pop(level)
                    first = join_rows(first, later_first, level)
                    second = join_rows(second, later_second, level)
                    level *= 2
                waiting[level] = (first, second)
                b_acc[pl.ds(t, 1)] += fold(adjoint * src_s[pl.ds(t, 1), cols])[None]
                a_total = a_total + dt_now * through
                later = jnp.exp2(dt_now * a2) * adjoint
            s1_s[pl.ds(block * 8, 8), cols], s2_s[pl.ds(block * 8, 8), cols] = waiting[8]
            return later, a_total

        _, a_total = lax.fori_loop(0, tokens // 8, backward, (zeros, zeros))
        misc_ref[:state, cols] = (scale / log2_e) * (a_total * a2_s[:, cols])

    s1 = s1_s[...]
    xg_ref[...] = dt_s[...] * s1 + skip_ref[...] * gy_s[...]
    dt_grad = x_ref[...].astype(f32) * s1 + s2_s[...] * (1.0 / log2_e)
    pre_float = dt_grad * sig_s[...]
    pre_grad = pre_float.astype(bf16)
    misc_ref[state : state + 1, :] = scale * jnp.sum(pre_float, axis=0, keepdims=True)
    misc_ref[state + 1 : state + 2, :] = scale * jnp.sum(
        gy_s[...] * x_ref[...].astype(f32), axis=0, keepdims=True
    )
    dt_normed = lax.dot_general(
        pre_grad, w_ref[...], contract_cols, preferred_element_type=f32
    ).astype(bf16)
    w_part = scale * lax.dot_general(
        low_s[...], pre_grad, contract_rows, preferred_element_type=f32
    )
    split_cores(core_ref, w_part.astype(bf16), w_keep_ref, w_send_ref)
    source_sum = jnp.sum(src_s[...] * gy_s[...], axis=1, keepdims=True)
    b_grad = jnp.sum(b_acc[...], axis=2)
    c_grad = jnp.sum(c_acc[...], axis=2) + b_rows * source_sum
    b_grad = b_grad.astype(bf16)
    c_grad = c_grad.astype(bf16)
    z_size, y_size, own = normed_ref.shape[1], normed_ref.shape[0], normed_ref.shape[2]
    for y in range(y_size):
        for z in range(z_size):
            rows = slice((z * y_size + y) * own, (z * y_size + y + 1) * own)
            normed_ref[y, z, :, :rank] = dt_normed[rows]
            normed_ref[y, z, :, rank : rank + state] = b_grad[rows]
            normed_ref[y, z, :, rank + state : rank + 2 * state] = c_grad[rows]
            normed_ref[y, z, :, rank + 2 * state :] = jnp.zeros(
                (own, lane - 2 * state), bf16
            )


def sum_kernel(parts_ref, out_ref):
    total = parts_ref[0].astype(f32)
    for peer in range(1, parts_ref.shape[0]):
        total = total + parts_ref[peer].astype(f32)
    out_ref[...] = total


def norm_kernel(
    y_ref, mine_ref, other_ref, proj_ref, dt_gain_ref, bc_gain_ref, out_ref, pack_s, *, state
):
    rank = dt_gain_ref.shape[1]
    rows = mine_ref.shape[0]
    grads = mine_ref[...] + other_ref[...]
    proj = jnp.concatenate([proj_ref[z, y_ref[0]] for z in range(proj_ref.shape[0])], axis=0)
    dt_norm, b_norm, c_norm = inverse_norms(proj.astype(f32), rank, state)
    dt_grad = grads[:, :rank]
    dt_unit = dt_norm[0] * dt_norm[1]
    dt_cot = dt_grad * dt_gain_ref[...]
    dt_mean = jnp.mean(dt_cot * dt_unit, axis=1, keepdims=True)
    pack_s[:, rank:] = jnp.zeros((rows, lane), f32)
    pack_s[:, :rank] = dt_norm[1] * (dt_cot - dt_unit * dt_mean)
    dt_gain_part = jnp.sum(dt_grad * dt_unit, axis=0, keepdims=True)
    last = rank + lane // 2
    for piece in range(rank // (lane // 2)):
        pack_s[piece : piece + 1, last:] = dt_gain_part[
            :, piece * (lane // 2) : (piece + 1) * (lane // 2)
        ]
    gain_row = rank // (lane // 2)
    for index, part in enumerate((b_norm, c_norm)):
        start = rank + index * state
        grad = grads[:, start : start + state]
        unit = part[0] * part[1]
        cot = grad * bc_gain_ref[:, index * state : (index + 1) * state]
        mean = jnp.mean(cot * unit, axis=1, keepdims=True)
        inner = jnp.where(part[2] > state_floor, mean, 0.0)
        inner = jnp.where(part[2] == state_floor, 0.5 * mean, inner)
        pack_s[:, start : start + state] = part[1] * (cot - unit * inner)
        pack_s[gain_row : gain_row + 1, last + index * state : last + (index + 1) * state] = (
            jnp.sum(grad * unit, axis=0, keepdims=True)
        )
    gains = pack_s[: rows // 2, last:]
    pack_s[rows // 2 :, last:] = gains - gains.astype(bf16).astype(f32)
    packed = pack_s[...].astype(bf16)
    for peer in range(out_ref.shape[0]):
        out_ref[peer] = packed


def project_kernel(
    core_ref,
    low_ref,
    xg_ref,
    x_ref,
    w_xdt_ref,
    w_xbc_ref,
    misc_ref,
    grad_x_ref,
    keep_ref,
    send_ref,
    out_s,
    all_s,
    low_s,
    *,
    scale,
):
    rank, width = w_xdt_ref.shape
    bc_width = w_xbc_ref.shape[0]
    y_size, z_size, own, _ = low_ref.shape
    for y in range(y_size):
        for z in range(z_size):
            start = (z * y_size + y) * own
            low_s[start : start + own, :] = low_ref[y, z]
    dt_low = low_s[:, :rank]
    bc_low = low_s[:, rank : rank + bc_width]
    summed = xg_ref[...] + jnp.dot(dt_low, w_xdt_ref[...], preferred_element_type=f32)
    summed = summed + jnp.dot(bc_low, w_xbc_ref[...], preferred_element_type=f32)
    grad_x_ref[...] = summed.astype(bf16)
    out_s[:, :width] = (
        scale
        * lax.dot_general(dt_low, x_ref[...], contract_rows, preferred_element_type=f32)
    ).astype(bf16)
    state = bc_width // 2
    all_s[...] = jnp.zeros_like(all_s)
    all_s[: state + 2, :] = misc_ref[: state + 2, :]
    all_s[state + 8 : state + 8 + bc_width, :] = scale * lax.dot_general(
        bc_low, x_ref[...], contract_rows, preferred_element_type=f32
    )
    gains = jnp.zeros((own, lane), f32)
    for y in range(y_size):
        for z in range(z_size):
            gains = gains + low_ref[y, z, :, rank:].astype(f32)
    gains = scale * gains[:, lane // 2 :]
    gain_row = state + 8 + bc_width
    for piece in range(rank // (lane // 2)):
        all_s[gain_row : gain_row + 1, piece * (lane // 2) : (piece + 1) * (lane // 2)] = gains[
            piece : piece + 1
        ]
    piece = rank // (lane // 2)
    all_s[gain_row : gain_row + 1, rank : rank + bc_width] = gains[piece : piece + 1, :bc_width]
    for piece in range(width // lane):
        out_s[piece * 64 : (piece + 1) * 64, width:] = all_s[
            :, piece * lane : (piece + 1) * lane
        ].astype(bf16)
    split_cores(core_ref, out_s, keep_ref, send_ref)


def total_kernel(parts_ref, xdt_ref, dt_ref, own_ref):
    width = xdt_ref.shape[1]
    total = parts_ref[0].astype(f32)
    for peer in range(1, parts_ref.shape[0]):
        total = total + parts_ref[peer].astype(f32)
    xdt_ref[...] = total[:, :width]
    dt_ref[...] = total[:, width : 2 * width]
    for peer in range(own_ref.shape[0]):
        own_ref[peer] = total[:, 2 * width :]


def spread_kernel(
    parts_ref, xbc_ref, alog_ref, bias_ref, skip_ref, dt_gain_ref, bc_gain_ref, all_s, *, order
):
    state = alog_ref.shape[0]
    bc_width = xbc_ref.shape[0]
    rank = dt_gain_ref.shape[1]
    for block, (peer, place) in enumerate(order):
        row, piece = 16 * (block % 4), lane * (block // 4)
        all_s[row : row + 16, piece : piece + lane] = parts_ref[
            peer, :, place * lane : (place + 1) * lane
        ]
    alog_ref[...] = all_s[:state, :]
    bias_ref[...] = all_s[state : state + 1, :]
    skip_ref[...] = all_s[state + 1 : state + 2, :]
    xbc_ref[...] = all_s[state + 8 : state + 8 + bc_width, :]
    gain_row = state + 8 + bc_width
    dt_gain_ref[...] = all_s[gain_row : gain_row + 1, :rank]
    bc_gain_ref[...] = all_s[gain_row : gain_row + 1, rank : rank + bc_width]


def call(kernel, name, outs, scratch, limit_mib, *args):
    in_smem = pl.BlockSpec(memory_space=pltpu.SMEM)
    return pl.pallas_call(
        kernel,
        out_shape=tuple(
            pltpu.VMEM(out[0], out[1]) if len(out) > 2 else jax.ShapeDtypeStruct(*out)
            for out in outs
        ),
        in_specs=[in_smem if arg.dtype == jnp.int32 else in_vmem for arg in args],
        out_specs=tuple([in_vmem] * len(outs)),
        scratch_shapes=[pltpu.VMEM(shape, dtype) for shape, dtype in scratch],
        compiler_params=pltpu.CompilerParams(vmem_limit_bytes=limit_mib * 2**20),
        name=name,
    )(*args)


def send_to_all(block, axis, groups=None):
    return lax.all_to_all(block, axis, 0, 0, axis_index_groups=groups)


def sum_low(parts):
    return jnp.sum(parts.astype(f32), axis=0).astype(bf16)


def body(
    x_inner, proj_dt, proj_bc, grad_y, w_xdt, w_xbc, w_dt, dt_bias, a_log, d_skip, dt_gain, bc_gain
):
    x_rows = x_inner[0]
    gy_rows = grad_y[0]
    tokens, width = x_rows.shape
    rank = proj_dt.shape[2]
    bc_width = proj_bc.shape[2]
    state = bc_width // 2
    own = proj_dt.shape[1]
    dp = lax.axis_size("dp")
    tensor = lax.axis_size("tensor")
    scale = 1.0 / math.sqrt(dp * tokens)
    bias_row = dt_bias.reshape(1, width)
    skip_row = d_skip.reshape(1, width)
    dt_gain_row = dt_gain.reshape(1, rank)
    bc_gain_row = bc_gain.reshape(1, bc_width)

    columns = rank + lane
    local = True
    (own_proj,) = call(
        pack_kernel,
        "pack",
        [((tensor, own, columns), bf16, local)],
        [],
        4,
        proj_dt[0],
        proj_bc[0],
    )
    full_proj = send_to_all(own_proj, "tensor").reshape(tokens, columns)

    cores, z_size, z_pair = 2, 4, 2
    x_size = dp // (cores * z_size)
    y_size = tensor // z_pair
    per_device = rank // dp
    core = (lax.axis_index("dp") % cores).astype(jnp.int32).reshape(1)
    other_core = [(index, index ^ 1) for index in range(dp)]
    z_stride, x_stride = cores, cores * z_size
    along_x = [[x * x_stride + rest for x in range(x_size)] for rest in range(x_stride)]
    along_z = [
        [x * x_stride + z * z_stride + c for z in range(z_size)]
        for x in range(x_size)
        for c in range(cores)
    ]
    along_xc = [
        [x * x_stride + z * z_stride + c for x in range(x_size) for c in range(cores)]
        for z in range(z_size)
    ]
    along_y = [[z * y_size + y for y in range(y_size)] for z in range(z_pair)]

    def swap_cores(sent):
        return lax.ppermute(sent, "dp", other_core)

    def sum_over_x(kept, other):
        both = (kept.astype(f32) + other.astype(f32)).astype(bf16)
        blocks = both.reshape((x_size, z_size) + both.shape[1:])
        return sum_low(send_to_all(blocks, "dp", along_x))

    rows = ((tokens, width), f32)
    by_token = (y_size, z_pair, own, columns)
    half = (x_size * z_size, per_device)
    normed_part, w_kept, w_sent, xg, misc = call(
        functools.partial(scan_kernel, wide_lanes=min(512, width), scale=scale),
        "scan",
        [
            (by_token, bf16, local),
            (half + (width,), bf16, local),
            (half + (width,), bf16, local),
            ((tokens, width), f32, local),
            ((state + 8, width), f32, local),
        ],
        [
            rows,
            rows,
            rows,
            rows,
            ((state, width), f32),
            ((tokens, rank), bf16),
            ((tokens, 2 * state, lane), f32),
            ((tokens, state, width), f32),
            ((tokens, state, lane), f32),
            ((tokens, state, lane), f32),
            rows,
            rows,
        ],
        56,
        core,
        full_proj,
        x_rows,
        gy_rows,
        w_dt,
        bias_row,
        a_log,
        skip_row,
        dt_gain_row,
        bc_gain_row,
    )
    shared_rows = z_pair * own
    normed_parts = send_to_all(
        normed_part.reshape(y_size, shared_rows, columns), "tensor", along_y
    )
    (mine,) = call(
        sum_kernel, "join", [((shared_rows, columns), f32, local)], [], 4, normed_parts
    )
    mine, w_other = lax.optimization_barrier((mine, swap_cores(w_sent)))
    w_by_x = sum_over_x(w_kept, w_other)
    other = lax.ppermute(
        mine, "tensor", [(index, (index + y_size) % tensor) for index in range(tensor)]
    )
    other, w_by_x = lax.optimization_barrier((other, w_by_x))
    y_index = (lax.axis_index("tensor") % y_size).astype(jnp.int32).reshape(1)
    (own_low,) = call(
        functools.partial(norm_kernel, state=state),
        "norm",
        [((y_size, shared_rows, columns), bf16, local)],
        [((shared_rows, columns), f32)],
        4,
        y_index,
        mine,
        other,
        full_proj.reshape(z_pair, y_size, own, columns),
        dt_gain_row,
        bc_gain_row,
    )
    low = send_to_all(own_low, "tensor", along_y).reshape(by_token)
    half_row = (half + (width + lane,), bf16)
    grad_x, kept, sent = call(
        functools.partial(project_kernel, scale=scale),
        "project",
        [((tokens, width), bf16), half_row + (local,), half_row + (local,)],
        [
            ((rank, width + lane), bf16),
            ((64, width), f32),
            ((tokens, columns), bf16),
        ],
        16,
        core,
        low,
        xg,
        x_rows,
        w_xdt,
        w_xbc,
        misc,
    )
    by_x = sum_over_x(kept, swap_cores(sent))
    by_z = by_x[:, :, width:].transpose(1, 0, 2).reshape(1, per_device, z_size * lane)
    by_z = jnp.broadcast_to(by_z, (z_size, per_device, z_size * lane))
    by_z = jnp.concatenate([by_x[:, :, :width], w_by_x, by_z], axis=2)
    all_parts = send_to_all(by_z, "dp", along_z)
    shared = x_size * cores
    grad_w_xdt, grad_w_dt, own_total = call(
        total_kernel,
        "total",
        [
            ((per_device, width), f32),
            ((per_device, width), f32),
            ((shared, per_device, z_size * lane), f32, local),
        ],
        [],
        4,
        all_parts,
    )
    totals = send_to_all(own_total, "dp", along_xc)
    order = tuple(
        (x * cores + c, z) for x in range(x_size) for z in range(z_size) for c in range(cores)
    )
    grad_w_xbc, grad_a_log, bias_total, skip_total, dt_gain_total, bc_gain_total = call(
        functools.partial(spread_kernel, order=order),
        "spread",
        [
            ((bc_width, width), f32),
            ((state, width), f32),
            ((1, width), f32),
            ((1, width), f32),
            ((1, rank), f32),
            ((1, bc_width), f32),
        ],
        [((64, width), f32)],
        4,
        totals,
    )
    return (
        grad_x[None],
        grad_w_xdt,
        grad_w_dt,
        grad_w_xbc,
        grad_a_log,
        bias_total.reshape(width),
        skip_total.reshape(width),
        dt_gain_total.reshape(rank),
        bc_gain_total.reshape(bc_width),
    )


def solution(mesh):
    return jax.shard_map(
        body,
        mesh=mesh,
        in_specs=(
            P("dp", None, "tensor"),
            P("dp", "tensor", None),
            P("dp", "tensor", None),
            P("dp", None, "tensor"),
            P(None, "tensor"),
            P(None, "tensor"),
            P(None, "tensor"),
            P("tensor"),
            P(None, "tensor"),
            P("tensor"),
            P(),
            P(),
        ),
        out_specs=(
            P("dp", None, "tensor"),
            P("dp", "tensor"),
            P("dp", "tensor"),
            P(None, "tensor"),
            P(None, "tensor"),
            P("tensor"),
            P("tensor"),
            P(),
            P(),
        ),
        check_vma=False,
    )
```

```python
import functools
import math

import jax
import jax.numpy as jnp
from jax import lax
from jax.experimental import pallas as pl
from jax.experimental.pallas import tpu as pltpu
from jax.sharding import PartitionSpec as P

norm_eps = 1e-06
state_floor = 0.25
log2_e = 1.4426950408889634
lane = 128
f32 = jnp.float32
bf16 = jnp.bfloat16
contract_rows = (((0,), (0,)), ((), ()))
contract_cols = (((1,), (1,)), ((), ()))
in_vmem = pl.BlockSpec(memory_space=pltpu.VMEM)


def inverse_norms(proj, rank, state):
    dt_part = proj[:, :rank]
    b_part = proj[:, rank : rank + state]
    c_part = proj[:, rank + state : rank + 2 * state]
    dt_square = jnp.mean(dt_part * dt_part, axis=1, keepdims=True)
    b_square = jnp.mean(b_part * b_part, axis=1, keepdims=True)
    c_square = jnp.mean(c_part * c_part, axis=1, keepdims=True)
    return (
        (dt_part, lax.rsqrt(dt_square + norm_eps)),
        (b_part, lax.rsqrt(jnp.maximum(b_square, state_floor)), b_square),
        (c_part, lax.rsqrt(jnp.maximum(c_square, state_floor)), c_square),
    )


def pack_kernel(dt_in, bc_in, out_ref, dt_ref, bc_ref, arrived):
    rank, bc_width = dt_ref.shape[1], bc_ref.shape[1]
    spare = out_ref.shape[2] - rank - bc_width
    arrivals = [
        pltpu.make_async_copy(dt_in, dt_ref, arrived.at[0]),
        pltpu.make_async_copy(bc_in, bc_ref, arrived.at[1]),
    ]
    for copy in arrivals:
        copy.start()
    for copy in arrivals:
        copy.wait()
    for peer in range(out_ref.shape[0]):
        out_ref[peer, :, :rank] = dt_ref[...]
        out_ref[peer, :, rank : rank + bc_width] = bc_ref[...]
        out_ref[peer, :, rank + bc_width :] = jnp.zeros((dt_ref.shape[0], spare), bf16)


def split_cores(core_ref, whole, keep_ref, send_ref):
    first_core = core_ref[0] == 0
    for pair in range(keep_ref.shape[0]):
        even = whole[32 * pair : 32 * pair + 16]
        odd = whole[32 * pair + 16 : 32 * pair + 32]
        keep_ref[pair] = jnp.where(first_core, even, odd)
        send_ref[pair] = jnp.where(first_core, odd, even)


def scan_kernel(
    core_ref,
    proj_ref,
    dt_gain_in,
    bc_gain_in,
    w_in,
    bias_in,
    x_in,
    gy_in,
    alog_in,
    skip_in,
    normed_ref,
    w_keep_ref,
    w_send_ref,
    xg_ref,
    misc_ref,
    dt_s,
    gy_s,
    src_s,
    sig_s,
    a2_s,
    low_s,
    bcb_s,
    u_s,
    b_acc,
    c_acc,
    s1_s,
    s2_s,
    dt_gain_ref,
    bc_gain_ref,
    w_ref,
    bias_ref,
    x_ref,
    gy_ref,
    alog_ref,
    skip_ref,
    arrived,
    *,
    scale,
    forward_lanes=512,
    forward_rows=32,
    backward_lanes=512,
    backward_rows=16,
):
    tokens, width = x_ref.shape
    state = alog_ref.shape[0]
    rank = w_ref.shape[0]
    arrivals = [
        pltpu.make_async_copy(source, held, arrived.at[index])
        for index, (source, held) in enumerate(
            (
                (dt_gain_in, dt_gain_ref),
                (bc_gain_in, bc_gain_ref),
                (w_in, w_ref),
                (bias_in, bias_ref),
                (x_in, x_ref),
                (gy_in, gy_ref),
                (alog_in, alog_ref),
                (skip_in, skip_ref),
            )
        )
    ]
    for copy in arrivals:
        copy.start()
    b_acc[...] = jnp.zeros_like(b_acc)
    c_acc[...] = jnp.zeros_like(c_acc)
    dt_norm, b_norm, c_norm = inverse_norms(proj_ref[...].astype(f32), rank, state)
    arrivals[0].wait()
    arrivals[1].wait()
    low_s[...] = (dt_norm[0] * dt_norm[1] * dt_gain_ref[...]).astype(bf16)
    b_rows = b_norm[0] * b_norm[1] * bc_gain_ref[:, :state]
    c_rows = c_norm[0] * c_norm[1] * bc_gain_ref[:, state:]
    bcb_s[:, :state] = jnp.broadcast_to(b_rows[:, :, None], (tokens, state, lane))
    bcb_s[:, state:] = jnp.broadcast_to(c_rows[:, :, None], (tokens, state, lane))
    arrivals[2].wait()
    arrivals[3].wait()
    pre = jnp.dot(low_s[...], w_ref[...], preferred_element_type=f32) + bias_ref[...]
    small = jnp.exp(-jnp.abs(pre))
    dt_rows = jnp.maximum(pre, 0.0) + jnp.log1p(small)
    sig_s[...] = jnp.where(pre >= 0, 1.0, small) / (1.0 + small)
    for copy in arrivals[4:]:
        copy.wait()
    x_float = x_ref[...].astype(f32)
    gy_float = gy_ref[...].astype(f32)
    dt_s[...] = dt_rows
    gy_s[...] = gy_float
    src_s[...] = dt_rows * x_float
    a_mat = -jnp.exp(alog_ref[...])
    a2_s[...] = a_mat * log2_e
    def widen(part, width):
        return jnp.concatenate([part] * (width // lane), axis=1)

    def fold(part):
        total = part[:, :lane]
        for start in range(lane, part.shape[1], lane):
            total = total + part[:, start : start + lane]
        return total

    def fold_states(part):
        total = part[:8]
        for rep in range(1, state // 8):
            total = total + part[rep * 8 : (rep + 1) * 8]
        return total

    def join_rows(early, late, level):
        mine = (lax.broadcasted_iota(jnp.int32, early.shape, 0) & level) == 0
        kept = jnp.where(mine, early, late)
        moved = jnp.where(mine, late, early)
        return kept + pltpu.roll(moved, 8 - level, 0)

    wide = min(forward_lanes, width)
    for group in range(width // wide):
        cols = slice(group * wide, (group + 1) * wide)

        def forward(block, held):
            a2 = a2_s[:, cols]
            for offset in range(forward_rows):
                t = block * forward_rows + offset
                decayed = jnp.exp2(dt_s[pl.ds(t, 1), cols] * a2) * held
                u_s[pl.ds(t, 1), :, cols] = decayed[None]
                c_acc[pl.ds(t, 1)] += fold(decayed * gy_s[pl.ds(t, 1), cols])[None]
                held = decayed + src_s[pl.ds(t, 1), cols] * widen(bcb_s[t, :state], wide)
            return held

        lax.fori_loop(0, tokens // forward_rows, forward, jnp.zeros((state, wide), f32))

    wide = min(backward_lanes, width)
    for group in range(width // wide):
        cols = slice(group * wide, (group + 1) * wide)

        def backward(step, carry):
            later, a_total = carry
            a2 = a2_s[:, cols]
            for part in range(backward_rows // 8 - 1, -1, -1):
                first_row = tokens - (step + 1) * backward_rows + part * 8
                waiting = {}
                for offset in range(7, -1, -1):
                    t = first_row + offset
                    dt_now = dt_s[pl.ds(t, 1), cols]
                    adjoint = (
                        widen(bcb_s[t, state:], wide) * gy_s[pl.ds(t, 1), cols] + later
                    )
                    through = adjoint * u_s[t, :, cols]
                    first = fold_states(adjoint * widen(bcb_s[t, :state], wide))
                    second = fold_states(through * a2)
                    level = 1
                    while level in waiting:
                        later_first, later_second = waiting.pop(level)
                        first = join_rows(first, later_first, level)
                        second = join_rows(second, later_second, level)
                        level *= 2
                    waiting[level] = (first, second)
                    b_acc[pl.ds(t, 1)] += fold(adjoint * src_s[pl.ds(t, 1), cols])[None]
                    a_total = a_total + dt_now * through
                    later = jnp.exp2(dt_now * a2) * adjoint
                rows = pl.ds(pl.multiple_of(first_row, 8), 8)
                s1_s[rows, cols], s2_s[rows, cols] = waiting[8]
            return later, a_total

        zeros = jnp.zeros((state, wide), f32)
        _, a_total = lax.fori_loop(0, tokens // backward_rows, backward, (zeros, zeros))
        misc_ref[:state, cols] = (scale / log2_e) * (a_total * a2_s[:, cols])

    s1 = s1_s[...]
    xg_ref[...] = dt_s[...] * s1 + skip_ref[...] * gy_s[...]
    dt_grad = x_ref[...].astype(f32) * s1 + s2_s[...] * (1.0 / log2_e)
    pre_float = dt_grad * sig_s[...]
    pre_grad = pre_float.astype(bf16)
    misc_ref[state : state + 1, :] = scale * jnp.sum(pre_float, axis=0, keepdims=True)
    misc_ref[state + 1 : state + 2, :] = scale * jnp.sum(
        gy_s[...] * x_ref[...].astype(f32), axis=0, keepdims=True
    )
    dt_normed = lax.dot_general(
        pre_grad, w_ref[...], contract_cols, preferred_element_type=f32
    ).astype(bf16)
    w_part = scale * lax.dot_general(
        low_s[...], pre_grad, contract_rows, preferred_element_type=f32
    )
    split_cores(core_ref, w_part.astype(bf16), w_keep_ref, w_send_ref)
    source_sum = jnp.sum(src_s[...] * gy_s[...], axis=1, keepdims=True)
    b_grad = jnp.sum(b_acc[...], axis=2)
    c_grad = jnp.sum(c_acc[...], axis=2) + b_rows * source_sum
    b_grad = b_grad.astype(bf16)
    c_grad = c_grad.astype(bf16)
    z_size, y_size, own = normed_ref.shape[1], normed_ref.shape[0], normed_ref.shape[2]
    for y in range(y_size):
        for z in range(z_size):
            rows = slice((z * y_size + y) * own, (z * y_size + y + 1) * own)
            normed_ref[y, z, :, :rank] = dt_normed[rows]
            normed_ref[y, z, :, rank : rank + state] = b_grad[rows]
            normed_ref[y, z, :, rank + state : rank + 2 * state] = c_grad[rows]
            normed_ref[y, z, :, rank + 2 * state :] = jnp.zeros(
                (own, lane - 2 * state), bf16
            )


def sum_kernel(parts_ref, out_ref):
    total = parts_ref[0].astype(f32)
    for peer in range(1, parts_ref.shape[0]):
        total = total + parts_ref[peer].astype(f32)
    out_ref[...] = total


def norm_kernel(
    y_ref, mine_ref, other_ref, proj_ref, dt_gain_ref, bc_gain_ref, out_ref, pack_s, *, state
):
    rank = dt_gain_ref.shape[1]
    rows = mine_ref.shape[0]
    grads = mine_ref[...] + other_ref[...]
    proj = jnp.concatenate([proj_ref[z, y_ref[0]] for z in range(proj_ref.shape[0])], axis=0)
    dt_norm, b_norm, c_norm = inverse_norms(proj.astype(f32), rank, state)
    dt_grad = grads[:, :rank]
    dt_unit = dt_norm[0] * dt_norm[1]
    dt_cot = dt_grad * dt_gain_ref[...]
    dt_mean = jnp.mean(dt_cot * dt_unit, axis=1, keepdims=True)
    pack_s[:, rank:] = jnp.zeros((rows, lane), f32)
    pack_s[:, :rank] = dt_norm[1] * (dt_cot - dt_unit * dt_mean)
    dt_gain_part = jnp.sum(dt_grad * dt_unit, axis=0, keepdims=True)
    last = rank + lane // 2
    for piece in range(rank // (lane // 2)):
        pack_s[piece : piece + 1, last:] = dt_gain_part[
            :, piece * (lane // 2) : (piece + 1) * (lane // 2)
        ]
    gain_row = rank // (lane // 2)
    for index, part in enumerate((b_norm, c_norm)):
        start = rank + index * state
        grad = grads[:, start : start + state]
        unit = part[0] * part[1]
        cot = grad * bc_gain_ref[:, index * state : (index + 1) * state]
        mean = jnp.mean(cot * unit, axis=1, keepdims=True)
        inner = jnp.where(part[2] > state_floor, mean, 0.0)
        inner = jnp.where(part[2] == state_floor, 0.5 * mean, inner)
        pack_s[:, start : start + state] = part[1] * (cot - unit * inner)
        pack_s[gain_row : gain_row + 1, last + index * state : last + (index + 1) * state] = (
            jnp.sum(grad * unit, axis=0, keepdims=True)
        )
    gains = pack_s[: rows // 2, last:]
    pack_s[rows // 2 :, last:] = gains - gains.astype(bf16).astype(f32)
    packed = pack_s[...].astype(bf16)
    for peer in range(out_ref.shape[0]):
        out_ref[peer] = packed


def to_tokens(low_ref, low_s):
    y_size, z_size, own, _ = low_ref.shape
    for y in range(y_size):
        for z in range(z_size):
            start = (z * y_size + y) * own
            low_s[start : start + own, :] = low_ref[y, z]


def grad_x_kernel(low_ref, xg_ref, w_xdt_ref, w_xbc_ref, grad_x_ref, low_s):
    rank = w_xdt_ref.shape[0]
    bc_width = w_xbc_ref.shape[0]
    to_tokens(low_ref, low_s)
    summed = xg_ref[...] + jnp.dot(
        low_s[:, :rank], w_xdt_ref[...], preferred_element_type=f32
    )
    summed = summed + jnp.dot(
        low_s[:, rank : rank + bc_width], w_xbc_ref[...], preferred_element_type=f32
    )
    grad_x_ref[...] = summed.astype(bf16)


def project_kernel(
    core_ref,
    low_ref,
    x_ref,
    misc_ref,
    keep_ref,
    send_ref,
    out_s,
    all_s,
    low_s,
    *,
    rank,
    bc_width,
    scale,
):
    width = x_ref.shape[1]
    y_size, z_size, own, _ = low_ref.shape
    to_tokens(low_ref, low_s)
    dt_low = low_s[:, :rank]
    bc_low = low_s[:, rank : rank + bc_width]
    out_s[:, :width] = (
        scale
        * lax.dot_general(dt_low, x_ref[...], contract_rows, preferred_element_type=f32)
    ).astype(bf16)
    state = bc_width // 2
    all_s[...] = jnp.zeros_like(all_s)
    all_s[: state + 2, :] = misc_ref[: state + 2, :]
    all_s[state + 8 : state + 8 + bc_width, :] = scale * lax.dot_general(
        bc_low, x_ref[...], contract_rows, preferred_element_type=f32
    )
    gains = jnp.zeros((own, lane), f32)
    for y in range(y_size):
        for z in range(z_size):
            gains = gains + low_ref[y, z, :, rank:].astype(f32)
    gains = scale * gains[:, lane // 2 :]
    gain_row = state + 8 + bc_width
    for piece in range(rank // (lane // 2)):
        all_s[gain_row : gain_row + 1, piece * (lane // 2) : (piece + 1) * (lane // 2)] = gains[
            piece : piece + 1
        ]
    piece = rank // (lane // 2)
    all_s[gain_row : gain_row + 1, rank : rank + bc_width] = gains[piece : piece + 1, :bc_width]
    for piece in range(width // lane):
        out_s[piece * 64 : (piece + 1) * 64, width:] = all_s[
            :, piece * lane : (piece + 1) * lane
        ].astype(bf16)
    split_cores(core_ref, out_s, keep_ref, send_ref)


def total_kernel(parts_ref, xdt_ref, dt_ref, own_ref):
    width = xdt_ref.shape[1]
    total = parts_ref[0].astype(f32)
    for peer in range(1, parts_ref.shape[0]):
        total = total + parts_ref[peer].astype(f32)
    xdt_ref[...] = total[:, :width]
    dt_ref[...] = total[:, width : 2 * width]
    for peer in range(own_ref.shape[0]):
        own_ref[peer] = total[:, 2 * width :]


def spread_kernel(
    parts_ref, xbc_ref, alog_ref, bias_ref, skip_ref, dt_gain_ref, bc_gain_ref, all_s, *, order
):
    state = alog_ref.shape[0]
    bc_width = xbc_ref.shape[0]
    rank = dt_gain_ref.shape[1]
    for block, (peer, place) in enumerate(order):
        row, piece = 16 * (block % 4), lane * (block // 4)
        all_s[row : row + 16, piece : piece + lane] = parts_ref[
            peer, :, place * lane : (place + 1) * lane
        ]
    alog_ref[...] = all_s[:state, :]
    bias_ref[...] = all_s[state : state + 1, :]
    skip_ref[...] = all_s[state + 1 : state + 2, :]
    xbc_ref[...] = all_s[state + 8 : state + 8 + bc_width, :]
    gain_row = state + 8 + bc_width
    dt_gain_ref[...] = all_s[gain_row : gain_row + 1, :rank]
    bc_gain_ref[...] = all_s[gain_row : gain_row + 1, rank : rank + bc_width]


def call(kernel, name, outs, scratch, limit_mib, *args, far=()):
    in_smem = pl.BlockSpec(memory_space=pltpu.SMEM)
    in_hbm = pl.BlockSpec(memory_space=pltpu.HBM)
    return pl.pallas_call(
        kernel,
        out_shape=tuple(
            pltpu.VMEM(out[0], out[1]) if len(out) > 2 else jax.ShapeDtypeStruct(*out)
            for out in outs
        ),
        in_specs=[in_smem if arg.dtype == jnp.int32 else in_vmem for arg in args]
        + [in_hbm] * len(far),
        out_specs=tuple([in_vmem] * len(outs)),
        scratch_shapes=[pltpu.VMEM(shape, dtype) for shape, dtype in scratch]
        + [pltpu.VMEM(arg.shape, arg.dtype) for arg in far]
        + ([pltpu.SemaphoreType.DMA((len(far),))] if far else []),
        compiler_params=pltpu.CompilerParams(vmem_limit_bytes=limit_mib * 2**20),
        name=name,
    )(*args, *[pltpu.with_memory_space_constraint(arg, pltpu.HBM) for arg in far])


def send_to_all(block, axis, groups=None):
    return lax.all_to_all(block, axis, 0, 0, axis_index_groups=groups)


def sum_low(parts):
    return jnp.sum(parts.astype(f32), axis=0).astype(bf16)


def body(
    x_inner, proj_dt, proj_bc, grad_y, w_xdt, w_xbc, w_dt, dt_bias, a_log, d_skip, dt_gain, bc_gain
):
    x_rows = x_inner[0]
    gy_rows = grad_y[0]
    tokens, width = x_rows.shape
    rank = proj_dt.shape[2]
    bc_width = proj_bc.shape[2]
    state = bc_width // 2
    own = proj_dt.shape[1]
    dp = lax.axis_size("dp")
    tensor = lax.axis_size("tensor")
    scale = 1.0 / math.sqrt(dp * tokens)
    bias_row = dt_bias.reshape(1, width)
    skip_row = d_skip.reshape(1, width)
    dt_gain_row = dt_gain.reshape(1, rank)
    bc_gain_row = bc_gain.reshape(1, bc_width)

    columns = rank + lane
    local = True
    (own_proj,) = call(
        pack_kernel,
        "pack",
        [((tensor, own, columns), bf16, local)],
        [],
        4,
        far=(proj_dt[0], proj_bc[0]),
    )
    full_proj = send_to_all(own_proj, "tensor").reshape(tokens, columns)

    cores, z_size, z_pair = 2, 4, 2
    x_size = dp // (cores * z_size)
    y_size = tensor // z_pair
    per_device = rank // dp
    core = (lax.axis_index("dp") % cores).astype(jnp.int32).reshape(1)
    other_core = [(index, index ^ 1) for index in range(dp)]
    z_stride, x_stride = cores, cores * z_size
    along_x = [[x * x_stride + rest for x in range(x_size)] for rest in range(x_stride)]
    along_z = [
        [x * x_stride + z * z_stride + c for z in range(z_size)]
        for x in range(x_size)
        for c in range(cores)
    ]
    along_xc = [
        [x * x_stride + z * z_stride + c for x in range(x_size) for c in range(cores)]
        for z in range(z_size)
    ]
    along_y = [[z * y_size + y for y in range(y_size)] for z in range(z_pair)]

    def swap_cores(sent):
        return lax.ppermute(sent, "dp", other_core)

    def sum_over_x(kept, other):
        both = (kept.astype(f32) + other.astype(f32)).astype(bf16)
        blocks = both.reshape((x_size, z_size) + both.shape[1:])
        return sum_low(send_to_all(blocks, "dp", along_x))

    rows = ((tokens, width), f32)
    by_token = (y_size, z_pair, own, columns)
    half = (x_size * z_size, per_device)
    normed_part, w_kept, w_sent, xg, misc = call(
        functools.partial(scan_kernel, scale=scale),
        "scan",
        [
            (by_token, bf16, local),
            (half + (width,), bf16, local),
            (half + (width,), bf16, local),
            ((tokens, width), f32, local),
            ((state + 8, width), f32, local),
        ],
        [
            rows,
            rows,
            rows,
            rows,
            ((state, width), f32),
            ((tokens, rank), bf16),
            ((tokens, 2 * state, lane), f32),
            ((tokens, state, width), f32),
            ((tokens, state, lane), f32),
            ((tokens, state, lane), f32),
            rows,
            rows,
        ],
        44,
        core,
        full_proj,
        far=(dt_gain_row, bc_gain_row, w_dt, bias_row, x_rows, gy_rows, a_log, skip_row),
    )
    shared_rows = z_pair * own
    normed_parts = send_to_all(
        normed_part.reshape(y_size, shared_rows, columns), "tensor", along_y
    )
    (mine,) = call(
        sum_kernel, "join", [((shared_rows, columns), f32, local)], [], 4, normed_parts
    )
    mine, w_other = lax.optimization_barrier((mine, swap_cores(w_sent)))
    w_by_x = sum_over_x(w_kept, w_other)
    other = lax.ppermute(
        mine, "tensor", [(index, (index + y_size) % tensor) for index in range(tensor)]
    )
    other, w_by_x = lax.optimization_barrier((other, w_by_x))
    y_index = (lax.axis_index("tensor") % y_size).astype(jnp.int32).reshape(1)
    (own_low,) = call(
        functools.partial(norm_kernel, state=state),
        "norm",
        [((y_size, shared_rows, columns), bf16, local)],
        [((shared_rows, columns), f32)],
        4,
        y_index,
        mine,
        other,
        full_proj.reshape(z_pair, y_size, own, columns),
        dt_gain_row,
        bc_gain_row,
    )
    low = send_to_all(own_low, "tensor", along_y).reshape(by_token)
    half_row = (half + (width + lane,), bf16)
    kept, sent = call(
        functools.partial(project_kernel, rank=rank, bc_width=bc_width, scale=scale),
        "project",
        [half_row + (local,), half_row + (local,)],
        [
            ((rank, width + lane), bf16),
            ((64, width), f32),
            ((tokens, columns), bf16),
        ],
        16,
        core,
        low,
        x_rows,
        misc,
    )
    (grad_x,) = call(
        grad_x_kernel,
        "grad_x",
        [((tokens, width), bf16)],
        [((tokens, columns), bf16)],
        16,
        low,
        xg,
        w_xdt,
        w_xbc,
    )
    swapped, grad_x = lax.optimization_barrier((swap_cores(sent), grad_x))
    by_x = sum_over_x(kept, swapped)
    by_z = by_x[:, :, width:].transpose(1, 0, 2).reshape(1, per_device, z_size * lane)
    by_z = jnp.broadcast_to(by_z, (z_size, per_device, z_size * lane))
    by_z = jnp.concatenate([by_x[:, :, :width], w_by_x, by_z], axis=2)
    all_parts = send_to_all(by_z, "dp", along_z)
    shared = x_size * cores
    grad_w_xdt, grad_w_dt, own_total = call(
        total_kernel,
        "total",
        [
            ((per_device, width), f32),
            ((per_device, width), f32),
            ((shared, per_device, z_size * lane), f32, local),
        ],
        [],
        4,
        all_parts,
    )
    totals = send_to_all(own_total, "dp", along_xc)
    order = tuple(
        (x * cores + c, z) for x in range(x_size) for z in range(z_size) for c in range(cores)
    )
    grad_w_xbc, grad_a_log, bias_total, skip_total, dt_gain_total, bc_gain_total = call(
        functools.partial(spread_kernel, order=order),
        "spread",
        [
            ((bc_width, width), f32),
            ((state, width), f32),
            ((1, width), f32),
            ((1, width), f32),
            ((1, rank), f32),
            ((1, bc_width), f32),
        ],
        [((64, width), f32)],
        4,
        totals,
    )
    return (
        grad_x[None],
        grad_w_xdt,
        grad_w_dt,
        grad_w_xbc,
        grad_a_log,
        bias_total.reshape(width),
        skip_total.reshape(width),
        dt_gain_total.reshape(rank),
        bc_gain_total.reshape(bc_width),
    )


def solution(mesh):
    return jax.shard_map(
        body,
        mesh=mesh,
        in_specs=(
            P("dp", None, "tensor"),
            P("dp", "tensor", None),
            P("dp", "tensor", None),
            P("dp", None, "tensor"),
            P(None, "tensor"),
            P(None, "tensor"),
            P(None, "tensor"),
            P("tensor"),
            P(None, "tensor"),
            P("tensor"),
            P(),
            P(),
        ),
        out_specs=(
            P("dp", None, "tensor"),
            P("dp", "tensor"),
            P("dp", "tensor"),
            P(None, "tensor"),
            P(None, "tensor"),
            P("tensor"),
            P("tensor"),
            P(),
            P(),
        ),
        check_vma=False,
    )
```

```python
import functools
import math

import jax
import jax.numpy as jnp
from jax import lax
from jax.experimental import pallas as pl
from jax.experimental.pallas import tpu as pltpu
from jax.sharding import PartitionSpec as P

norm_eps = 1e-06
state_floor = 0.25
log2_e = 1.4426950408889634
lane = 128
f32 = jnp.float32
bf16 = jnp.bfloat16
contract_rows = (((0,), (0,)), ((), ()))
contract_cols = (((1,), (1,)), ((), ()))
in_vmem = pl.BlockSpec(memory_space=pltpu.VMEM)


def inverse_norms(proj, rank, state):
    dt_part = proj[:, :rank]
    b_part = proj[:, rank : rank + state]
    c_part = proj[:, rank + state : rank + 2 * state]
    dt_square = jnp.mean(dt_part * dt_part, axis=1, keepdims=True)
    b_square = jnp.mean(b_part * b_part, axis=1, keepdims=True)
    c_square = jnp.mean(c_part * c_part, axis=1, keepdims=True)
    return (
        (dt_part, lax.rsqrt(dt_square + norm_eps)),
        (b_part, lax.rsqrt(jnp.maximum(b_square, state_floor)), b_square),
        (c_part, lax.rsqrt(jnp.maximum(c_square, state_floor)), c_square),
    )


def pack_kernel(dt_in, bc_in, out_ref, dt_ref, bc_ref, arrived):
    rank, bc_width = dt_ref.shape[1], bc_ref.shape[1]
    spare = out_ref.shape[2] - rank - bc_width
    arrivals = [
        pltpu.make_async_copy(dt_in, dt_ref, arrived.at[0]),
        pltpu.make_async_copy(bc_in, bc_ref, arrived.at[1]),
    ]
    for copy in arrivals:
        copy.start()
    for copy in arrivals:
        copy.wait()
    for peer in range(out_ref.shape[0]):
        out_ref[peer, :, :rank] = dt_ref[...]
        out_ref[peer, :, rank : rank + bc_width] = bc_ref[...]
        out_ref[peer, :, rank + bc_width :] = jnp.zeros((dt_ref.shape[0], spare), bf16)


def split_cores(core_ref, whole, keep_ref, send_ref):
    first_core = core_ref[0] == 0
    for pair in range(keep_ref.shape[0] // 16):
        even = whole[32 * pair : 32 * pair + 16]
        odd = whole[32 * pair + 16 : 32 * pair + 32]
        keep_ref[16 * pair : 16 * pair + 16] = jnp.where(first_core, even, odd)
        send_ref[16 * pair : 16 * pair + 16] = jnp.where(first_core, odd, even)


def scan_kernel(
    core_ref,
    proj_ref,
    dt_gain_in,
    bc_gain_in,
    w_in,
    bias_in,
    x_in,
    gy_in,
    alog_in,
    skip_in,
    normed_ref,
    w_keep_ref,
    w_send_ref,
    xg_ref,
    misc_ref,
    dt_s,
    gy_s,
    src_s,
    sig_s,
    a2_s,
    low_s,
    bcb_s,
    u_s,
    b_acc,
    c_acc,
    s1_s,
    s2_s,
    dt_gain_ref,
    bc_gain_ref,
    w_ref,
    bias_ref,
    x_ref,
    gy_ref,
    alog_ref,
    skip_ref,
    arrived,
    *,
    scale,
    forward_lanes=512,
    forward_rows=32,
    backward_lanes=512,
    backward_rows=16,
):
    tokens, width = x_ref.shape
    state = alog_ref.shape[0]
    rank = w_ref.shape[0]
    arrivals = [
        pltpu.make_async_copy(source, held, arrived.at[index])
        for index, (source, held) in enumerate(
            (
                (dt_gain_in, dt_gain_ref),
                (bc_gain_in, bc_gain_ref),
                (w_in, w_ref),
                (bias_in, bias_ref),
                (x_in, x_ref),
                (gy_in, gy_ref),
                (alog_in, alog_ref),
                (skip_in, skip_ref),
            )
        )
    ]
    for copy in arrivals:
        copy.start()
    b_acc[...] = jnp.zeros_like(b_acc)
    c_acc[...] = jnp.zeros_like(c_acc)
    dt_norm, b_norm, c_norm = inverse_norms(proj_ref[...].astype(f32), rank, state)
    arrivals[0].wait()
    arrivals[1].wait()
    low_s[...] = (dt_norm[0] * dt_norm[1] * dt_gain_ref[...]).astype(bf16)
    b_rows = b_norm[0] * b_norm[1] * bc_gain_ref[:, :state]
    c_rows = c_norm[0] * c_norm[1] * bc_gain_ref[:, state:]
    bcb_s[:, :state] = jnp.broadcast_to(b_rows[:, :, None], (tokens, state, lane))
    bcb_s[:, state:] = jnp.broadcast_to(c_rows[:, :, None], (tokens, state, lane))
    arrivals[2].wait()
    arrivals[3].wait()
    pre = jnp.dot(low_s[...], w_ref[...], preferred_element_type=f32) + bias_ref[...]
    small = jnp.exp(-jnp.abs(pre))
    dt_rows = jnp.maximum(pre, 0.0) + jnp.log1p(small)
    sig_s[...] = jnp.where(pre >= 0, 1.0, small) / (1.0 + small)
    for copy in arrivals[4:]:
        copy.wait()
    x_float = x_ref[...].astype(f32)
    gy_float = gy_ref[...].astype(f32)
    dt_s[...] = dt_rows
    gy_s[...] = gy_float
    src_s[...] = dt_rows * x_float
    a_mat = -jnp.exp(alog_ref[...])
    a2_s[...] = a_mat * log2_e
    def widen(part, width):
        return jnp.concatenate([part] * (width // lane), axis=1)

    def fold(part):
        total = part[:, :lane]
        for start in range(lane, part.shape[1], lane):
            total = total + part[:, start : start + lane]
        return total

    def fold_states(part):
        total = part[:8]
        for rep in range(1, state // 8):
            total = total + part[rep * 8 : (rep + 1) * 8]
        return total

    def join_rows(early, late, level):
        mine = (lax.broadcasted_iota(jnp.int32, early.shape, 0) & level) == 0
        kept = jnp.where(mine, early, late)
        moved = jnp.where(mine, late, early)
        return kept + pltpu.roll(moved, 8 - level, 0)

    wide = min(forward_lanes, width)
    for group in range(width // wide):
        cols = slice(group * wide, (group + 1) * wide)

        def forward(block, held):
            a2 = a2_s[:, cols]
            for offset in range(forward_rows):
                t = block * forward_rows + offset
                decayed = jnp.exp2(dt_s[pl.ds(t, 1), cols] * a2) * held
                u_s[pl.ds(t, 1), :, cols] = decayed[None]
                c_acc[pl.ds(t, 1)] += fold(decayed * gy_s[pl.ds(t, 1), cols])[None]
                held = decayed + src_s[pl.ds(t, 1), cols] * widen(bcb_s[t, :state], wide)
            return held

        lax.fori_loop(0, tokens // forward_rows, forward, jnp.zeros((state, wide), f32))

    wide = min(backward_lanes, width)
    for group in range(width // wide):
        cols = slice(group * wide, (group + 1) * wide)

        def backward(step, carry):
            later, a_total = carry
            a2 = a2_s[:, cols]
            for part in range(backward_rows // 8 - 1, -1, -1):
                first_row = tokens - (step + 1) * backward_rows + part * 8
                waiting = {}
                for offset in range(7, -1, -1):
                    t = first_row + offset
                    dt_now = dt_s[pl.ds(t, 1), cols]
                    adjoint = (
                        widen(bcb_s[t, state:], wide) * gy_s[pl.ds(t, 1), cols] + later
                    )
                    through = adjoint * u_s[t, :, cols]
                    first = fold_states(adjoint * widen(bcb_s[t, :state], wide))
                    second = fold_states(through * a2)
                    level = 1
                    while level in waiting:
                        later_first, later_second = waiting.pop(level)
                        first = join_rows(first, later_first, level)
                        second = join_rows(second, later_second, level)
                        level *= 2
                    waiting[level] = (first, second)
                    b_acc[pl.ds(t, 1)] += fold(adjoint * src_s[pl.ds(t, 1), cols])[None]
                    a_total = a_total + dt_now * through
                    later = jnp.exp2(dt_now * a2) * adjoint
                rows = pl.ds(pl.multiple_of(first_row, 8), 8)
                s1_s[rows, cols], s2_s[rows, cols] = waiting[8]
            return later, a_total

        zeros = jnp.zeros((state, wide), f32)
        _, a_total = lax.fori_loop(0, tokens // backward_rows, backward, (zeros, zeros))
        misc_ref[:state, cols] = (scale / log2_e) * (a_total * a2_s[:, cols])

    s1 = s1_s[...]
    xg_ref[...] = dt_s[...] * s1 + skip_ref[...] * gy_s[...]
    dt_grad = x_ref[...].astype(f32) * s1 + s2_s[...] * (1.0 / log2_e)
    pre_float = dt_grad * sig_s[...]
    pre_grad = pre_float.astype(bf16)
    misc_ref[state : state + 1, :] = scale * jnp.sum(pre_float, axis=0, keepdims=True)
    misc_ref[state + 1 : state + 2, :] = scale * jnp.sum(
        gy_s[...] * x_ref[...].astype(f32), axis=0, keepdims=True
    )
    dt_normed = lax.dot_general(
        pre_grad, w_ref[...], contract_cols, preferred_element_type=f32
    ).astype(bf16)
    w_part = scale * lax.dot_general(
        low_s[...], pre_grad, contract_rows, preferred_element_type=f32
    )
    split_cores(core_ref, w_part.astype(bf16), w_keep_ref, w_send_ref)
    source_sum = jnp.sum(src_s[...] * gy_s[...], axis=1, keepdims=True)
    b_grad = jnp.sum(b_acc[...], axis=2)
    c_grad = jnp.sum(c_acc[...], axis=2) + b_rows * source_sum
    b_grad = b_grad.astype(bf16)
    c_grad = c_grad.astype(bf16)
    z_size, y_size, own = normed_ref.shape[1], normed_ref.shape[0], normed_ref.shape[2]
    for y in range(y_size):
        for z in range(z_size):
            rows = slice((z * y_size + y) * own, (z * y_size + y + 1) * own)
            normed_ref[y, z, :, :rank] = dt_normed[rows]
            normed_ref[y, z, :, rank : rank + state] = b_grad[rows]
            normed_ref[y, z, :, rank + state : rank + 2 * state] = c_grad[rows]
            normed_ref[y, z, :, rank + 2 * state :] = jnp.zeros(
                (own, lane - 2 * state), bf16
            )


def join_kernel(parts_ref, kept_ref, other_ref, out_ref, both_ref):
    both_ref[...] = (kept_ref[...].astype(f32) + other_ref[...].astype(f32)).astype(bf16)
    total = parts_ref[0].astype(f32)
    for peer in range(1, parts_ref.shape[0]):
        total = total + parts_ref[peer].astype(f32)
    out_ref[...] = total


def norm_kernel(
    y_ref, mine_ref, other_ref, proj_ref, dt_gain_ref, bc_gain_ref, out_ref, pack_s, *, state
):
    rank = dt_gain_ref.shape[1]
    rows = mine_ref.shape[0]
    grads = mine_ref[...] + other_ref[...]
    proj = jnp.concatenate([proj_ref[z, y_ref[0]] for z in range(proj_ref.shape[0])], axis=0)
    dt_norm, b_norm, c_norm = inverse_norms(proj.astype(f32), rank, state)
    dt_grad = grads[:, :rank]
    dt_unit = dt_norm[0] * dt_norm[1]
    dt_cot = dt_grad * dt_gain_ref[...]
    dt_mean = jnp.mean(dt_cot * dt_unit, axis=1, keepdims=True)
    pack_s[:, rank:] = jnp.zeros((rows, lane), f32)
    pack_s[:, :rank] = dt_norm[1] * (dt_cot - dt_unit * dt_mean)
    dt_gain_part = jnp.sum(dt_grad * dt_unit, axis=0, keepdims=True)
    last = rank + lane // 2
    for piece in range(rank // (lane // 2)):
        pack_s[piece : piece + 1, last:] = dt_gain_part[
            :, piece * (lane // 2) : (piece + 1) * (lane // 2)
        ]
    gain_row = rank // (lane // 2)
    for index, part in enumerate((b_norm, c_norm)):
        start = rank + index * state
        grad = grads[:, start : start + state]
        unit = part[0] * part[1]
        cot = grad * bc_gain_ref[:, index * state : (index + 1) * state]
        mean = jnp.mean(cot * unit, axis=1, keepdims=True)
        inner = jnp.where(part[2] > state_floor, mean, 0.0)
        inner = jnp.where(part[2] == state_floor, 0.5 * mean, inner)
        pack_s[:, start : start + state] = part[1] * (cot - unit * inner)
        pack_s[gain_row : gain_row + 1, last + index * state : last + (index + 1) * state] = (
            jnp.sum(grad * unit, axis=0, keepdims=True)
        )
    gains = pack_s[: rows // 2, last:]
    pack_s[rows // 2 :, last:] = gains - gains.astype(bf16).astype(f32)
    packed = pack_s[...].astype(bf16)
    for peer in range(out_ref.shape[0]):
        out_ref[peer] = packed


def to_tokens(low_ref, low_s):
    y_size, z_size, own, _ = low_ref.shape
    for y in range(y_size):
        for z in range(z_size):
            start = (z * y_size + y) * own
            low_s[start : start + own, :] = low_ref[y, z]


def grad_x_kernel(low_ref, xg_ref, w_xdt_ref, w_xbc_ref, grad_x_ref, low_s):
    rank = w_xdt_ref.shape[0]
    bc_width = w_xbc_ref.shape[0]
    to_tokens(low_ref, low_s)
    summed = xg_ref[...] + jnp.dot(
        low_s[:, :rank], w_xdt_ref[...], preferred_element_type=f32
    )
    summed = summed + jnp.dot(
        low_s[:, rank : rank + bc_width], w_xbc_ref[...], preferred_element_type=f32
    )
    grad_x_ref[...] = summed.astype(bf16)


def project_kernel(
    core_ref,
    low_ref,
    x_ref,
    misc_ref,
    keep_ref,
    send_ref,
    sums_ref,
    all_s,
    low_s,
    *,
    rank,
    bc_width,
    scale,
):
    width = x_ref.shape[1]
    y_size, z_size, own, _ = low_ref.shape
    to_tokens(low_ref, low_s)
    dt_low = low_s[:, :rank]
    bc_low = low_s[:, rank : rank + bc_width]
    part = (
        scale
        * lax.dot_general(dt_low, x_ref[...], contract_rows, preferred_element_type=f32)
    ).astype(bf16)
    state = bc_width // 2
    all_s[...] = jnp.zeros_like(all_s)
    all_s[: state + 2, :] = misc_ref[: state + 2, :]
    all_s[state + 8 : state + 8 + bc_width, :] = scale * lax.dot_general(
        bc_low, x_ref[...], contract_rows, preferred_element_type=f32
    )
    gains = jnp.zeros((own, lane), f32)
    for y in range(y_size):
        for z in range(z_size):
            gains = gains + low_ref[y, z, :, rank:].astype(f32)
    gains = scale * gains[:, lane // 2 :]
    gain_row = state + 8 + bc_width
    for piece in range(rank // (lane // 2)):
        all_s[gain_row : gain_row + 1, piece * (lane // 2) : (piece + 1) * (lane // 2)] = gains[
            piece : piece + 1
        ]
    piece = rank // (lane // 2)
    all_s[gain_row : gain_row + 1, rank : rank + bc_width] = gains[piece : piece + 1, :bc_width]
    split_cores(core_ref, part, keep_ref, send_ref)
    sums = all_s[...].astype(bf16)
    sums_ref[...] = sums
    send_ref[rank // 2 :, :] = sums


def total_kernel(parts_ref, xdt_ref, dt_ref):
    width = xdt_ref.shape[1]
    total = parts_ref[0].astype(f32)
    for peer in range(1, parts_ref.shape[0]):
        total = total + parts_ref[peer].astype(f32)
    xdt_ref[...] = total[:, :width]
    dt_ref[...] = total[:, width:]


def add_kernel(one_ref, other_ref, out_ref):
    out_ref[...] = (one_ref[...].astype(f32) + other_ref[...].astype(f32)).astype(bf16)


def spread_kernel(
    one_ref, other_ref, xbc_ref, alog_ref, bias_ref, skip_ref, dt_gain_ref, bc_gain_ref
):
    state = alog_ref.shape[0]
    bc_width = xbc_ref.shape[0]
    rank = dt_gain_ref.shape[1]
    total = one_ref[...].astype(f32) + other_ref[...].astype(f32)
    alog_ref[...] = total[:state, :]
    bias_ref[...] = total[state : state + 1, :]
    skip_ref[...] = total[state + 1 : state + 2, :]
    xbc_ref[...] = total[state + 8 : state + 8 + bc_width, :]
    gain_row = state + 8 + bc_width
    dt_gain_ref[...] = total[gain_row : gain_row + 1, :rank]
    bc_gain_ref[...] = total[gain_row : gain_row + 1, rank : rank + bc_width]


def call(kernel, name, outs, scratch, limit_mib, *args, far=()):
    in_smem = pl.BlockSpec(memory_space=pltpu.SMEM)
    in_hbm = pl.BlockSpec(memory_space=pltpu.HBM)
    return pl.pallas_call(
        kernel,
        out_shape=tuple(
            pltpu.VMEM(out[0], out[1]) if len(out) > 2 else jax.ShapeDtypeStruct(*out)
            for out in outs
        ),
        in_specs=[in_smem if arg.dtype == jnp.int32 else in_vmem for arg in args]
        + [in_hbm] * len(far),
        out_specs=tuple([in_vmem] * len(outs)),
        scratch_shapes=[pltpu.VMEM(shape, dtype) for shape, dtype in scratch]
        + [pltpu.VMEM(arg.shape, arg.dtype) for arg in far]
        + ([pltpu.SemaphoreType.DMA((len(far),))] if far else []),
        compiler_params=pltpu.CompilerParams(vmem_limit_bytes=limit_mib * 2**20),
        name=name,
    )(*args, *[pltpu.with_memory_space_constraint(arg, pltpu.HBM) for arg in far])


def send_to_all(block, axis, groups=None):
    return lax.all_to_all(block, axis, 0, 0, axis_index_groups=groups)


def sum_low(parts):
    return jnp.sum(parts.astype(f32), axis=0).astype(bf16)


def body(
    x_inner, proj_dt, proj_bc, grad_y, w_xdt, w_xbc, w_dt, dt_bias, a_log, d_skip, dt_gain, bc_gain
):
    x_rows = x_inner[0]
    gy_rows = grad_y[0]
    tokens, width = x_rows.shape
    rank = proj_dt.shape[2]
    bc_width = proj_bc.shape[2]
    state = bc_width // 2
    own = proj_dt.shape[1]
    dp = lax.axis_size("dp")
    tensor = lax.axis_size("tensor")
    scale = 1.0 / math.sqrt(dp * tokens)
    bias_row = dt_bias.reshape(1, width)
    skip_row = d_skip.reshape(1, width)
    dt_gain_row = dt_gain.reshape(1, rank)
    bc_gain_row = bc_gain.reshape(1, bc_width)

    columns = rank + lane
    local = True
    (own_proj,) = call(
        pack_kernel,
        "pack",
        [((tensor, own, columns), bf16, local)],
        [],
        4,
        far=(proj_dt[0], proj_bc[0]),
    )
    full_proj = send_to_all(own_proj, "tensor").reshape(tokens, columns)

    cores, z_size, z_pair = 2, 4, 2
    x_size = dp // (cores * z_size)
    y_size = tensor // z_pair
    per_device = rank // dp
    core = (lax.axis_index("dp") % cores).astype(jnp.int32).reshape(1)
    z_stride, x_stride = cores, cores * z_size
    along_x = [[x * x_stride + rest for x in range(x_size)] for rest in range(x_stride)]
    along_z = [
        [x * x_stride + z * z_stride + c for z in range(z_size)]
        for x in range(x_size)
        for c in range(cores)
    ]
    along_y = [[z * y_size + y for y in range(y_size)] for z in range(z_pair)]

    def swap(sent, flip):
        return lax.ppermute(sent, "dp", [(index, index ^ flip) for index in range(dp)])

    def sum_over_x(both):
        blocks = both.reshape(x_size, z_size, per_device, width)
        return sum_low(send_to_all(blocks, "dp", along_x))

    rows = ((tokens, width), f32)
    by_token = (y_size, z_pair, own, columns)
    half = (rank // cores, width)
    normed_part, w_kept, w_sent, xg, misc = call(
        functools.partial(scan_kernel, scale=scale),
        "scan",
        [
            (by_token, bf16, local),
            (half, bf16, local),
            (half, bf16, local),
            ((tokens, width), f32, local),
            ((state + 8, width), f32, local),
        ],
        [
            rows,
            rows,
            rows,
            rows,
            ((state, width), f32),
            ((tokens, rank), bf16),
            ((tokens, 2 * state, lane), f32),
            ((tokens, state, width), f32),
            ((tokens, state, lane), f32),
            ((tokens, state, lane), f32),
            rows,
            rows,
        ],
        44,
        core,
        full_proj,
        far=(dt_gain_row, bc_gain_row, w_dt, bias_row, x_rows, gy_rows, a_log, skip_row),
    )
    shared_rows = z_pair * own
    normed_parts = send_to_all(
        normed_part.reshape(y_size, shared_rows, columns), "tensor", along_y
    )
    mine, w_both = call(
        join_kernel,
        "join",
        [((shared_rows, columns), f32, local), (half, bf16)],
        [],
        16,
        normed_parts,
        w_kept,
        swap(w_sent, 1),
    )
    w_by_x = sum_over_x(w_both)
    other = lax.ppermute(
        mine, "tensor", [(index, (index + y_size) % tensor) for index in range(tensor)]
    )
    other, w_by_x = lax.optimization_barrier((other, w_by_x))
    y_index = (lax.axis_index("tensor") % y_size).astype(jnp.int32).reshape(1)
    (own_low,) = call(
        functools.partial(norm_kernel, state=state),
        "norm",
        [((y_size, shared_rows, columns), bf16, local)],
        [((shared_rows, columns), f32)],
        4,
        y_index,
        mine,
        other,
        full_proj.reshape(z_pair, y_size, own, columns),
        dt_gain_row,
        bc_gain_row,
    )
    low = send_to_all(own_low, "tensor", along_y).reshape(by_token)
    sums_shape = (64, width)
    kept, sent, sums = call(
        functools.partial(project_kernel, rank=rank, bc_width=bc_width, scale=scale),
        "project",
        [
            (half, bf16, local),
            ((half[0] + sums_shape[0], width), bf16, local),
            (sums_shape, bf16, local),
        ],
        [(sums_shape, f32), ((tokens, columns), bf16)],
        16,
        core,
        low,
        x_rows,
        misc,
    )
    (grad_x,) = call(
        grad_x_kernel,
        "grad_x",
        [((tokens, width), bf16)],
        [((tokens, columns), bf16)],
        16,
        low,
        xg,
        w_xdt,
        w_xbc,
    )
    swapped, grad_x = lax.optimization_barrier((swap(sent, 1), grad_x))
    both = (kept.astype(f32) + swapped[: half[0]].astype(f32)).astype(bf16)
    sums = (sums.astype(f32) + swapped[half[0] :].astype(f32)).astype(bf16)

    def add(one, other):
        (total,) = call(add_kernel, "add", [(sums_shape, bf16, local)], [], 4, one, other)
        return total

    by_x = sum_over_x(both)
    for flip in (x_stride, 3 * x_stride):
        sums = add(sums, swap(sums, flip))
    by_x, sums = lax.optimization_barrier((by_x, sums))
    all_parts = send_to_all(jnp.concatenate([by_x, w_by_x], axis=2), "dp", along_z)
    sums = add(sums, swap(sums, z_stride))
    last = swap(sums, 2 * z_stride)
    all_parts, last = lax.optimization_barrier((all_parts, last))
    grad_w_xdt, grad_w_dt = call(
        total_kernel,
        "total",
        [((per_device, width), f32), ((per_device, width), f32)],
        [],
        4,
        all_parts,
    )
    grad_w_xbc, grad_a_log, bias_total, skip_total, dt_gain_total, bc_gain_total = call(
        spread_kernel,
        "spread",
        [
            ((bc_width, width), f32),
            ((state, width), f32),
            ((1, width), f32),
            ((1, width), f32),
            ((1, rank), f32),
            ((1, bc_width), f32),
        ],
        [],
        4,
        sums,
        last,
    )
    return (
        grad_x[None],
        grad_w_xdt,
        grad_w_dt,
        grad_w_xbc,
        grad_a_log,
        bias_total.reshape(width),
        skip_total.reshape(width),
        dt_gain_total.reshape(rank),
        bc_gain_total.reshape(bc_width),
    )


def solution(mesh):
    return jax.shard_map(
        body,
        mesh=mesh,
        in_specs=(
            P("dp", None, "tensor"),
            P("dp", "tensor", None),
            P("dp", "tensor", None),
            P("dp", None, "tensor"),
            P(None, "tensor"),
            P(None, "tensor"),
            P(None, "tensor"),
            P("tensor"),
            P(None, "tensor"),
            P("tensor"),
            P(),
            P(),
        ),
        out_specs=(
            P("dp", None, "tensor"),
            P("dp", "tensor"),
            P("dp", "tensor"),
            P(None, "tensor"),
            P(None, "tensor"),
            P("tensor"),
            P("tensor"),
            P(),
            P(),
        ),
        check_vma=False,
    )
```

```python
import functools
import math

import jax
import jax.numpy as jnp
from jax import lax
from jax.experimental import pallas as pl
from jax.experimental.pallas import tpu as pltpu
from jax.sharding import PartitionSpec as P

norm_eps = 1e-06
state_floor = 0.25
log2_e = 1.4426950408889634
lane = 128
f32 = jnp.float32
bf16 = jnp.bfloat16
contract_rows = (((0,), (0,)), ((), ()))
contract_cols = (((1,), (1,)), ((), ()))
in_vmem = pl.BlockSpec(memory_space=pltpu.VMEM)


def inverse_norms(proj, rank, state):
    dt_part = proj[:, :rank]
    b_part = proj[:, rank : rank + state]
    c_part = proj[:, rank + state : rank + 2 * state]
    dt_square = jnp.mean(dt_part * dt_part, axis=1, keepdims=True)
    b_square = jnp.mean(b_part * b_part, axis=1, keepdims=True)
    c_square = jnp.mean(c_part * c_part, axis=1, keepdims=True)
    return (
        (dt_part, lax.rsqrt(dt_square + norm_eps)),
        (b_part, lax.rsqrt(jnp.maximum(b_square, state_floor)), b_square),
        (c_part, lax.rsqrt(jnp.maximum(c_square, state_floor)), c_square),
    )


def pack_kernel(dt_in, bc_in, out_ref, dt_ref, bc_ref, arrived):
    rank, bc_width = dt_ref.shape[1], bc_ref.shape[1]
    spare = out_ref.shape[2] - rank - bc_width
    arrivals = [
        pltpu.make_async_copy(dt_in, dt_ref, arrived.at[0]),
        pltpu.make_async_copy(bc_in, bc_ref, arrived.at[1]),
    ]
    for copy in arrivals:
        copy.start()
    for copy in arrivals:
        copy.wait()
    for peer in range(out_ref.shape[0]):
        out_ref[peer, :, :rank] = dt_ref[...]
        out_ref[peer, :, rank : rank + bc_width] = bc_ref[...]
        out_ref[peer, :, rank + bc_width :] = jnp.zeros((dt_ref.shape[0], spare), bf16)


def split_cores(core_ref, whole, keep_ref, send_ref):
    first_core = core_ref[0] == 0
    for pair in range(keep_ref.shape[0]):
        even = whole[32 * pair : 32 * pair + 16]
        odd = whole[32 * pair + 16 : 32 * pair + 32]
        keep_ref[pair] = jnp.where(first_core, even, odd)
        send_ref[pair] = jnp.where(first_core, odd, even).astype(bf16)


def scan_kernel(
    core_ref,
    proj_ref,
    dt_gain_in,
    bc_gain_in,
    w_in,
    bias_in,
    x_in,
    gy_in,
    alog_in,
    skip_in,
    normed_ref,
    w_keep_ref,
    w_send_ref,
    xg_ref,
    misc_ref,
    dt_s,
    gy_s,
    src_s,
    sig_s,
    a2_s,
    low_s,
    bcb_s,
    u_s,
    b_acc,
    c_acc,
    s1_s,
    s2_s,
    dt_gain_ref,
    bc_gain_ref,
    w_ref,
    bias_ref,
    x_ref,
    gy_ref,
    alog_ref,
    skip_ref,
    arrived,
    *,
    scale,
    forward_lanes=512,
    forward_rows=32,
    backward_lanes=512,
    backward_rows=16,
):
    tokens, width = x_ref.shape
    state = alog_ref.shape[0]
    rank = w_ref.shape[0]
    arrivals = [
        pltpu.make_async_copy(source, held, arrived.at[index])
        for index, (source, held) in enumerate(
            (
                (dt_gain_in, dt_gain_ref),
                (bc_gain_in, bc_gain_ref),
                (w_in, w_ref),
                (bias_in, bias_ref),
                (x_in, x_ref),
                (gy_in, gy_ref),
                (alog_in, alog_ref),
                (skip_in, skip_ref),
            )
        )
    ]
    for copy in arrivals:
        copy.start()
    b_acc[...] = jnp.zeros_like(b_acc)
    c_acc[...] = jnp.zeros_like(c_acc)
    dt_norm, b_norm, c_norm = inverse_norms(proj_ref[...].astype(f32), rank, state)
    arrivals[0].wait()
    arrivals[1].wait()
    low_s[...] = (dt_norm[0] * dt_norm[1] * dt_gain_ref[...]).astype(bf16)
    b_rows = b_norm[0] * b_norm[1] * bc_gain_ref[:, :state]
    c_rows = c_norm[0] * c_norm[1] * bc_gain_ref[:, state:]
    bcb_s[:, :state] = jnp.broadcast_to(b_rows[:, :, None], (tokens, state, lane))
    bcb_s[:, state:] = jnp.broadcast_to(c_rows[:, :, None], (tokens, state, lane))
    arrivals[2].wait()
    arrivals[3].wait()
    pre = jnp.dot(low_s[...], w_ref[...], preferred_element_type=f32) + bias_ref[...]
    small = jnp.exp(-jnp.abs(pre))
    dt_rows = jnp.maximum(pre, 0.0) + jnp.log1p(small)
    sig_s[...] = jnp.where(pre >= 0, 1.0, small) / (1.0 + small)
    for copy in arrivals[4:]:
        copy.wait()
    x_float = x_ref[...].astype(f32)
    gy_float = gy_ref[...].astype(f32)
    dt_s[...] = dt_rows
    gy_s[...] = gy_float
    src_s[...] = dt_rows * x_float
    a_mat = -jnp.exp(alog_ref[...])
    a2_s[...] = a_mat * log2_e
    def widen(part, width):
        return jnp.concatenate([part] * (width // lane), axis=1)

    def fold(part):
        total = part[:, :lane]
        for start in range(lane, part.shape[1], lane):
            total = total + part[:, start : start + lane]
        return total

    def fold_states(part):
        total = part[:8]
        for rep in range(1, state // 8):
            total = total + part[rep * 8 : (rep + 1) * 8]
        return total

    def join_rows(early, late, level):
        mine = (lax.broadcasted_iota(jnp.int32, early.shape, 0) & level) == 0
        kept = jnp.where(mine, early, late)
        moved = jnp.where(mine, late, early)
        return kept + pltpu.roll(moved, 8 - level, 0)

    wide = min(forward_lanes, width)
    for group in range(width // wide):
        cols = slice(group * wide, (group + 1) * wide)

        def forward(block, held):
            a2 = a2_s[:, cols]
            for offset in range(forward_rows):
                t = block * forward_rows + offset
                decayed = jnp.exp2(dt_s[pl.ds(t, 1), cols] * a2) * held
                u_s[pl.ds(t, 1), :, cols] = decayed[None]
                c_acc[pl.ds(t, 1)] += fold(decayed * gy_s[pl.ds(t, 1), cols])[None]
                held = decayed + src_s[pl.ds(t, 1), cols] * widen(bcb_s[t, :state], wide)
            return held

        lax.fori_loop(0, tokens // forward_rows, forward, jnp.zeros((state, wide), f32))

    wide = min(backward_lanes, width)
    for group in range(width // wide):
        cols = slice(group * wide, (group + 1) * wide)

        def backward(step, carry):
            later, a_total = carry
            a2 = a2_s[:, cols]
            for part in range(backward_rows // 8 - 1, -1, -1):
                first_row = tokens - (step + 1) * backward_rows + part * 8
                waiting = {}
                for offset in range(7, -1, -1):
                    t = first_row + offset
                    dt_now = dt_s[pl.ds(t, 1), cols]
                    adjoint = (
                        widen(bcb_s[t, state:], wide) * gy_s[pl.ds(t, 1), cols] + later
                    )
                    through = adjoint * u_s[t, :, cols]
                    first = fold_states(adjoint * widen(bcb_s[t, :state], wide))
                    second = fold_states(through * a2)
                    level = 1
                    while level in waiting:
                        later_first, later_second = waiting.pop(level)
                        first = join_rows(first, later_first, level)
                        second = join_rows(second, later_second, level)
                        level *= 2
                    waiting[level] = (first, second)
                    b_acc[pl.ds(t, 1)] += fold(adjoint * src_s[pl.ds(t, 1), cols])[None]
                    a_total = a_total + dt_now * through
                    later = jnp.exp2(dt_now * a2) * adjoint
                rows = pl.ds(pl.multiple_of(first_row, 8), 8)
                s1_s[rows, cols], s2_s[rows, cols] = waiting[8]
            return later, a_total

        zeros = jnp.zeros((state, wide), f32)
        _, a_total = lax.fori_loop(0, tokens // backward_rows, backward, (zeros, zeros))
        misc_ref[:state, cols] = (scale / log2_e) * (a_total * a2_s[:, cols])

    s1 = s1_s[...]
    xg_ref[...] = dt_s[...] * s1 + skip_ref[...] * gy_s[...]
    dt_grad = x_ref[...].astype(f32) * s1 + s2_s[...] * (1.0 / log2_e)
    pre_float = dt_grad * sig_s[...]
    pre_grad = pre_float.astype(bf16)
    misc_ref[state : state + 1, :] = scale * jnp.sum(pre_float, axis=0, keepdims=True)
    misc_ref[state + 1 : state + 2, :] = scale * jnp.sum(
        gy_s[...] * x_ref[...].astype(f32), axis=0, keepdims=True
    )
    dt_normed = lax.dot_general(
        pre_grad, w_ref[...], contract_cols, preferred_element_type=f32
    ).astype(bf16)
    w_part = scale * lax.dot_general(
        low_s[...], pre_grad, contract_rows, preferred_element_type=f32
    )
    split_cores(core_ref, w_part, w_keep_ref, w_send_ref)
    source_sum = jnp.sum(src_s[...] * gy_s[...], axis=1, keepdims=True)
    b_grad = jnp.sum(b_acc[...], axis=2)
    c_grad = jnp.sum(c_acc[...], axis=2) + b_rows * source_sum
    b_grad = b_grad.astype(bf16)
    c_grad = c_grad.astype(bf16)
    z_size, y_size, own = normed_ref.shape[1], normed_ref.shape[0], normed_ref.shape[2]
    for y in range(y_size):
        for z in range(z_size):
            rows = slice((z * y_size + y) * own, (z * y_size + y + 1) * own)
            normed_ref[y, z, :, :rank] = dt_normed[rows]
            normed_ref[y, z, :, rank : rank + state] = b_grad[rows]
            normed_ref[y, z, :, rank + state : rank + 2 * state] = c_grad[rows]
            normed_ref[y, z, :, rank + 2 * state :] = jnp.zeros(
                (own, lane - 2 * state), bf16
            )


def join_kernel(parts_ref, kept_ref, other_ref, out_ref, both_ref):
    both_ref[...] = (kept_ref[...] + other_ref[...].astype(f32)).astype(bf16)
    total = parts_ref[0].astype(f32)
    for peer in range(1, parts_ref.shape[0]):
        total = total + parts_ref[peer].astype(f32)
    out_ref[...] = total


def norm_kernel(
    y_ref, mine_ref, other_ref, proj_ref, dt_gain_ref, bc_gain_ref, out_ref, pack_s, *, state
):
    rank = dt_gain_ref.shape[1]
    rows = mine_ref.shape[0]
    grads = mine_ref[...] + other_ref[...]
    proj = jnp.concatenate([proj_ref[z, y_ref[0]] for z in range(proj_ref.shape[0])], axis=0)
    dt_norm, b_norm, c_norm = inverse_norms(proj.astype(f32), rank, state)
    dt_grad = grads[:, :rank]
    dt_unit = dt_norm[0] * dt_norm[1]
    dt_cot = dt_grad * dt_gain_ref[...]
    dt_mean = jnp.mean(dt_cot * dt_unit, axis=1, keepdims=True)
    pack_s[:, rank:] = jnp.zeros((rows, lane), f32)
    pack_s[:, :rank] = dt_norm[1] * (dt_cot - dt_unit * dt_mean)
    dt_gain_part = jnp.sum(dt_grad * dt_unit, axis=0, keepdims=True)
    last = rank + lane // 2
    for piece in range(rank // (lane // 2)):
        pack_s[piece : piece + 1, last:] = dt_gain_part[
            :, piece * (lane // 2) : (piece + 1) * (lane // 2)
        ]
    gain_row = rank // (lane // 2)
    for index, part in enumerate((b_norm, c_norm)):
        start = rank + index * state
        grad = grads[:, start : start + state]
        unit = part[0] * part[1]
        cot = grad * bc_gain_ref[:, index * state : (index + 1) * state]
        mean = jnp.mean(cot * unit, axis=1, keepdims=True)
        inner = jnp.where(part[2] > state_floor, mean, 0.0)
        inner = jnp.where(part[2] == state_floor, 0.5 * mean, inner)
        pack_s[:, start : start + state] = part[1] * (cot - unit * inner)
        pack_s[gain_row : gain_row + 1, last + index * state : last + (index + 1) * state] = (
            jnp.sum(grad * unit, axis=0, keepdims=True)
        )
    gains = pack_s[: rows // 2, last:]
    pack_s[rows // 2 :, last:] = gains - gains.astype(bf16).astype(f32)
    packed = pack_s[...].astype(bf16)
    for peer in range(out_ref.shape[0]):
        out_ref[peer] = packed


def to_tokens(low_ref, low_s):
    y_size, z_size, own, _ = low_ref.shape
    for y in range(y_size):
        for z in range(z_size):
            start = (z * y_size + y) * own
            low_s[start : start + own, :] = low_ref[y, z]


def grad_x_kernel(low_ref, xg_ref, w_xdt_ref, w_xbc_ref, grad_x_ref, low_s):
    rank = w_xdt_ref.shape[0]
    bc_width = w_xbc_ref.shape[0]
    to_tokens(low_ref, low_s)
    summed = xg_ref[...] + jnp.dot(
        low_s[:, :rank], w_xdt_ref[...], preferred_element_type=f32
    )
    summed = summed + jnp.dot(
        low_s[:, rank : rank + bc_width], w_xbc_ref[...], preferred_element_type=f32
    )
    grad_x_ref[...] = summed.astype(bf16)


def project_kernel(
    core_ref,
    low_ref,
    x_ref,
    misc_ref,
    keep_ref,
    send_ref,
    out_s,
    all_s,
    low_s,
    *,
    rank,
    bc_width,
    scale,
):
    width = x_ref.shape[1]
    y_size, z_size, own, _ = low_ref.shape
    to_tokens(low_ref, low_s)
    dt_low = low_s[:, :rank]
    bc_low = low_s[:, rank : rank + bc_width]
    out_s[:, :width] = scale * lax.dot_general(
        dt_low, x_ref[...], contract_rows, preferred_element_type=f32
    )
    state = bc_width // 2
    all_s[...] = jnp.zeros_like(all_s)
    all_s[: state + 2, :] = misc_ref[: state + 2, :]
    all_s[state + 8 : state + 8 + bc_width, :] = scale * lax.dot_general(
        bc_low, x_ref[...], contract_rows, preferred_element_type=f32
    )
    gains = jnp.zeros((own, lane), f32)
    for y in range(y_size):
        for z in range(z_size):
            gains = gains + low_ref[y, z, :, rank:].astype(f32)
    gains = scale * gains[:, lane // 2 :]
    gain_row = state + 8 + bc_width
    for piece in range(rank // (lane // 2)):
        all_s[gain_row : gain_row + 1, piece * (lane // 2) : (piece + 1) * (lane // 2)] = gains[
            piece : piece + 1
        ]
    piece = rank // (lane // 2)
    all_s[gain_row : gain_row + 1, rank : rank + bc_width] = gains[piece : piece + 1, :bc_width]
    for piece in range(width // lane):
        out_s[piece * 64 : (piece + 1) * 64, width:] = all_s[
            :, piece * lane : (piece + 1) * lane
        ]
    split_cores(core_ref, out_s, keep_ref, send_ref)


def total_kernel(parts_ref, xdt_ref, dt_ref, own_ref):
    width = xdt_ref.shape[1]
    total = parts_ref[0].astype(f32)
    for peer in range(1, parts_ref.shape[0]):
        total = total + parts_ref[peer].astype(f32)
    xdt_ref[...] = total[:, :width]
    dt_ref[...] = total[:, width : 2 * width]
    for peer in range(own_ref.shape[0]):
        own_ref[peer] = total[:, 2 * width :].astype(bf16)


def spread_kernel(
    parts_ref, xbc_ref, alog_ref, bias_ref, skip_ref, dt_gain_ref, bc_gain_ref, all_s, *, order
):
    state = alog_ref.shape[0]
    bc_width = xbc_ref.shape[0]
    rank = dt_gain_ref.shape[1]
    for block, (peer, place) in enumerate(order):
        row, piece = 16 * (block % 4), lane * (block // 4)
        all_s[row : row + 16, piece : piece + lane] = parts_ref[
            peer, :, place * lane : (place + 1) * lane
        ].astype(f32)
    alog_ref[...] = all_s[:state, :]
    bias_ref[...] = all_s[state : state + 1, :]
    skip_ref[...] = all_s[state + 1 : state + 2, :]
    xbc_ref[...] = all_s[state + 8 : state + 8 + bc_width, :]
    gain_row = state + 8 + bc_width
    dt_gain_ref[...] = all_s[gain_row : gain_row + 1, :rank]
    bc_gain_ref[...] = all_s[gain_row : gain_row + 1, rank : rank + bc_width]


def call(kernel, name, outs, scratch, limit_mib, *args, far=()):
    in_smem = pl.BlockSpec(memory_space=pltpu.SMEM)
    in_hbm = pl.BlockSpec(memory_space=pltpu.HBM)
    return pl.pallas_call(
        kernel,
        out_shape=tuple(
            pltpu.VMEM(out[0], out[1]) if len(out) > 2 else jax.ShapeDtypeStruct(*out)
            for out in outs
        ),
        in_specs=[in_smem if arg.dtype == jnp.int32 else in_vmem for arg in args]
        + [in_hbm] * len(far),
        out_specs=tuple([in_vmem] * len(outs)),
        scratch_shapes=[pltpu.VMEM(shape, dtype) for shape, dtype in scratch]
        + [pltpu.VMEM(arg.shape, arg.dtype) for arg in far]
        + ([pltpu.SemaphoreType.DMA((len(far),))] if far else []),
        compiler_params=pltpu.CompilerParams(vmem_limit_bytes=limit_mib * 2**20),
        name=name,
    )(*args, *[pltpu.with_memory_space_constraint(arg, pltpu.HBM) for arg in far])


def send_to_all(block, axis, groups=None):
    return lax.all_to_all(block, axis, 0, 0, axis_index_groups=groups)


def sum_low(parts):
    return jnp.sum(parts.astype(f32), axis=0).astype(bf16)


def body(
    x_inner, proj_dt, proj_bc, grad_y, w_xdt, w_xbc, w_dt, dt_bias, a_log, d_skip, dt_gain, bc_gain
):
    x_rows = x_inner[0]
    gy_rows = grad_y[0]
    tokens, width = x_rows.shape
    rank = proj_dt.shape[2]
    bc_width = proj_bc.shape[2]
    state = bc_width // 2
    own = proj_dt.shape[1]
    dp = lax.axis_size("dp")
    tensor = lax.axis_size("tensor")
    scale = 1.0 / math.sqrt(dp * tokens)
    bias_row = dt_bias.reshape(1, width)
    skip_row = d_skip.reshape(1, width)
    dt_gain_row = dt_gain.reshape(1, rank)
    bc_gain_row = bc_gain.reshape(1, bc_width)

    columns = rank + lane
    cores, z_size, z_pair = 2, 4, 2
    x_size = dp // (cores * z_size)
    y_size = tensor // z_pair
    per_device = rank // dp
    other_core = [(index, index ^ 1) for index in range(dp)]
    core = (lax.axis_index("dp") % cores).astype(jnp.int32).reshape(1)
    y_index = (lax.axis_index("tensor") % y_size).astype(jnp.int32).reshape(1)
    local = True
    (own_proj,) = call(
        pack_kernel,
        "pack",
        [((tensor, own, columns), bf16, local)],
        [],
        4,
        far=(proj_dt[0], proj_bc[0]),
    )
    own_proj, core, y_index = lax.optimization_barrier((own_proj, core, y_index))
    full_proj = send_to_all(own_proj, "tensor").reshape(tokens, columns)

    z_stride, x_stride = cores, cores * z_size
    along_x = [[x * x_stride + rest for x in range(x_size)] for rest in range(x_stride)]
    along_z = [
        [x * x_stride + z * z_stride + c for z in range(z_size)]
        for x in range(x_size)
        for c in range(cores)
    ]
    along_xc = [
        [x * x_stride + z * z_stride + c for x in range(x_size) for c in range(cores)]
        for z in range(z_size)
    ]
    along_y = [[z * y_size + y for y in range(y_size)] for z in range(z_pair)]

    def swap_cores(sent):
        return lax.ppermute(sent, "dp", other_core)

    def sum_over_x(both):
        blocks = both.reshape((x_size, z_size) + both.shape[1:])
        return sum_low(send_to_all(blocks, "dp", along_x))

    rows = ((tokens, width), f32)
    by_token = (y_size, z_pair, own, columns)
    half = (x_size * z_size, per_device)
    normed_part, w_kept, w_sent, xg, misc = call(
        functools.partial(scan_kernel, scale=scale),
        "scan",
        [
            (by_token, bf16, local),
            (half + (width,), f32, local),
            (half + (width,), bf16, local),
            ((tokens, width), f32, local),
            ((state + 8, width), f32, local),
        ],
        [
            rows,
            rows,
            rows,
            rows,
            ((state, width), f32),
            ((tokens, rank), bf16),
            ((tokens, 2 * state, lane), f32),
            ((tokens, state, width), f32),
            ((tokens, state, lane), f32),
            ((tokens, state, lane), f32),
            rows,
            rows,
        ],
        44,
        core,
        full_proj,
        far=(dt_gain_row, bc_gain_row, w_dt, bias_row, x_rows, gy_rows, a_log, skip_row),
    )
    shared_rows = z_pair * own
    normed_parts = send_to_all(
        normed_part.reshape(y_size, shared_rows, columns), "tensor", along_y
    )
    mine, w_both = call(
        join_kernel,
        "join",
        [((shared_rows, columns), f32, local), (half + (width,), bf16)],
        [],
        16,
        normed_parts,
        w_kept,
        swap_cores(w_sent),
    )
    w_by_x = sum_over_x(w_both)
    other = lax.ppermute(
        mine, "tensor", [(index, (index + y_size) % tensor) for index in range(tensor)]
    )
    other, w_by_x = lax.optimization_barrier((other, w_by_x))
    (own_low,) = call(
        functools.partial(norm_kernel, state=state),
        "norm",
        [((y_size, shared_rows, columns), bf16, local)],
        [((shared_rows, columns), f32)],
        4,
        y_index,
        mine,
        other,
        full_proj.reshape(z_pair, y_size, own, columns),
        dt_gain_row,
        bc_gain_row,
    )
    low = send_to_all(own_low, "tensor", along_y).reshape(by_token)
    half_row = (half + (width + lane,), bf16)
    kept, sent = call(
        functools.partial(project_kernel, rank=rank, bc_width=bc_width, scale=scale),
        "project",
        [(half_row[0], f32, local), half_row + (local,)],
        [
            ((rank, width + lane), f32),
            ((64, width), f32),
            ((tokens, columns), bf16),
        ],
        16,
        core,
        low,
        x_rows,
        misc,
    )
    (grad_x,) = call(
        grad_x_kernel,
        "grad_x",
        [((tokens, width), bf16)],
        [((tokens, columns), bf16)],
        16,
        low,
        xg,
        w_xdt,
        w_xbc,
    )
    swapped, grad_x = lax.optimization_barrier((swap_cores(sent), grad_x))
    by_x = sum_over_x((kept + swapped.astype(f32)).astype(bf16))
    by_z = by_x[:, :, width:].transpose(1, 0, 2).reshape(1, per_device, z_size * lane)
    by_z = jnp.broadcast_to(by_z, (z_size, per_device, z_size * lane))
    by_z = jnp.concatenate([by_x[:, :, :width], w_by_x, by_z], axis=2)
    all_parts = send_to_all(by_z, "dp", along_z)
    shared = x_size * cores
    grad_w_xdt, grad_w_dt, own_total = call(
        total_kernel,
        "total",
        [
            ((per_device, width), f32),
            ((per_device, width), f32),
            ((shared, per_device, z_size * lane), bf16, local),
        ],
        [],
        4,
        all_parts,
    )
    totals = send_to_all(own_total, "dp", along_xc)
    order = tuple(
        (x * cores + c, z) for x in range(x_size) for z in range(z_size) for c in range(cores)
    )
    grad_w_xbc, grad_a_log, bias_total, skip_total, dt_gain_total, bc_gain_total = call(
        functools.partial(spread_kernel, order=order),
        "spread",
        [
            ((bc_width, width), f32),
            ((state, width), f32),
            ((1, width), f32),
            ((1, width), f32),
            ((1, rank), f32),
            ((1, bc_width), f32),
        ],
        [((64, width), f32)],
        4,
        totals,
    )
    return (
        grad_x[None],
        grad_w_xdt,
        grad_w_dt,
        grad_w_xbc,
        grad_a_log,
        bias_total.reshape(width),
        skip_total.reshape(width),
        dt_gain_total.reshape(rank),
        bc_gain_total.reshape(bc_width),
    )


def solution(mesh):
    return jax.shard_map(
        body,
        mesh=mesh,
        in_specs=(
            P("dp", None, "tensor"),
            P("dp", "tensor", None),
            P("dp", "tensor", None),
            P("dp", None, "tensor"),
            P(None, "tensor"),
            P(None, "tensor"),
            P(None, "tensor"),
            P("tensor"),
            P(None, "tensor"),
            P("tensor"),
            P(),
            P(),
        ),
        out_specs=(
            P("dp", None, "tensor"),
            P("dp", "tensor"),
            P("dp", "tensor"),
            P(None, "tensor"),
            P(None, "tensor"),
            P("tensor"),
            P("tensor"),
            P(),
            P(),
        ),
        check_vma=False,
    )
```

```python
import functools
import math

import jax
import jax.numpy as jnp
from jax import lax
from jax.experimental import pallas as pl
from jax.experimental.pallas import tpu as pltpu
from jax.sharding import PartitionSpec as P

norm_eps = 1e-06
state_floor = 0.25
log2_e = 1.4426950408889634
lane = 128
f32 = jnp.float32
bf16 = jnp.bfloat16
contract_rows = (((0,), (0,)), ((), ()))
contract_cols = (((1,), (1,)), ((), ()))
in_vmem = pl.BlockSpec(memory_space=pltpu.VMEM)


def inverse_norms(proj, rank, state):
    dt_part = proj[:, :rank]
    b_part = proj[:, rank : rank + state]
    c_part = proj[:, rank + state : rank + 2 * state]
    dt_square = jnp.mean(dt_part * dt_part, axis=1, keepdims=True)
    b_square = jnp.mean(b_part * b_part, axis=1, keepdims=True)
    c_square = jnp.mean(c_part * c_part, axis=1, keepdims=True)
    return (
        (dt_part, lax.rsqrt(dt_square + norm_eps)),
        (b_part, lax.rsqrt(jnp.maximum(b_square, state_floor)), b_square),
        (c_part, lax.rsqrt(jnp.maximum(c_square, state_floor)), c_square),
    )


def pack_kernel(dt_in, bc_in, out_ref, dt_ref, bc_ref, arrived):
    rank, bc_width = dt_ref.shape[1], bc_ref.shape[1]
    spare = out_ref.shape[2] - rank - bc_width
    arrivals = [
        pltpu.make_async_copy(dt_in, dt_ref, arrived.at[0]),
        pltpu.make_async_copy(bc_in, bc_ref, arrived.at[1]),
    ]
    for copy in arrivals:
        copy.start()
    for copy in arrivals:
        copy.wait()
    for peer in range(out_ref.shape[0]):
        out_ref[peer, :, :rank] = dt_ref[...]
        out_ref[peer, :, rank : rank + bc_width] = bc_ref[...]
        out_ref[peer, :, rank + bc_width :] = jnp.zeros((dt_ref.shape[0], spare), bf16)


def split_cores(core_ref, whole, keep_ref, send_ref):
    first_core = core_ref[0] == 0
    for pair in range(keep_ref.shape[0]):
        even = whole[32 * pair : 32 * pair + 16]
        odd = whole[32 * pair + 16 : 32 * pair + 32]
        keep_ref[pair] = jnp.where(first_core, even, odd)
        send_ref[pair] = jnp.where(first_core, odd, even).astype(bf16)


def scan_kernel(
    core_ref,
    proj_ref,
    dt_gain_in,
    bc_gain_in,
    w_in,
    bias_in,
    x_in,
    gy_in,
    alog_in,
    skip_in,
    normed_ref,
    w_keep_ref,
    w_send_ref,
    xg_ref,
    misc_ref,
    dt_s,
    gy_s,
    src_s,
    sig_s,
    a2_s,
    low_s,
    bcb_s,
    u_s,
    b_acc,
    c_acc,
    s1_s,
    s2_s,
    dt_gain_ref,
    bc_gain_ref,
    w_ref,
    bias_ref,
    x_ref,
    gy_ref,
    alog_ref,
    skip_ref,
    arrived,
    *,
    scale,
    z_pair,
    forward_lanes=512,
    forward_rows=32,
    backward_lanes=512,
    backward_rows=16,
):
    tokens, width = x_ref.shape
    state = alog_ref.shape[0]
    rank = w_ref.shape[0]
    arrivals = [
        pltpu.make_async_copy(source, held, arrived.at[index])
        for index, (source, held) in enumerate(
            (
                (dt_gain_in, dt_gain_ref),
                (bc_gain_in, bc_gain_ref),
                (w_in, w_ref),
                (bias_in, bias_ref),
                (x_in, x_ref),
                (gy_in, gy_ref),
                (alog_in, alog_ref),
                (skip_in, skip_ref),
            )
        )
    ]
    for copy in arrivals:
        copy.start()
    b_acc[...] = jnp.zeros_like(b_acc)
    c_acc[...] = jnp.zeros_like(c_acc)
    dt_norm, b_norm, c_norm = inverse_norms(proj_ref[...].astype(f32), rank, state)
    arrivals[0].wait()
    arrivals[1].wait()
    low_s[...] = (dt_norm[0] * dt_norm[1] * dt_gain_ref[...]).astype(bf16)
    b_rows = b_norm[0] * b_norm[1] * bc_gain_ref[:, :state]
    c_rows = c_norm[0] * c_norm[1] * bc_gain_ref[:, state:]
    bcb_s[:, :state] = jnp.broadcast_to(b_rows[:, :, None], (tokens, state, lane))
    bcb_s[:, state:] = jnp.broadcast_to(c_rows[:, :, None], (tokens, state, lane))
    arrivals[2].wait()
    arrivals[3].wait()
    pre = jnp.dot(low_s[...], w_ref[...], preferred_element_type=f32) + bias_ref[...]
    small = jnp.exp(-jnp.abs(pre))
    dt_rows = jnp.maximum(pre, 0.0) + jnp.log1p(small)
    sig_s[...] = jnp.where(pre >= 0, 1.0, small) / (1.0 + small)
    for copy in arrivals[4:]:
        copy.wait()
    x_float = x_ref[...].astype(f32)
    gy_float = gy_ref[...].astype(f32)
    dt_s[...] = dt_rows
    gy_s[...] = gy_float
    src_s[...] = dt_rows * x_float
    a_mat = -jnp.exp(alog_ref[...])
    a2_s[...] = a_mat * log2_e
    def widen(part, width):
        return jnp.concatenate([part] * (width // lane), axis=1)

    def fold(part):
        total = part[:, :lane]
        for start in range(lane, part.shape[1], lane):
            total = total + part[:, start : start + lane]
        return total

    def fold_states(part):
        total = part[:8]
        for rep in range(1, state // 8):
            total = total + part[rep * 8 : (rep + 1) * 8]
        return total

    def join_rows(early, late, level):
        mine = (lax.broadcasted_iota(jnp.int32, early.shape, 0) & level) == 0
        kept = jnp.where(mine, early, late)
        moved = jnp.where(mine, late, early)
        return kept + pltpu.roll(moved, 8 - level, 0)

    wide = min(forward_lanes, width)
    for group in range(width // wide):
        cols = slice(group * wide, (group + 1) * wide)

        def forward(block, held):
            a2 = a2_s[:, cols]
            for offset in range(forward_rows):
                t = block * forward_rows + offset
                decayed = jnp.exp2(dt_s[pl.ds(t, 1), cols] * a2) * held
                u_s[pl.ds(t, 1), :, cols] = decayed[None]
                c_acc[pl.ds(t, 1)] += fold(decayed * gy_s[pl.ds(t, 1), cols])[None]
                held = decayed + src_s[pl.ds(t, 1), cols] * widen(bcb_s[t, :state], wide)
            return held

        lax.fori_loop(0, tokens // forward_rows, forward, jnp.zeros((state, wide), f32))

    wide = min(backward_lanes, width)
    for group in range(width // wide):
        cols = slice(group * wide, (group + 1) * wide)

        def backward(step, carry):
            later, a_total = carry
            a2 = a2_s[:, cols]
            for part in range(backward_rows // 8 - 1, -1, -1):
                first_row = tokens - (step + 1) * backward_rows + part * 8
                waiting = {}
                for offset in range(7, -1, -1):
                    t = first_row + offset
                    dt_now = dt_s[pl.ds(t, 1), cols]
                    adjoint = (
                        widen(bcb_s[t, state:], wide) * gy_s[pl.ds(t, 1), cols] + later
                    )
                    through = adjoint * u_s[t, :, cols]
                    first = fold_states(adjoint * widen(bcb_s[t, :state], wide))
                    second = fold_states(through * a2)
                    level = 1
                    while level in waiting:
                        later_first, later_second = waiting.pop(level)
                        first = join_rows(first, later_first, level)
                        second = join_rows(second, later_second, level)
                        level *= 2
                    waiting[level] = (first, second)
                    b_acc[pl.ds(t, 1)] += fold(adjoint * src_s[pl.ds(t, 1), cols])[None]
                    a_total = a_total + dt_now * through
                    later = jnp.exp2(dt_now * a2) * adjoint
                rows = pl.ds(pl.multiple_of(first_row, 8), 8)
                s1_s[rows, cols], s2_s[rows, cols] = waiting[8]
            return later, a_total

        zeros = jnp.zeros((state, wide), f32)
        _, a_total = lax.fori_loop(0, tokens // backward_rows, backward, (zeros, zeros))
        misc_ref[:state, cols] = (scale / log2_e) * (a_total * a2_s[:, cols])

    s1 = s1_s[...]
    xg_ref[...] = dt_s[...] * s1 + skip_ref[...] * gy_s[...]
    dt_grad = x_ref[...].astype(f32) * s1 + s2_s[...] * (1.0 / log2_e)
    pre_float = dt_grad * sig_s[...]
    pre_grad = pre_float.astype(bf16)
    misc_ref[state : state + 1, :] = scale * jnp.sum(pre_float, axis=0, keepdims=True)
    misc_ref[state + 1 : state + 2, :] = scale * jnp.sum(
        gy_s[...] * x_ref[...].astype(f32), axis=0, keepdims=True
    )
    dt_normed = lax.dot_general(
        pre_grad, w_ref[...], contract_cols, preferred_element_type=f32
    ).astype(bf16)
    w_part = scale * lax.dot_general(
        low_s[...], pre_grad, contract_rows, preferred_element_type=f32
    )
    split_cores(core_ref, w_part, w_keep_ref, w_send_ref)
    source_sum = jnp.sum(src_s[...] * gy_s[...], axis=1, keepdims=True)
    b_grad = jnp.sum(b_acc[...], axis=2)
    c_grad = jnp.sum(c_acc[...], axis=2) + b_rows * source_sum
    y_size = normed_ref.shape[0]
    own = tokens // (y_size * z_pair)
    b_grad = b_grad.astype(bf16)
    c_grad = c_grad.astype(bf16)
    bc_width = 2 * state
    for y in range(y_size):
        last = normed_ref.shape[1] - own
        normed_ref[y, last:, z_pair * bc_width :] = jnp.zeros(
            (own, lane - z_pair * bc_width), bf16
        )
        for z in range(z_pair):
            rows = slice((z * y_size + y) * own, (z * y_size + y + 1) * own)
            for piece in range(rank // lane):
                place = (piece * z_pair + z) * own
                normed_ref[y, place : place + own, :] = dt_normed[
                    rows, piece * lane : (piece + 1) * lane
                ]
            start = z * bc_width
            normed_ref[y, last:, start : start + state] = b_grad[rows]
            normed_ref[y, last:, start + state : start + bc_width] = c_grad[rows]


def join_kernel(parts_ref, kept_ref, other_ref, out_ref, both_ref):
    both_ref[...] = (kept_ref[...] + other_ref[...].astype(f32)).astype(bf16)
    total = parts_ref[0].astype(f32)
    for peer in range(1, parts_ref.shape[0]):
        total = total + parts_ref[peer].astype(f32)
    out_ref[...] = total


def norm_kernel(
    y_ref, mine_ref, other_ref, proj_ref, dt_gain_ref, bc_gain_ref, out_ref, pack_s, *, state
):
    rank = dt_gain_ref.shape[1]
    z_pair, _, own, _ = proj_ref.shape
    rows = z_pair * own
    last = mine_ref.shape[0] - own
    bc_width = 2 * state
    packed = mine_ref[...] + other_ref[...]
    pieces = range(rank // lane)
    dt_grad = jnp.concatenate([packed[p * rows : (p + 1) * rows] for p in pieces], axis=1)
    bc_grad = jnp.concatenate(
        [packed[last:, z * bc_width : (z + 1) * bc_width] for z in range(z_pair)], axis=0
    )
    proj = jnp.concatenate([proj_ref[z, y_ref[0]] for z in range(z_pair)], axis=0)
    dt_norm, b_norm, c_norm = inverse_norms(proj.astype(f32), rank, state)
    dt_unit = dt_norm[0] * dt_norm[1]
    dt_cot = dt_grad * dt_gain_ref[...]
    dt_mean = jnp.mean(dt_cot * dt_unit, axis=1, keepdims=True)
    dt_back = dt_norm[1] * (dt_cot - dt_unit * dt_mean)
    for p in pieces:
        pack_s[p * rows : (p + 1) * rows, :] = dt_back[:, p * lane : (p + 1) * lane]
    pack_s[last:, :] = jnp.zeros((own, lane), f32)
    side = z_pair * bc_width
    free = lane - side
    dt_gain_part = jnp.sum(dt_grad * dt_unit, axis=0, keepdims=True)
    for piece in range(rank // free):
        pack_s[last + piece : last + piece + 1, side:] = dt_gain_part[
            :, piece * free : (piece + 1) * free
        ]
    gain_row = last + rank // free
    for index, part in enumerate((b_norm, c_norm)):
        start = index * state
        grad = bc_grad[:, start : start + state]
        unit = part[0] * part[1]
        cot = grad * bc_gain_ref[:, start : start + state]
        mean = jnp.mean(cot * unit, axis=1, keepdims=True)
        inner = jnp.where(part[2] > state_floor, mean, 0.0)
        inner = jnp.where(part[2] == state_floor, 0.5 * mean, inner)
        back = part[1] * (cot - unit * inner)
        for z in range(z_pair):
            place = z * bc_width + start
            pack_s[last:, place : place + state] = back[z * own : (z + 1) * own]
        pack_s[gain_row : gain_row + 1, side + start : side + start + state] = jnp.sum(
            grad * unit, axis=0, keepdims=True
        )
    sent = pack_s[...].astype(bf16)
    for peer in range(out_ref.shape[0]):
        out_ref[peer] = sent


def to_tokens(low_ref, low_s, z_pair, bc_width):
    y_size, packed_rows, _ = low_ref.shape
    own = low_s.shape[0] // (y_size * z_pair)
    pieces = packed_rows // (z_pair * own)
    for y in range(y_size):
        for z in range(z_pair):
            start = (z * y_size + y) * own
            for p in range(pieces):
                place = (p * z_pair + z) * own
                low_s[start : start + own, p * lane : (p + 1) * lane] = low_ref[
                    y, place : place + own, :
                ]
            low_s[start : start + own, pieces * lane : pieces * lane + bc_width] = low_ref[
                y, packed_rows - own :, z * bc_width : (z + 1) * bc_width
            ]


def grad_x_kernel(low_ref, xg_ref, w_xdt_ref, w_xbc_ref, grad_x_ref, low_s, *, z_pair):
    rank = w_xdt_ref.shape[0]
    bc_width = w_xbc_ref.shape[0]
    to_tokens(low_ref, low_s, z_pair, bc_width)
    summed = xg_ref[...] + jnp.dot(
        low_s[:, :rank], w_xdt_ref[...], preferred_element_type=f32
    )
    summed = summed + jnp.dot(
        low_s[:, rank : rank + bc_width], w_xbc_ref[...], preferred_element_type=f32
    )
    grad_x_ref[...] = summed.astype(bf16)


def project_kernel(
    core_ref,
    low_ref,
    x_ref,
    misc_ref,
    keep_ref,
    send_ref,
    out_s,
    all_s,
    low_s,
    *,
    rank,
    bc_width,
    z_pair,
    scale,
):
    width = x_ref.shape[1]
    y_size = low_ref.shape[0]
    own = low_s.shape[0] // (y_size * z_pair)
    to_tokens(low_ref, low_s, z_pair, bc_width)
    dt_low = low_s[:, :rank]
    bc_low = low_s[:, rank : rank + bc_width]
    out_s[:, :width] = scale * lax.dot_general(
        dt_low, x_ref[...], contract_rows, preferred_element_type=f32
    )
    state = bc_width // 2
    all_s[...] = jnp.zeros_like(all_s)
    all_s[: state + 2, :] = misc_ref[: state + 2, :]
    all_s[state + 8 : state + 8 + bc_width, :] = scale * lax.dot_general(
        bc_low, x_ref[...], contract_rows, preferred_element_type=f32
    )
    gains = jnp.zeros((own, lane), f32)
    for y in range(y_size):
        gains = gains + low_ref[y, low_ref.shape[1] - own :, :].astype(f32)
    side = z_pair * bc_width
    free = lane - side
    gains = scale * gains[:, side:]
    gain_row = state + 8 + bc_width
    for piece in range(rank // free):
        all_s[gain_row : gain_row + 1, piece * free : (piece + 1) * free] = gains[
            piece : piece + 1
        ]
    piece = rank // free
    all_s[gain_row : gain_row + 1, rank : rank + bc_width] = gains[piece : piece + 1, :bc_width]
    for piece in range(width // lane):
        out_s[piece * 64 : (piece + 1) * 64, width:] = all_s[
            :, piece * lane : (piece + 1) * lane
        ]
    split_cores(core_ref, out_s, keep_ref, send_ref)


def total_kernel(parts_ref, xdt_ref, dt_ref, own_ref):
    width = xdt_ref.shape[1]
    total = parts_ref[0].astype(f32)
    for peer in range(1, parts_ref.shape[0]):
        total = total + parts_ref[peer].astype(f32)
    xdt_ref[...] = total[:, :width]
    dt_ref[...] = total[:, width : 2 * width]
    for peer in range(own_ref.shape[0]):
        own_ref[peer] = total[:, 2 * width :].astype(bf16)


def spread_kernel(
    parts_ref, xbc_ref, alog_ref, bias_ref, skip_ref, dt_gain_ref, bc_gain_ref, all_s, *, order
):
    state = alog_ref.shape[0]
    bc_width = xbc_ref.shape[0]
    rank = dt_gain_ref.shape[1]
    for block, (peer, place) in enumerate(order):
        row, piece = 16 * (block % 4), lane * (block // 4)
        all_s[row : row + 16, piece : piece + lane] = parts_ref[
            peer, :, place * lane : (place + 1) * lane
        ].astype(f32)
    alog_ref[...] = all_s[:state, :]
    bias_ref[...] = all_s[state : state + 1, :]
    skip_ref[...] = all_s[state + 1 : state + 2, :]
    xbc_ref[...] = all_s[state + 8 : state + 8 + bc_width, :]
    gain_row = state + 8 + bc_width
    dt_gain_ref[...] = all_s[gain_row : gain_row + 1, :rank]
    bc_gain_ref[...] = all_s[gain_row : gain_row + 1, rank : rank + bc_width]


def call(kernel, name, outs, scratch, limit_mib, *args, far=()):
    in_smem = pl.BlockSpec(memory_space=pltpu.SMEM)
    in_hbm = pl.BlockSpec(memory_space=pltpu.HBM)
    return pl.pallas_call(
        kernel,
        out_shape=tuple(
            pltpu.VMEM(out[0], out[1]) if len(out) > 2 else jax.ShapeDtypeStruct(*out)
            for out in outs
        ),
        in_specs=[in_smem if arg.dtype == jnp.int32 else in_vmem for arg in args]
        + [in_hbm] * len(far),
        out_specs=tuple([in_vmem] * len(outs)),
        scratch_shapes=[pltpu.VMEM(shape, dtype) for shape, dtype in scratch]
        + [pltpu.VMEM(arg.shape, arg.dtype) for arg in far]
        + ([pltpu.SemaphoreType.DMA((len(far),))] if far else []),
        compiler_params=pltpu.CompilerParams(vmem_limit_bytes=limit_mib * 2**20),
        name=name,
    )(*args, *[pltpu.with_memory_space_constraint(arg, pltpu.HBM) for arg in far])


def send_to_all(block, axis, groups=None):
    return lax.all_to_all(block, axis, 0, 0, axis_index_groups=groups)


def sum_low(parts):
    return jnp.sum(parts.astype(f32), axis=0).astype(bf16)


def body(
    x_inner, proj_dt, proj_bc, grad_y, w_xdt, w_xbc, w_dt, dt_bias, a_log, d_skip, dt_gain, bc_gain
):
    x_rows = x_inner[0]
    gy_rows = grad_y[0]
    tokens, width = x_rows.shape
    rank = proj_dt.shape[2]
    bc_width = proj_bc.shape[2]
    state = bc_width // 2
    own = proj_dt.shape[1]
    dp = lax.axis_size("dp")
    tensor = lax.axis_size("tensor")
    scale = 1.0 / math.sqrt(dp * tokens)
    bias_row = dt_bias.reshape(1, width)
    skip_row = d_skip.reshape(1, width)
    dt_gain_row = dt_gain.reshape(1, rank)
    bc_gain_row = bc_gain.reshape(1, bc_width)

    columns = rank + lane
    cores, z_size, z_pair = 2, 4, 2
    x_size = dp // (cores * z_size)
    y_size = tensor // z_pair
    per_device = rank // dp
    other_core = [(index, index ^ 1) for index in range(dp)]
    core = (lax.axis_index("dp") % cores).astype(jnp.int32).reshape(1)
    y_index = (lax.axis_index("tensor") % y_size).astype(jnp.int32).reshape(1)
    local = True
    (own_proj,) = call(
        pack_kernel,
        "pack",
        [((tensor, own, columns), bf16, local)],
        [],
        4,
        far=(proj_dt[0], proj_bc[0]),
    )
    own_proj, core, y_index = lax.optimization_barrier((own_proj, core, y_index))
    full_proj = send_to_all(own_proj, "tensor").reshape(tokens, columns)

    z_stride, x_stride = cores, cores * z_size
    along_x = [[x * x_stride + rest for x in range(x_size)] for rest in range(x_stride)]
    along_z = [
        [x * x_stride + z * z_stride + c for z in range(z_size)]
        for x in range(x_size)
        for c in range(cores)
    ]
    along_xc = [
        [x * x_stride + z * z_stride + c for x in range(x_size) for c in range(cores)]
        for z in range(z_size)
    ]
    along_y = [[z * y_size + y for y in range(y_size)] for z in range(z_pair)]

    def swap_cores(sent):
        return lax.ppermute(sent, "dp", other_core)

    def sum_over_x(both):
        blocks = both.reshape((x_size, z_size) + both.shape[1:])
        return sum_low(send_to_all(blocks, "dp", along_x))

    rows = ((tokens, width), f32)
    packed_rows = z_pair * own * (rank // lane) + own
    by_y = (y_size, packed_rows, lane)
    half = (x_size * z_size, per_device)
    normed_part, w_kept, w_sent, xg, misc = call(
        functools.partial(scan_kernel, scale=scale, z_pair=z_pair),
        "scan",
        [
            (by_y, bf16, local),
            (half + (width,), f32, local),
            (half + (width,), bf16),
            ((tokens, width), f32, local),
            ((state + 8, width), f32),
        ],
        [
            rows,
            rows,
            rows,
            rows,
            ((state, width), f32),
            ((tokens, rank), bf16),
            ((tokens, 2 * state, lane), f32),
            ((tokens, state, width), f32),
            ((tokens, state, lane), f32),
            ((tokens, state, lane), f32),
            rows,
            rows,
        ],
        44,
        core,
        full_proj,
        far=(dt_gain_row, bc_gain_row, w_dt, bias_row, x_rows, gy_rows, a_log, skip_row),
    )
    normed_parts = send_to_all(normed_part, "tensor", along_y)
    mine, w_both = call(
        join_kernel,
        "join",
        [((packed_rows, lane), f32, local), (half + (width,), bf16)],
        [],
        16,
        normed_parts,
        w_kept,
        swap_cores(w_sent),
    )
    w_by_x = sum_over_x(w_both)
    other = lax.ppermute(
        mine, "tensor", [(index, (index + y_size) % tensor) for index in range(tensor)]
    )
    other, w_by_x = lax.optimization_barrier((other, w_by_x))
    (own_low,) = call(
        functools.partial(norm_kernel, state=state),
        "norm",
        [(by_y, bf16, local)],
        [((packed_rows, lane), f32)],
        4,
        y_index,
        mine,
        other,
        full_proj.reshape(z_pair, y_size, own, columns),
        dt_gain_row,
        bc_gain_row,
    )
    low = send_to_all(own_low, "tensor", along_y)
    half_row = (half + (width + lane,), bf16)
    kept, sent = call(
        functools.partial(
            project_kernel, rank=rank, bc_width=bc_width, z_pair=z_pair, scale=scale
        ),
        "project",
        [(half_row[0], f32, local), half_row + (local,)],
        [
            ((rank, width + lane), f32),
            ((64, width), f32),
            ((tokens, columns), bf16),
        ],
        16,
        core,
        low,
        x_rows,
        misc,
    )
    (grad_x,) = call(
        functools.partial(grad_x_kernel, z_pair=z_pair),
        "grad_x",
        [((tokens, width), bf16)],
        [((tokens, columns), bf16)],
        16,
        low,
        xg,
        w_xdt,
        w_xbc,
    )
    swapped, grad_x = lax.optimization_barrier((swap_cores(sent), grad_x))
    by_x = sum_over_x((kept + swapped.astype(f32)).astype(bf16))
    by_z = by_x[:, :, width:].transpose(1, 0, 2).reshape(1, per_device, z_size * lane)
    by_z = jnp.broadcast_to(by_z, (z_size, per_device, z_size * lane))
    by_z = jnp.concatenate([by_x[:, :, :width], w_by_x, by_z], axis=2)
    all_parts = send_to_all(by_z, "dp", along_z)
    shared = x_size * cores
    grad_w_xdt, grad_w_dt, own_total = call(
        total_kernel,
        "total",
        [
            ((per_device, width), f32),
            ((per_device, width), f32),
            ((shared, per_device, z_size * lane), bf16, local),
        ],
        [],
        4,
        all_parts,
    )
    totals = send_to_all(own_total, "dp", along_xc)
    order = tuple(
        (x * cores + c, z) for x in range(x_size) for z in range(z_size) for c in range(cores)
    )
    grad_w_xbc, grad_a_log, bias_total, skip_total, dt_gain_total, bc_gain_total = call(
        functools.partial(spread_kernel, order=order),
        "spread",
        [
            ((bc_width, width), f32),
            ((state, width), f32),
            ((1, width), f32),
            ((1, width), f32),
            ((1, rank), f32),
            ((1, bc_width), f32),
        ],
        [((64, width), f32)],
        4,
        totals,
    )
    return (
        grad_x[None],
        grad_w_xdt,
        grad_w_dt,
        grad_w_xbc,
        grad_a_log,
        bias_total.reshape(width),
        skip_total.reshape(width),
        dt_gain_total.reshape(rank),
        bc_gain_total.reshape(bc_width),
    )


def solution(mesh):
    return jax.shard_map(
        body,
        mesh=mesh,
        in_specs=(
            P("dp", None, "tensor"),
            P("dp", "tensor", None),
            P("dp", "tensor", None),
            P("dp", None, "tensor"),
            P(None, "tensor"),
            P(None, "tensor"),
            P(None, "tensor"),
            P("tensor"),
            P(None, "tensor"),
            P("tensor"),
            P(),
            P(),
        ),
        out_specs=(
            P("dp", None, "tensor"),
            P("dp", "tensor"),
            P("dp", "tensor"),
            P(None, "tensor"),
            P(None, "tensor"),
            P("tensor"),
            P("tensor"),
            P(),
            P(),
        ),
        check_vma=False,
    )
```

```python
import functools
import math

import jax
import jax.numpy as jnp
from jax import lax
from jax.experimental import pallas as pl
from jax.experimental.pallas import tpu as pltpu
from jax.sharding import PartitionSpec as P

norm_eps = 1e-06
state_floor = 0.25
log2_e = 1.4426950408889634
lane = 128
f32 = jnp.float32
bf16 = jnp.bfloat16
contract_rows = (((0,), (0,)), ((), ()))
contract_cols = (((1,), (1,)), ((), ()))
in_vmem = pl.BlockSpec(memory_space=pltpu.VMEM)


def inverse_norms(proj, rank, state):
    dt_part = proj[:, :rank]
    b_part = proj[:, rank : rank + state]
    c_part = proj[:, rank + state : rank + 2 * state]
    dt_square = jnp.mean(dt_part * dt_part, axis=1, keepdims=True)
    b_square = jnp.mean(b_part * b_part, axis=1, keepdims=True)
    c_square = jnp.mean(c_part * c_part, axis=1, keepdims=True)
    return (
        (dt_part, lax.rsqrt(dt_square + norm_eps)),
        (b_part, lax.rsqrt(jnp.maximum(b_square, state_floor)), b_square),
        (c_part, lax.rsqrt(jnp.maximum(c_square, state_floor)), c_square),
    )


def pack_kernel(dt_in, bc_in, out_ref, dt_ref, bc_ref, arrived):
    rank, bc_width = dt_ref.shape[1], bc_ref.shape[1]
    spare = out_ref.shape[2] - rank - bc_width
    arrivals = [
        pltpu.make_async_copy(dt_in, dt_ref, arrived.at[0]),
        pltpu.make_async_copy(bc_in, bc_ref, arrived.at[1]),
    ]
    for copy in arrivals:
        copy.start()
    for copy in arrivals:
        copy.wait()
    for peer in range(out_ref.shape[0]):
        out_ref[peer, :, :rank] = dt_ref[...]
        out_ref[peer, :, rank : rank + bc_width] = bc_ref[...]
        out_ref[peer, :, rank + bc_width :] = jnp.zeros((dt_ref.shape[0], spare), bf16)


def split_cores(core_ref, whole, keep_ref, send_ref):
    first_core = core_ref[0] == 0
    for pair in range(keep_ref.shape[0]):
        even = whole[32 * pair : 32 * pair + 16]
        odd = whole[32 * pair + 16 : 32 * pair + 32]
        keep_ref[pair] = jnp.where(first_core, even, odd).astype(keep_ref.dtype)
        send_ref[pair] = jnp.where(first_core, odd, even).astype(bf16)


def scan_kernel(
    core_ref,
    proj_ref,
    dt_gain_in,
    bc_gain_in,
    w_in,
    bias_in,
    x_in,
    gy_in,
    alog_in,
    skip_in,
    normed_ref,
    w_keep_ref,
    w_send_ref,
    xg_ref,
    misc_ref,
    dt_s,
    gy_s,
    src_s,
    sig_s,
    a2_s,
    low_s,
    bcb_s,
    u_s,
    b_acc,
    c_acc,
    s1_s,
    s2_s,
    dt_gain_ref,
    bc_gain_ref,
    w_ref,
    bias_ref,
    x_ref,
    gy_ref,
    alog_ref,
    skip_ref,
    arrived,
    *,
    scale,
    z_pair,
    forward_lanes=512,
    forward_rows=32,
    backward_lanes=512,
    backward_rows=16,
):
    tokens, width = x_ref.shape
    state = alog_ref.shape[0]
    rank = w_ref.shape[0]
    arrivals = [
        pltpu.make_async_copy(source, held, arrived.at[index])
        for index, (source, held) in enumerate(
            (
                (dt_gain_in, dt_gain_ref),
                (bc_gain_in, bc_gain_ref),
                (w_in, w_ref),
                (bias_in, bias_ref),
                (x_in, x_ref),
                (gy_in, gy_ref),
                (alog_in, alog_ref),
                (skip_in, skip_ref),
            )
        )
    ]
    for copy in arrivals:
        copy.start()
    b_acc[...] = jnp.zeros_like(b_acc)
    c_acc[...] = jnp.zeros_like(c_acc)
    dt_norm, b_norm, c_norm = inverse_norms(proj_ref[...].astype(f32), rank, state)
    arrivals[0].wait()
    arrivals[1].wait()
    low_s[...] = (dt_norm[0] * dt_norm[1] * dt_gain_ref[...]).astype(bf16)
    b_rows = b_norm[0] * b_norm[1] * bc_gain_ref[:, :state]
    c_rows = c_norm[0] * c_norm[1] * bc_gain_ref[:, state:]
    bcb_s[:, :state] = jnp.broadcast_to(b_rows[:, :, None], (tokens, state, lane))
    bcb_s[:, state:] = jnp.broadcast_to(c_rows[:, :, None], (tokens, state, lane))
    arrivals[2].wait()
    arrivals[3].wait()
    pre = jnp.dot(low_s[...], w_ref[...], preferred_element_type=f32) + bias_ref[...]
    small = jnp.exp(-jnp.abs(pre))
    dt_rows = jnp.maximum(pre, 0.0) + jnp.log1p(small)
    sig_s[...] = jnp.where(pre >= 0, 1.0, small) / (1.0 + small)
    for copy in arrivals[4:]:
        copy.wait()
    x_float = x_ref[...].astype(f32)
    gy_float = gy_ref[...].astype(f32)
    dt_s[...] = dt_rows
    gy_s[...] = gy_float
    src_s[...] = dt_rows * x_float
    a_mat = -jnp.exp(alog_ref[...])
    a2_s[...] = a_mat * log2_e
    def widen(part, width):
        return jnp.concatenate([part] * (width // lane), axis=1)

    def fold(part):
        total = part[:, :lane]
        for start in range(lane, part.shape[1], lane):
            total = total + part[:, start : start + lane]
        return total

    def fold_states(part):
        total = part[:8]
        for rep in range(1, state // 8):
            total = total + part[rep * 8 : (rep + 1) * 8]
        return total

    def join_rows(early, late, level):
        mine = (lax.broadcasted_iota(jnp.int32, early.shape, 0) & level) == 0
        kept = jnp.where(mine, early, late)
        moved = jnp.where(mine, late, early)
        return kept + pltpu.roll(moved, 8 - level, 0)

    wide = min(forward_lanes, width)
    for group in range(width // wide):
        cols = slice(group * wide, (group + 1) * wide)

        def forward(block, held):
            a2 = a2_s[:, cols]
            for offset in range(forward_rows):
                t = block * forward_rows + offset
                decayed = jnp.exp2(dt_s[pl.ds(t, 1), cols] * a2) * held
                u_s[pl.ds(t, 1), :, cols] = decayed[None]
                c_acc[pl.ds(t, 1)] += fold(decayed * gy_s[pl.ds(t, 1), cols])[None]
                held = decayed + src_s[pl.ds(t, 1), cols] * widen(bcb_s[t, :state], wide)
            return held

        lax.fori_loop(0, tokens // forward_rows, forward, jnp.zeros((state, wide), f32))

    wide = min(backward_lanes, width)
    for group in range(width // wide):
        cols = slice(group * wide, (group + 1) * wide)

        def backward(step, carry):
            later, a_total = carry
            a2 = a2_s[:, cols]
            for part in range(backward_rows // 8 - 1, -1, -1):
                first_row = tokens - (step + 1) * backward_rows + part * 8
                waiting = {}
                for offset in range(7, -1, -1):
                    t = first_row + offset
                    dt_now = dt_s[pl.ds(t, 1), cols]
                    adjoint = (
                        widen(bcb_s[t, state:], wide) * gy_s[pl.ds(t, 1), cols] + later
                    )
                    through = adjoint * u_s[t, :, cols]
                    first = fold_states(adjoint * widen(bcb_s[t, :state], wide))
                    second = fold_states(through * a2)
                    level = 1
                    while level in waiting:
                        later_first, later_second = waiting.pop(level)
                        first = join_rows(first, later_first, level)
                        second = join_rows(second, later_second, level)
                        level *= 2
                    waiting[level] = (first, second)
                    b_acc[pl.ds(t, 1)] += fold(adjoint * src_s[pl.ds(t, 1), cols])[None]
                    a_total = a_total + dt_now * through
                    later = jnp.exp2(dt_now * a2) * adjoint
                rows = pl.ds(pl.multiple_of(first_row, 8), 8)
                s1_s[rows, cols], s2_s[rows, cols] = waiting[8]
            return later, a_total

        zeros = jnp.zeros((state, wide), f32)
        _, a_total = lax.fori_loop(0, tokens // backward_rows, backward, (zeros, zeros))
        misc_ref[:state, cols] = (scale / log2_e) * (a_total * a2_s[:, cols])

    s1 = s1_s[...]
    xg_ref[...] = dt_s[...] * s1 + skip_ref[...] * gy_s[...]
    dt_grad = x_ref[...].astype(f32) * s1 + s2_s[...] * (1.0 / log2_e)
    pre_float = dt_grad * sig_s[...]
    pre_grad = pre_float.astype(bf16)
    misc_ref[state : state + 1, :] = scale * jnp.sum(pre_float, axis=0, keepdims=True)
    misc_ref[state + 1 : state + 2, :] = scale * jnp.sum(
        gy_s[...] * x_ref[...].astype(f32), axis=0, keepdims=True
    )
    dt_normed = lax.dot_general(
        pre_grad, w_ref[...], contract_cols, preferred_element_type=f32
    ).astype(bf16)
    w_part = scale * lax.dot_general(
        low_s[...], pre_grad, contract_rows, preferred_element_type=f32
    )
    split_cores(core_ref, w_part, w_keep_ref, w_send_ref)
    source_sum = jnp.sum(src_s[...] * gy_s[...], axis=1, keepdims=True)
    b_grad = jnp.sum(b_acc[...], axis=2)
    c_grad = jnp.sum(c_acc[...], axis=2) + b_rows * source_sum
    y_size = normed_ref.shape[0]
    own = tokens // (y_size * z_pair)
    b_grad = b_grad.astype(bf16)
    c_grad = c_grad.astype(bf16)
    bc_width = 2 * state
    for y in range(y_size):
        last = normed_ref.shape[1] - own
        normed_ref[y, last:, z_pair * bc_width :] = jnp.zeros(
            (own, lane - z_pair * bc_width), bf16
        )
        for z in range(z_pair):
            rows = slice((z * y_size + y) * own, (z * y_size + y + 1) * own)
            for piece in range(rank // lane):
                place = (piece * z_pair + z) * own
                normed_ref[y, place : place + own, :] = dt_normed[
                    rows, piece * lane : (piece + 1) * lane
                ]
            start = z * bc_width
            normed_ref[y, last:, start : start + state] = b_grad[rows]
            normed_ref[y, last:, start + state : start + bc_width] = c_grad[rows]


def join_kernel(parts_ref, kept_ref, other_ref, out_ref, both_ref):
    both_ref[...] = (kept_ref[...].astype(f32) + other_ref[...].astype(f32)).astype(bf16)
    total = parts_ref[0].astype(f32)
    for peer in range(1, parts_ref.shape[0]):
        total = total + parts_ref[peer].astype(f32)
    out_ref[...] = total


def norm_kernel(
    y_ref, mine_ref, other_ref, proj_ref, dt_gain_ref, bc_gain_ref, out_ref, pack_s, *, state
):
    rank = dt_gain_ref.shape[1]
    z_pair, _, own, _ = proj_ref.shape
    rows = z_pair * own
    last = mine_ref.shape[0] - own
    bc_width = 2 * state
    packed = mine_ref[...] + other_ref[...]
    pieces = range(rank // lane)
    dt_grad = jnp.concatenate([packed[p * rows : (p + 1) * rows] for p in pieces], axis=1)
    bc_grad = jnp.concatenate(
        [packed[last:, z * bc_width : (z + 1) * bc_width] for z in range(z_pair)], axis=0
    )
    proj = jnp.concatenate([proj_ref[z, y_ref[0]] for z in range(z_pair)], axis=0)
    dt_norm, b_norm, c_norm = inverse_norms(proj.astype(f32), rank, state)
    dt_unit = dt_norm[0] * dt_norm[1]
    dt_cot = dt_grad * dt_gain_ref[...]
    dt_mean = jnp.mean(dt_cot * dt_unit, axis=1, keepdims=True)
    dt_back = dt_norm[1] * (dt_cot - dt_unit * dt_mean)
    for p in pieces:
        pack_s[p * rows : (p + 1) * rows, :] = dt_back[:, p * lane : (p + 1) * lane]
    pack_s[last:, :] = jnp.zeros((own, lane), f32)
    side = z_pair * bc_width
    free = lane - side
    dt_gain_part = jnp.sum(dt_grad * dt_unit, axis=0, keepdims=True)
    for piece in range(rank // free):
        pack_s[last + piece : last + piece + 1, side:] = dt_gain_part[
            :, piece * free : (piece + 1) * free
        ]
    gain_row = last + rank // free
    for index, part in enumerate((b_norm, c_norm)):
        start = index * state
        grad = bc_grad[:, start : start + state]
        unit = part[0] * part[1]
        cot = grad * bc_gain_ref[:, start : start + state]
        mean = jnp.mean(cot * unit, axis=1, keepdims=True)
        inner = jnp.where(part[2] > state_floor, mean, 0.0)
        inner = jnp.where(part[2] == state_floor, 0.5 * mean, inner)
        back = part[1] * (cot - unit * inner)
        for z in range(z_pair):
            place = z * bc_width + start
            pack_s[last:, place : place + state] = back[z * own : (z + 1) * own]
        pack_s[gain_row : gain_row + 1, side + start : side + start + state] = jnp.sum(
            grad * unit, axis=0, keepdims=True
        )
    sent = pack_s[...].astype(bf16)
    for peer in range(out_ref.shape[0]):
        out_ref[peer] = sent


def to_tokens(low_ref, low_s, z_pair, bc_width):
    y_size, packed_rows, _ = low_ref.shape
    own = low_s.shape[0] // (y_size * z_pair)
    pieces = packed_rows // (z_pair * own)
    for y in range(y_size):
        for z in range(z_pair):
            start = (z * y_size + y) * own
            for p in range(pieces):
                place = (p * z_pair + z) * own
                low_s[start : start + own, p * lane : (p + 1) * lane] = low_ref[
                    y, place : place + own, :
                ]
            low_s[start : start + own, pieces * lane : pieces * lane + bc_width] = low_ref[
                y, packed_rows - own :, z * bc_width : (z + 1) * bc_width
            ]


def grad_x_kernel(low_ref, xg_ref, w_xdt_ref, w_xbc_ref, grad_x_ref, low_s, *, z_pair):
    rank = w_xdt_ref.shape[0]
    bc_width = w_xbc_ref.shape[0]
    to_tokens(low_ref, low_s, z_pair, bc_width)
    summed = xg_ref[...] + jnp.dot(
        low_s[:, :rank], w_xdt_ref[...], preferred_element_type=f32
    )
    summed = summed + jnp.dot(
        low_s[:, rank : rank + bc_width], w_xbc_ref[...], preferred_element_type=f32
    )
    grad_x_ref[...] = summed.astype(bf16)


def project_kernel(
    core_ref,
    low_ref,
    x_ref,
    misc_ref,
    keep_ref,
    send_ref,
    out_s,
    all_s,
    low_s,
    *,
    rank,
    bc_width,
    z_pair,
    scale,
):
    width = x_ref.shape[1]
    y_size = low_ref.shape[0]
    own = low_s.shape[0] // (y_size * z_pair)
    to_tokens(low_ref, low_s, z_pair, bc_width)
    dt_low = low_s[:, :rank]
    bc_low = low_s[:, rank : rank + bc_width]
    out_s[:, :width] = scale * lax.dot_general(
        dt_low, x_ref[...], contract_rows, preferred_element_type=f32
    )
    state = bc_width // 2
    all_s[...] = jnp.zeros_like(all_s)
    all_s[: state + 2, :] = misc_ref[: state + 2, :]
    all_s[state + 8 : state + 8 + bc_width, :] = scale * lax.dot_general(
        bc_low, x_ref[...], contract_rows, preferred_element_type=f32
    )
    gains = jnp.zeros((own, lane), f32)
    for y in range(y_size):
        gains = gains + low_ref[y, low_ref.shape[1] - own :, :].astype(f32)
    side = z_pair * bc_width
    free = lane - side
    gains = scale * gains[:, side:]
    gain_row = state + 8 + bc_width
    for piece in range(rank // free):
        all_s[gain_row : gain_row + 1, piece * free : (piece + 1) * free] = gains[
            piece : piece + 1
        ]
    piece = rank // free
    all_s[gain_row : gain_row + 1, rank : rank + bc_width] = gains[piece : piece + 1, :bc_width]
    for piece in range(width // lane):
        out_s[piece * 64 : (piece + 1) * 64, width:] = all_s[
            :, piece * lane : (piece + 1) * lane
        ]
    split_cores(core_ref, out_s, keep_ref, send_ref)


def total_kernel(parts_ref, xdt_ref, dt_ref, own_ref):
    width = xdt_ref.shape[1]
    total = parts_ref[0].astype(f32)
    for peer in range(1, parts_ref.shape[0]):
        total = total + parts_ref[peer].astype(f32)
    xdt_ref[...] = total[:, :width]
    dt_ref[...] = total[:, width : 2 * width]
    for peer in range(own_ref.shape[0]):
        own_ref[peer] = total[:, 2 * width :].astype(bf16)


def spread_kernel(
    parts_ref, xbc_ref, alog_ref, bias_ref, skip_ref, dt_gain_ref, bc_gain_ref, all_s, *, order
):
    state = alog_ref.shape[0]
    bc_width = xbc_ref.shape[0]
    rank = dt_gain_ref.shape[1]
    for block, (peer, place) in enumerate(order):
        row, piece = 16 * (block % 4), lane * (block // 4)
        all_s[row : row + 16, piece : piece + lane] = parts_ref[
            peer, :, place * lane : (place + 1) * lane
        ].astype(f32)
    alog_ref[...] = all_s[:state, :]
    bias_ref[...] = all_s[state : state + 1, :]
    skip_ref[...] = all_s[state + 1 : state + 2, :]
    xbc_ref[...] = all_s[state + 8 : state + 8 + bc_width, :]
    gain_row = state + 8 + bc_width
    dt_gain_ref[...] = all_s[gain_row : gain_row + 1, :rank]
    bc_gain_ref[...] = all_s[gain_row : gain_row + 1, rank : rank + bc_width]


def call(kernel, name, outs, scratch, limit_mib, *args, far=()):
    in_smem = pl.BlockSpec(memory_space=pltpu.SMEM)
    in_hbm = pl.BlockSpec(memory_space=pltpu.HBM)
    return pl.pallas_call(
        kernel,
        out_shape=tuple(
            pltpu.VMEM(out[0], out[1]) if len(out) > 2 else jax.ShapeDtypeStruct(*out)
            for out in outs
        ),
        in_specs=[in_smem if arg.dtype == jnp.int32 else in_vmem for arg in args]
        + [in_hbm] * len(far),
        out_specs=tuple([in_vmem] * len(outs)),
        scratch_shapes=[pltpu.VMEM(shape, dtype) for shape, dtype in scratch]
        + [pltpu.VMEM(arg.shape, arg.dtype) for arg in far]
        + ([pltpu.SemaphoreType.DMA((len(far),))] if far else []),
        compiler_params=pltpu.CompilerParams(vmem_limit_bytes=limit_mib * 2**20),
        name=name,
    )(*args, *[pltpu.with_memory_space_constraint(arg, pltpu.HBM) for arg in far])


def send_to_all(block, axis, groups=None):
    return lax.all_to_all(block, axis, 0, 0, axis_index_groups=groups)


def sum_low(parts):
    return jnp.sum(parts.astype(f32), axis=0).astype(bf16)


def body(
    x_inner, proj_dt, proj_bc, grad_y, w_xdt, w_xbc, w_dt, dt_bias, a_log, d_skip, dt_gain, bc_gain
):
    x_rows = x_inner[0]
    gy_rows = grad_y[0]
    tokens, width = x_rows.shape
    rank = proj_dt.shape[2]
    bc_width = proj_bc.shape[2]
    state = bc_width // 2
    own = proj_dt.shape[1]
    dp = lax.axis_size("dp")
    tensor = lax.axis_size("tensor")
    scale = 1.0 / math.sqrt(dp * tokens)
    bias_row = dt_bias.reshape(1, width)
    skip_row = d_skip.reshape(1, width)
    dt_gain_row = dt_gain.reshape(1, rank)
    bc_gain_row = bc_gain.reshape(1, bc_width)

    columns = rank + lane
    cores, z_size, z_pair = 2, 4, 2
    x_size = dp // (cores * z_size)
    y_size = tensor // z_pair
    per_device = rank // dp
    other_core = [(index, index ^ 1) for index in range(dp)]
    core = (lax.axis_index("dp") % cores).astype(jnp.int32).reshape(1)
    y_index = (lax.axis_index("tensor") % y_size).astype(jnp.int32).reshape(1)
    local = True
    (own_proj,) = call(
        pack_kernel,
        "pack",
        [((tensor, own, columns), bf16, local)],
        [],
        4,
        far=(proj_dt[0], proj_bc[0]),
    )
    own_proj, core, y_index = lax.optimization_barrier((own_proj, core, y_index))
    full_proj = send_to_all(own_proj, "tensor").reshape(tokens, columns)

    z_stride, x_stride = cores, cores * z_size
    along_x = [[x * x_stride + rest for x in range(x_size)] for rest in range(x_stride)]
    along_z = [
        [x * x_stride + z * z_stride + c for z in range(z_size)]
        for x in range(x_size)
        for c in range(cores)
    ]
    along_xc = [
        [x * x_stride + z * z_stride + c for x in range(x_size) for c in range(cores)]
        for z in range(z_size)
    ]
    along_y = [[z * y_size + y for y in range(y_size)] for z in range(z_pair)]

    def swap_cores(sent):
        return lax.ppermute(sent, "dp", other_core)

    def sum_over_x(both):
        blocks = both.reshape((x_size, z_size) + both.shape[1:])
        return sum_low(send_to_all(blocks, "dp", along_x))

    rows = ((tokens, width), f32)
    packed_rows = z_pair * own * (rank // lane) + own
    by_y = (y_size, packed_rows, lane)
    half = (x_size * z_size, per_device)
    normed_part, w_kept, w_sent, xg, misc = call(
        functools.partial(scan_kernel, scale=scale, z_pair=z_pair),
        "scan",
        [
            (by_y, bf16, local),
            (half + (width,), bf16, local),
            (half + (width,), bf16, local),
            ((tokens, width), f32, local),
            ((state + 8, width), f32, local),
        ],
        [
            rows,
            rows,
            rows,
            rows,
            ((state, width), f32),
            ((tokens, rank), bf16),
            ((tokens, 2 * state, lane), f32),
            ((tokens, state, width), f32),
            ((tokens, state, lane), f32),
            ((tokens, state, lane), f32),
            rows,
            rows,
        ],
        42,
        core,
        full_proj,
        far=(dt_gain_row, bc_gain_row, w_dt, bias_row, x_rows, gy_rows, a_log, skip_row),
    )
    normed_parts = send_to_all(normed_part, "tensor", along_y)
    mine, w_both = call(
        join_kernel,
        "join",
        [((packed_rows, lane), f32, local), (half + (width,), bf16)],
        [],
        16,
        normed_parts,
        w_kept,
        swap_cores(w_sent),
    )
    w_by_x = sum_over_x(w_both)
    other = lax.ppermute(
        mine, "tensor", [(index, (index + y_size) % tensor) for index in range(tensor)]
    )
    other, w_by_x = lax.optimization_barrier((other, w_by_x))
    (own_low,) = call(
        functools.partial(norm_kernel, state=state),
        "norm",
        [(by_y, bf16, local)],
        [((packed_rows, lane), f32)],
        4,
        y_index,
        mine,
        other,
        full_proj.reshape(z_pair, y_size, own, columns),
        dt_gain_row,
        bc_gain_row,
    )
    low = send_to_all(own_low, "tensor", along_y)
    half_row = (half + (width + lane,), bf16)
    kept, sent = call(
        functools.partial(
            project_kernel, rank=rank, bc_width=bc_width, z_pair=z_pair, scale=scale
        ),
        "project",
        [(half_row[0], f32, local), half_row + (local,)],
        [
            ((rank, width + lane), f32),
            ((64, width), f32),
            ((tokens, columns), bf16),
        ],
        16,
        core,
        low,
        x_rows,
        misc,
    )
    (grad_x,) = call(
        functools.partial(grad_x_kernel, z_pair=z_pair),
        "grad_x",
        [((tokens, width), bf16)],
        [((tokens, columns), bf16)],
        16,
        low,
        xg,
        w_xdt,
        w_xbc,
    )
    swapped, grad_x = lax.optimization_barrier((swap_cores(sent), grad_x))
    by_x = sum_over_x((kept + swapped.astype(f32)).astype(bf16))
    by_z = by_x[:, :, width:].transpose(1, 0, 2).reshape(1, per_device, z_size * lane)
    by_z = jnp.broadcast_to(by_z, (z_size, per_device, z_size * lane))
    by_z = jnp.concatenate([by_x[:, :, :width], w_by_x, by_z], axis=2)
    all_parts = send_to_all(by_z, "dp", along_z)
    shared = x_size * cores
    grad_w_xdt, grad_w_dt, own_total = call(
        total_kernel,
        "total",
        [
            ((per_device, width), f32),
            ((per_device, width), f32),
            ((shared, per_device, z_size * lane), bf16, local),
        ],
        [],
        4,
        all_parts,
    )
    totals = send_to_all(own_total, "dp", along_xc)
    order = tuple(
        (x * cores + c, z) for x in range(x_size) for z in range(z_size) for c in range(cores)
    )
    grad_w_xbc, grad_a_log, bias_total, skip_total, dt_gain_total, bc_gain_total = call(
        functools.partial(spread_kernel, order=order),
        "spread",
        [
            ((bc_width, width), f32),
            ((state, width), f32),
            ((1, width), f32),
            ((1, width), f32),
            ((1, rank), f32),
            ((1, bc_width), f32),
        ],
        [((64, width), f32)],
        4,
        totals,
    )
    return (
        grad_x[None],
        grad_w_xdt,
        grad_w_dt,
        grad_w_xbc,
        grad_a_log,
        bias_total.reshape(width),
        skip_total.reshape(width),
        dt_gain_total.reshape(rank),
        bc_gain_total.reshape(bc_width),
    )


def solution(mesh):
    return jax.shard_map(
        body,
        mesh=mesh,
        in_specs=(
            P("dp", None, "tensor"),
            P("dp", "tensor", None),
            P("dp", "tensor", None),
            P("dp", None, "tensor"),
            P(None, "tensor"),
            P(None, "tensor"),
            P(None, "tensor"),
            P("tensor"),
            P(None, "tensor"),
            P("tensor"),
            P(),
            P(),
        ),
        out_specs=(
            P("dp", None, "tensor"),
            P("dp", "tensor"),
            P("dp", "tensor"),
            P(None, "tensor"),
            P(None, "tensor"),
            P("tensor"),
            P("tensor"),
            P(),
            P(),
        ),
        check_vma=False,
    )
```

```python
import functools
import math

import jax
import jax.numpy as jnp
from jax import lax
from jax.experimental import pallas as pl
from jax.experimental.pallas import tpu as pltpu
from jax.sharding import PartitionSpec as P

norm_eps = 1e-06
state_floor = 0.25
log2_e = 1.4426950408889634
lane = 128
f32 = jnp.float32
bf16 = jnp.bfloat16
contract_rows = (((0,), (0,)), ((), ()))
contract_cols = (((1,), (1,)), ((), ()))
in_vmem = pl.BlockSpec(memory_space=pltpu.VMEM)


def inverse_norms(proj, rank, state):
    dt_part = proj[:, :rank]
    b_part = proj[:, rank : rank + state]
    c_part = proj[:, rank + state : rank + 2 * state]
    dt_square = jnp.mean(dt_part * dt_part, axis=1, keepdims=True)
    b_square = jnp.mean(b_part * b_part, axis=1, keepdims=True)
    c_square = jnp.mean(c_part * c_part, axis=1, keepdims=True)
    return (
        (dt_part, lax.rsqrt(dt_square + norm_eps)),
        (b_part, lax.rsqrt(jnp.maximum(b_square, state_floor)), b_square),
        (c_part, lax.rsqrt(jnp.maximum(c_square, state_floor)), c_square),
    )


def pack_kernel(dt_in, bc_in, out_ref, dt_ref, bc_ref, arrived):
    rank, bc_width = dt_ref.shape[1], bc_ref.shape[1]
    spare = out_ref.shape[2] - rank - bc_width
    arrivals = [
        pltpu.make_async_copy(dt_in, dt_ref, arrived.at[0]),
        pltpu.make_async_copy(bc_in, bc_ref, arrived.at[1]),
    ]
    for copy in arrivals:
        copy.start()
    for copy in arrivals:
        copy.wait()
    for peer in range(out_ref.shape[0]):
        out_ref[peer, :, :rank] = dt_ref[...]
        out_ref[peer, :, rank : rank + bc_width] = bc_ref[...]
        out_ref[peer, :, rank + bc_width :] = jnp.zeros((dt_ref.shape[0], spare), bf16)


def split_cores(core_ref, whole, keep_ref, send_ref):
    first_core = core_ref[0] == 0
    for pair in range(keep_ref.shape[0]):
        even = whole[32 * pair : 32 * pair + 16]
        odd = whole[32 * pair + 16 : 32 * pair + 32]
        keep_ref[pair] = jnp.where(first_core, even, odd).astype(keep_ref.dtype)
        send_ref[pair] = jnp.where(first_core, odd, even).astype(bf16)


def scan_kernel(
    core_ref,
    proj_ref,
    dt_gain_in,
    bc_gain_in,
    w_in,
    bias_in,
    x_in,
    gy_in,
    alog_in,
    skip_in,
    normed_ref,
    w_keep_ref,
    w_send_ref,
    xg_ref,
    misc_ref,
    dt_s,
    gy_s,
    src_s,
    sig_s,
    a2_s,
    low_s,
    bcb_s,
    u_s,
    b_acc,
    c_acc,
    s1_s,
    s2_s,
    dt_gain_ref,
    bc_gain_ref,
    w_ref,
    bias_ref,
    x_ref,
    gy_ref,
    alog_ref,
    skip_ref,
    arrived,
    *,
    scale,
    z_pair,
    forward_lanes=512,
    forward_rows=32,
    backward_lanes=512,
    backward_rows=16,
):
    tokens, width = x_ref.shape
    state = alog_ref.shape[0]
    rank = w_ref.shape[0]
    arrivals = [
        pltpu.make_async_copy(source, held, arrived.at[index])
        for index, (source, held) in enumerate(
            (
                (dt_gain_in, dt_gain_ref),
                (bc_gain_in, bc_gain_ref),
                (w_in, w_ref),
                (bias_in, bias_ref),
                (x_in, x_ref),
                (gy_in, gy_ref),
                (alog_in, alog_ref),
                (skip_in, skip_ref),
            )
        )
    ]
    for copy in arrivals:
        copy.start()
    b_acc[...] = jnp.zeros_like(b_acc)
    c_acc[...] = jnp.zeros_like(c_acc)
    dt_norm, b_norm, c_norm = inverse_norms(proj_ref[...].astype(f32), rank, state)
    arrivals[0].wait()
    arrivals[1].wait()
    low_s[...] = (dt_norm[0] * dt_norm[1] * dt_gain_ref[...]).astype(bf16)
    b_rows = b_norm[0] * b_norm[1] * bc_gain_ref[:, :state]
    c_rows = c_norm[0] * c_norm[1] * bc_gain_ref[:, state:]
    bcb_s[:, :state] = jnp.broadcast_to(b_rows[:, :, None], (tokens, state, lane))
    bcb_s[:, state:] = jnp.broadcast_to(c_rows[:, :, None], (tokens, state, lane))
    arrivals[2].wait()
    arrivals[3].wait()
    pre = jnp.dot(low_s[...], w_ref[...], preferred_element_type=f32) + bias_ref[...]
    small = jnp.exp(-jnp.abs(pre))
    dt_rows = jnp.maximum(pre, 0.0) + jnp.log1p(small)
    sig_s[...] = jnp.where(pre >= 0, 1.0, small) / (1.0 + small)
    for copy in arrivals[4:]:
        copy.wait()
    x_float = x_ref[...].astype(f32)
    gy_float = gy_ref[...].astype(f32)
    dt_s[...] = dt_rows
    gy_s[...] = gy_float
    src_s[...] = dt_rows * x_float
    a_mat = -jnp.exp(alog_ref[...])
    a2_s[...] = a_mat * log2_e
    def widen(part, width):
        return jnp.concatenate([part] * (width // lane), axis=1)

    def fold(part):
        total = part[:, :lane]
        for start in range(lane, part.shape[1], lane):
            total = total + part[:, start : start + lane]
        return total

    def fold_states(part):
        total = part[:8]
        for rep in range(1, state // 8):
            total = total + part[rep * 8 : (rep + 1) * 8]
        return total

    def join_rows(early, late, level):
        mine = (lax.broadcasted_iota(jnp.int32, early.shape, 0) & level) == 0
        kept = jnp.where(mine, early, late)
        moved = jnp.where(mine, late, early)
        return kept + pltpu.roll(moved, 8 - level, 0)

    wide = min(forward_lanes, width)
    for group in range(width // wide):
        cols = slice(group * wide, (group + 1) * wide)

        def forward(block, held):
            a2 = a2_s[:, cols]
            for offset in range(forward_rows):
                t = block * forward_rows + offset
                decayed = jnp.exp2(dt_s[pl.ds(t, 1), cols] * a2) * held
                u_s[pl.ds(t, 1), :, cols] = decayed[None]
                c_acc[pl.ds(t, 1)] += fold(decayed * gy_s[pl.ds(t, 1), cols])[None]
                held = decayed + src_s[pl.ds(t, 1), cols] * widen(bcb_s[t, :state], wide)
            return held

        lax.fori_loop(0, tokens // forward_rows, forward, jnp.zeros((state, wide), f32))

    wide = min(backward_lanes, width)
    for group in range(width // wide):
        cols = slice(group * wide, (group + 1) * wide)

        def backward(step, carry):
            later, a_total = carry
            a2 = a2_s[:, cols]
            for part in range(backward_rows // 8 - 1, -1, -1):
                first_row = tokens - (step + 1) * backward_rows + part * 8
                waiting = {}
                for offset in range(7, -1, -1):
                    t = first_row + offset
                    dt_now = dt_s[pl.ds(t, 1), cols]
                    adjoint = (
                        widen(bcb_s[t, state:], wide) * gy_s[pl.ds(t, 1), cols] + later
                    )
                    through = adjoint * u_s[t, :, cols]
                    first = fold_states(adjoint * widen(bcb_s[t, :state], wide))
                    second = fold_states(through * a2)
                    level = 1
                    while level in waiting:
                        later_first, later_second = waiting.pop(level)
                        first = join_rows(first, later_first, level)
                        second = join_rows(second, later_second, level)
                        level *= 2
                    waiting[level] = (first, second)
                    b_acc[pl.ds(t, 1)] += fold(adjoint * src_s[pl.ds(t, 1), cols])[None]
                    a_total = a_total + dt_now * through
                    later = jnp.exp2(dt_now * a2) * adjoint
                rows = pl.ds(pl.multiple_of(first_row, 8), 8)
                s1_s[rows, cols], s2_s[rows, cols] = waiting[8]
            return later, a_total

        zeros = jnp.zeros((state, wide), f32)
        _, a_total = lax.fori_loop(0, tokens // backward_rows, backward, (zeros, zeros))
        misc_ref[:state, cols] = (scale / log2_e) * (a_total * a2_s[:, cols])

    s1 = s1_s[...]
    xg_ref[...] = dt_s[...] * s1 + skip_ref[...] * gy_s[...]
    dt_grad = x_ref[...].astype(f32) * s1 + s2_s[...] * (1.0 / log2_e)
    pre_float = dt_grad * sig_s[...]
    pre_grad = pre_float.astype(bf16)
    misc_ref[state : state + 1, :] = scale * jnp.sum(pre_float, axis=0, keepdims=True)
    misc_ref[state + 1 : state + 2, :] = scale * jnp.sum(
        gy_s[...] * x_ref[...].astype(f32), axis=0, keepdims=True
    )
    dt_normed = lax.dot_general(
        pre_grad, w_ref[...], contract_cols, preferred_element_type=f32
    ).astype(bf16)
    w_part = scale * lax.dot_general(
        low_s[...], pre_grad, contract_rows, preferred_element_type=f32
    )
    split_cores(core_ref, w_part, w_keep_ref, w_send_ref)
    source_sum = jnp.sum(src_s[...] * gy_s[...], axis=1, keepdims=True)
    b_grad = jnp.sum(b_acc[...], axis=2)
    c_grad = jnp.sum(c_acc[...], axis=2) + b_rows * source_sum
    y_size = normed_ref.shape[0]
    own = tokens // (y_size * z_pair)
    b_grad = b_grad.astype(bf16)
    c_grad = c_grad.astype(bf16)
    bc_width = 2 * state
    for y in range(y_size):
        last = normed_ref.shape[1] - own
        normed_ref[y, last:, z_pair * bc_width :] = jnp.zeros(
            (own, lane - z_pair * bc_width), bf16
        )
        for z in range(z_pair):
            rows = slice((z * y_size + y) * own, (z * y_size + y + 1) * own)
            for piece in range(rank // lane):
                place = (piece * z_pair + z) * own
                normed_ref[y, place : place + own, :] = dt_normed[
                    rows, piece * lane : (piece + 1) * lane
                ]
            start = z * bc_width
            normed_ref[y, last:, start : start + state] = b_grad[rows]
            normed_ref[y, last:, start + state : start + bc_width] = c_grad[rows]


def join_kernel(parts_ref, kept_ref, other_ref, out_ref, both_ref):
    both_ref[...] = (kept_ref[...].astype(f32) + other_ref[...].astype(f32)).astype(bf16)
    total = parts_ref[0].astype(f32)
    for peer in range(1, parts_ref.shape[0]):
        total = total + parts_ref[peer].astype(f32)
    out_ref[...] = total


def norm_kernel(
    y_ref, mine_ref, other_ref, proj_ref, dt_gain_ref, bc_gain_ref, out_ref, pack_s, *, state
):
    rank = dt_gain_ref.shape[1]
    z_pair, _, own, _ = proj_ref.shape
    rows = z_pair * own
    last = mine_ref.shape[0] - own
    bc_width = 2 * state
    packed = mine_ref[...] + other_ref[...]
    pieces = range(rank // lane)
    dt_grad = jnp.concatenate([packed[p * rows : (p + 1) * rows] for p in pieces], axis=1)
    bc_grad = jnp.concatenate(
        [packed[last:, z * bc_width : (z + 1) * bc_width] for z in range(z_pair)], axis=0
    )
    proj = jnp.concatenate([proj_ref[z, y_ref[0]] for z in range(z_pair)], axis=0)
    dt_norm, b_norm, c_norm = inverse_norms(proj.astype(f32), rank, state)
    dt_unit = dt_norm[0] * dt_norm[1]
    dt_cot = dt_grad * dt_gain_ref[...]
    dt_mean = jnp.mean(dt_cot * dt_unit, axis=1, keepdims=True)
    dt_back = dt_norm[1] * (dt_cot - dt_unit * dt_mean)
    for p in pieces:
        pack_s[p * rows : (p + 1) * rows, :] = dt_back[:, p * lane : (p + 1) * lane]
    pack_s[last:, :] = jnp.zeros((own, lane), f32)
    side = z_pair * bc_width
    free = lane - side
    dt_gain_part = jnp.sum(dt_grad * dt_unit, axis=0, keepdims=True)
    for piece in range(rank // free):
        pack_s[last + piece : last + piece + 1, side:] = dt_gain_part[
            :, piece * free : (piece + 1) * free
        ]
    gain_row = last + rank // free
    for index, part in enumerate((b_norm, c_norm)):
        start = index * state
        grad = bc_grad[:, start : start + state]
        unit = part[0] * part[1]
        cot = grad * bc_gain_ref[:, start : start + state]
        mean = jnp.mean(cot * unit, axis=1, keepdims=True)
        inner = jnp.where(part[2] > state_floor, mean, 0.0)
        inner = jnp.where(part[2] == state_floor, 0.5 * mean, inner)
        back = part[1] * (cot - unit * inner)
        for z in range(z_pair):
            place = z * bc_width + start
            pack_s[last:, place : place + state] = back[z * own : (z + 1) * own]
        pack_s[gain_row : gain_row + 1, side + start : side + start + state] = jnp.sum(
            grad * unit, axis=0, keepdims=True
        )
    sent = pack_s[...].astype(bf16)
    for peer in range(out_ref.shape[0]):
        out_ref[peer] = sent


def to_tokens(low_ref, low_s, z_pair, bc_width):
    y_size, packed_rows, _ = low_ref.shape
    own = low_s.shape[0] // (y_size * z_pair)
    pieces = packed_rows // (z_pair * own)
    for y in range(y_size):
        for z in range(z_pair):
            start = (z * y_size + y) * own
            for p in range(pieces):
                place = (p * z_pair + z) * own
                low_s[start : start + own, p * lane : (p + 1) * lane] = low_ref[
                    y, place : place + own, :
                ]
            low_s[start : start + own, pieces * lane : pieces * lane + bc_width] = low_ref[
                y, packed_rows - own :, z * bc_width : (z + 1) * bc_width
            ]


def grad_x_kernel(low_ref, xg_ref, w_xdt_ref, w_xbc_ref, grad_x_ref, low_s, *, z_pair):
    rank = w_xdt_ref.shape[0]
    bc_width = w_xbc_ref.shape[0]
    to_tokens(low_ref, low_s, z_pair, bc_width)
    summed = xg_ref[...] + jnp.dot(
        low_s[:, :rank], w_xdt_ref[...], preferred_element_type=f32
    )
    summed = summed + jnp.dot(
        low_s[:, rank : rank + bc_width], w_xbc_ref[...], preferred_element_type=f32
    )
    grad_x_ref[...] = summed.astype(bf16)


def project_kernel(
    core_ref,
    low_ref,
    x_ref,
    misc_ref,
    keep_ref,
    send_ref,
    out_s,
    all_s,
    low_s,
    *,
    rank,
    bc_width,
    z_pair,
    scale,
):
    width = x_ref.shape[1]
    y_size = low_ref.shape[0]
    own = low_s.shape[0] // (y_size * z_pair)
    to_tokens(low_ref, low_s, z_pair, bc_width)
    dt_low = low_s[:, :rank]
    bc_low = low_s[:, rank : rank + bc_width]
    out_s[:, :width] = scale * lax.dot_general(
        dt_low, x_ref[...], contract_rows, preferred_element_type=f32
    )
    state = bc_width // 2
    all_s[...] = jnp.zeros_like(all_s)
    all_s[: state + 2, :] = misc_ref[: state + 2, :]
    all_s[state + 8 : state + 8 + bc_width, :] = scale * lax.dot_general(
        bc_low, x_ref[...], contract_rows, preferred_element_type=f32
    )
    gains = jnp.zeros((own, lane), f32)
    for y in range(y_size):
        gains = gains + low_ref[y, low_ref.shape[1] - own :, :].astype(f32)
    side = z_pair * bc_width
    free = lane - side
    gains = scale * gains[:, side:]
    gain_row = state + 8 + bc_width
    for piece in range(rank // free):
        all_s[gain_row : gain_row + 1, piece * free : (piece + 1) * free] = gains[
            piece : piece + 1
        ]
    piece = rank // free
    all_s[gain_row : gain_row + 1, rank : rank + bc_width] = gains[piece : piece + 1, :bc_width]
    for piece in range(width // lane):
        out_s[piece * 64 : (piece + 1) * 64, width:] = all_s[
            :, piece * lane : (piece + 1) * lane
        ]
    split_cores(core_ref, out_s, keep_ref, send_ref)


def total_kernel(parts_ref, xdt_ref, dt_ref, own_ref):
    width = xdt_ref.shape[1]
    total = parts_ref[0].astype(f32)
    for peer in range(1, parts_ref.shape[0]):
        total = total + parts_ref[peer].astype(f32)
    xdt_ref[...] = total[:, :width]
    dt_ref[...] = total[:, width : 2 * width]
    for peer in range(own_ref.shape[0]):
        own_ref[peer] = total[:, 2 * width :].astype(bf16)


def spread_kernel(
    parts_ref, xbc_ref, alog_ref, bias_ref, skip_ref, dt_gain_ref, bc_gain_ref, all_s, *, order
):
    state = alog_ref.shape[0]
    bc_width = xbc_ref.shape[0]
    rank = dt_gain_ref.shape[1]
    for block, (peer, place) in enumerate(order):
        row, piece = 16 * (block % 4), lane * (block // 4)
        all_s[row : row + 16, piece : piece + lane] = parts_ref[
            peer, :, place * lane : (place + 1) * lane
        ].astype(f32)
    alog_ref[...] = all_s[:state, :]
    bias_ref[...] = all_s[state : state + 1, :]
    skip_ref[...] = all_s[state + 1 : state + 2, :]
    xbc_ref[...] = all_s[state + 8 : state + 8 + bc_width, :]
    gain_row = state + 8 + bc_width
    dt_gain_ref[...] = all_s[gain_row : gain_row + 1, :rank]
    bc_gain_ref[...] = all_s[gain_row : gain_row + 1, rank : rank + bc_width]


def call(kernel, name, outs, scratch, limit_mib, *args, far=()):
    in_smem = pl.BlockSpec(memory_space=pltpu.SMEM)
    in_hbm = pl.BlockSpec(memory_space=pltpu.HBM)
    return pl.pallas_call(
        kernel,
        out_shape=tuple(
            pltpu.VMEM(out[0], out[1]) if len(out) > 2 else jax.ShapeDtypeStruct(*out)
            for out in outs
        ),
        in_specs=[in_smem if arg.dtype == jnp.int32 else in_vmem for arg in args]
        + [in_hbm] * len(far),
        out_specs=tuple([in_vmem] * len(outs)),
        scratch_shapes=[pltpu.VMEM(shape, dtype) for shape, dtype in scratch]
        + [pltpu.VMEM(arg.shape, arg.dtype) for arg in far]
        + ([pltpu.SemaphoreType.DMA((len(far),))] if far else []),
        compiler_params=pltpu.CompilerParams(vmem_limit_bytes=limit_mib * 2**20),
        name=name,
    )(*args, *[pltpu.with_memory_space_constraint(arg, pltpu.HBM) for arg in far])


def send_to_all(block, axis, groups=None):
    return lax.all_to_all(block, axis, 0, 0, axis_index_groups=groups)


def sum_low(parts):
    return jnp.sum(parts.astype(f32), axis=0).astype(bf16)


def body(
    x_inner, proj_dt, proj_bc, grad_y, w_xdt, w_xbc, w_dt, dt_bias, a_log, d_skip, dt_gain, bc_gain
):
    x_rows = x_inner[0]
    gy_rows = grad_y[0]
    tokens, width = x_rows.shape
    rank = proj_dt.shape[2]
    bc_width = proj_bc.shape[2]
    state = bc_width // 2
    own = proj_dt.shape[1]
    dp = lax.axis_size("dp")
    tensor = lax.axis_size("tensor")
    scale = 1.0 / math.sqrt(dp * tokens)
    bias_row = dt_bias.reshape(1, width)
    skip_row = d_skip.reshape(1, width)
    dt_gain_row = dt_gain.reshape(1, rank)
    bc_gain_row = bc_gain.reshape(1, bc_width)

    columns = rank + lane
    cores, z_size, z_pair = 2, 4, 2
    x_size = dp // (cores * z_size)
    y_size = tensor // z_pair
    per_device = rank // dp
    other_core = [(index, index ^ 1) for index in range(dp)]
    core = (lax.axis_index("dp") % cores).astype(jnp.int32).reshape(1)
    y_index = (lax.axis_index("tensor") % y_size).astype(jnp.int32).reshape(1)
    local = True
    (own_proj,) = call(
        pack_kernel,
        "pack",
        [((tensor, own, columns), bf16, local)],
        [],
        4,
        far=(proj_dt[0], proj_bc[0]),
    )
    own_proj, core = lax.optimization_barrier((own_proj, core))
    full_proj = send_to_all(own_proj, "tensor").reshape(tokens, columns)

    z_stride, x_stride = cores, cores * z_size
    along_x = [[x * x_stride + rest for x in range(x_size)] for rest in range(x_stride)]
    along_z = [
        [x * x_stride + z * z_stride + c for z in range(z_size)]
        for x in range(x_size)
        for c in range(cores)
    ]
    along_xc = [
        [x * x_stride + z * z_stride + c for x in range(x_size) for c in range(cores)]
        for z in range(z_size)
    ]
    along_y = [[z * y_size + y for y in range(y_size)] for z in range(z_pair)]

    def swap_cores(sent):
        return lax.ppermute(sent, "dp", other_core)

    def sum_over_x(both):
        blocks = both.reshape((x_size, z_size) + both.shape[1:])
        return sum_low(send_to_all(blocks, "dp", along_x))

    rows = ((tokens, width), f32)
    packed_rows = z_pair * own * (rank // lane) + own
    by_y = (y_size, packed_rows, lane)
    half = (x_size * z_size, per_device)
    normed_part, w_kept, w_sent, xg, misc = call(
        functools.partial(scan_kernel, scale=scale, z_pair=z_pair),
        "scan",
        [
            (by_y, bf16, local),
            (half + (width,), bf16, local),
            (half + (width,), bf16, local),
            ((tokens, width), f32, local),
            ((state + 8, width), f32, local),
        ],
        [
            rows,
            rows,
            rows,
            rows,
            ((state, width), f32),
            ((tokens, rank), bf16),
            ((tokens, 2 * state, lane), f32),
            ((tokens, state, width), f32),
            ((tokens, state, lane), f32),
            ((tokens, state, lane), f32),
            rows,
            rows,
        ],
        42,
        core,
        full_proj,
        far=(dt_gain_row, bc_gain_row, w_dt, bias_row, x_rows, gy_rows, a_log, skip_row),
    )
    normed_parts = send_to_all(normed_part, "tensor", along_y)
    mine, w_both = call(
        join_kernel,
        "join",
        [((packed_rows, lane), f32, local), (half + (width,), bf16)],
        [],
        16,
        normed_parts,
        w_kept,
        swap_cores(w_sent),
    )
    w_by_x = sum_over_x(w_both)
    other = lax.ppermute(
        mine, "tensor", [(index, (index + y_size) % tensor) for index in range(tensor)]
    )
    other, w_by_x = lax.optimization_barrier((other, w_by_x))
    (own_low,) = call(
        functools.partial(norm_kernel, state=state),
        "norm",
        [(by_y, bf16, local)],
        [((packed_rows, lane), f32)],
        4,
        y_index,
        mine,
        other,
        full_proj.reshape(z_pair, y_size, own, columns),
        dt_gain_row,
        bc_gain_row,
    )
    low = send_to_all(own_low, "tensor", along_y)
    half_row = (half + (width + lane,), bf16)
    kept, sent = call(
        functools.partial(
            project_kernel, rank=rank, bc_width=bc_width, z_pair=z_pair, scale=scale
        ),
        "project",
        [(half_row[0], f32, local), half_row + (local,)],
        [
            ((rank, width + lane), f32),
            ((64, width), f32),
            ((tokens, columns), bf16),
        ],
        16,
        core,
        low,
        x_rows,
        misc,
    )
    (grad_x,) = call(
        functools.partial(grad_x_kernel, z_pair=z_pair),
        "grad_x",
        [((tokens, width), bf16)],
        [((tokens, columns), bf16)],
        16,
        low,
        xg,
        w_xdt,
        w_xbc,
    )
    swapped, grad_x = lax.optimization_barrier((swap_cores(sent), grad_x))
    by_x = sum_over_x((kept + swapped.astype(f32)).astype(bf16))
    by_z = by_x[:, :, width:].transpose(1, 0, 2).reshape(1, per_device, z_size * lane)
    by_z = jnp.broadcast_to(by_z, (z_size, per_device, z_size * lane))
    by_z = jnp.concatenate([by_x[:, :, :width], w_by_x, by_z], axis=2)
    all_parts = send_to_all(by_z, "dp", along_z)
    shared = x_size * cores
    grad_w_xdt, grad_w_dt, own_total = call(
        total_kernel,
        "total",
        [
            ((per_device, width), f32),
            ((per_device, width), f32),
            ((shared, per_device, z_size * lane), bf16, local),
        ],
        [],
        4,
        all_parts,
    )
    totals = send_to_all(own_total, "dp", along_xc)
    order = tuple(
        (x * cores + c, z) for x in range(x_size) for z in range(z_size) for c in range(cores)
    )
    grad_w_xbc, grad_a_log, bias_total, skip_total, dt_gain_total, bc_gain_total = call(
        functools.partial(spread_kernel, order=order),
        "spread",
        [
            ((bc_width, width), f32),
            ((state, width), f32),
            ((1, width), f32),
            ((1, width), f32),
            ((1, rank), f32),
            ((1, bc_width), f32),
        ],
        [((64, width), f32)],
        4,
        totals,
    )
    return (
        grad_x[None],
        grad_w_xdt,
        grad_w_dt,
        grad_w_xbc,
        grad_a_log,
        bias_total.reshape(width),
        skip_total.reshape(width),
        dt_gain_total.reshape(rank),
        bc_gain_total.reshape(bc_width),
    )


def solution(mesh):
    return jax.shard_map(
        body,
        mesh=mesh,
        in_specs=(
            P("dp", None, "tensor"),
            P("dp", "tensor", None),
            P("dp", "tensor", None),
            P("dp", None, "tensor"),
            P(None, "tensor"),
            P(None, "tensor"),
            P(None, "tensor"),
            P("tensor"),
            P(None, "tensor"),
            P("tensor"),
            P(),
            P(),
        ),
        out_specs=(
            P("dp", None, "tensor"),
            P("dp", "tensor"),
            P("dp", "tensor"),
            P(None, "tensor"),
            P(None, "tensor"),
            P("tensor"),
            P("tensor"),
            P(),
            P(),
        ),
        check_vma=False,
    )
```

```python
import functools
import math

import jax
import jax.numpy as jnp
from jax import lax
from jax.experimental import pallas as pl
from jax.experimental.pallas import tpu as pltpu
from jax.sharding import PartitionSpec as P

norm_eps = 1e-06
state_floor = 0.25
log2_e = 1.4426950408889634
lane = 128
f32 = jnp.float32
bf16 = jnp.bfloat16
contract_rows = (((0,), (0,)), ((), ()))
contract_cols = (((1,), (1,)), ((), ()))
in_vmem = pl.BlockSpec(memory_space=pltpu.VMEM)


def inverse_norms(proj, rank, state):
    dt_part = proj[:, :rank]
    b_part = proj[:, rank : rank + state]
    c_part = proj[:, rank + state : rank + 2 * state]
    dt_square = jnp.mean(dt_part * dt_part, axis=1, keepdims=True)
    b_square = jnp.mean(b_part * b_part, axis=1, keepdims=True)
    c_square = jnp.mean(c_part * c_part, axis=1, keepdims=True)
    return (
        (dt_part, lax.rsqrt(dt_square + norm_eps)),
        (b_part, lax.rsqrt(jnp.maximum(b_square, state_floor)), b_square),
        (c_part, lax.rsqrt(jnp.maximum(c_square, state_floor)), c_square),
    )


def pack_kernel(dt_in, bc_in, out_ref, dt_ref, bc_ref, arrived):
    rank, bc_width = dt_ref.shape[1], bc_ref.shape[1]
    spare = out_ref.shape[2] - rank - bc_width
    arrivals = [
        pltpu.make_async_copy(dt_in, dt_ref, arrived.at[0]),
        pltpu.make_async_copy(bc_in, bc_ref, arrived.at[1]),
    ]
    for copy in arrivals:
        copy.start()
    for copy in arrivals:
        copy.wait()
    for peer in range(out_ref.shape[0]):
        out_ref[peer, :, :rank] = dt_ref[...]
        out_ref[peer, :, rank : rank + bc_width] = bc_ref[...]
        out_ref[peer, :, rank + bc_width :] = jnp.zeros((dt_ref.shape[0], spare), bf16)


def split_cores(core_ref, whole, keep_ref, send_ref):
    first_core = core_ref[0] == 0
    for pair in range(keep_ref.shape[0]):
        even = whole[32 * pair : 32 * pair + 16]
        odd = whole[32 * pair + 16 : 32 * pair + 32]
        keep_ref[pair] = jnp.where(first_core, even, odd).astype(keep_ref.dtype)
        send_ref[pair] = jnp.where(first_core, odd, even).astype(bf16)


def scan_kernel(
    proj_ref,
    dt_gain_in,
    bc_gain_in,
    w_in,
    bias_in,
    x_in,
    gy_in,
    alog_in,
    skip_in,
    normed_ref,
    w_part_ref,
    xg_ref,
    misc_ref,
    dt_s,
    gy_s,
    src_s,
    sig_s,
    a2_s,
    low_s,
    bcb_s,
    u_s,
    b_acc,
    c_acc,
    s1_s,
    s2_s,
    dt_gain_ref,
    bc_gain_ref,
    w_ref,
    bias_ref,
    x_ref,
    gy_ref,
    alog_ref,
    skip_ref,
    arrived,
    *,
    scale,
    z_pair,
    forward_lanes=512,
    forward_rows=32,
    backward_lanes=512,
    backward_rows=16,
):
    tokens, width = x_ref.shape
    state = alog_ref.shape[0]
    rank = w_ref.shape[0]
    arrivals = [
        pltpu.make_async_copy(source, held, arrived.at[index])
        for index, (source, held) in enumerate(
            (
                (dt_gain_in, dt_gain_ref),
                (bc_gain_in, bc_gain_ref),
                (w_in, w_ref),
                (bias_in, bias_ref),
                (x_in, x_ref),
                (gy_in, gy_ref),
                (alog_in, alog_ref),
                (skip_in, skip_ref),
            )
        )
    ]
    for copy in arrivals:
        copy.start()
    b_acc[...] = jnp.zeros_like(b_acc)
    c_acc[...] = jnp.zeros_like(c_acc)
    dt_norm, b_norm, c_norm = inverse_norms(proj_ref[...].astype(f32), rank, state)
    arrivals[0].wait()
    arrivals[1].wait()
    low_s[...] = (dt_norm[0] * dt_norm[1] * dt_gain_ref[...]).astype(bf16)
    b_rows = b_norm[0] * b_norm[1] * bc_gain_ref[:, :state]
    c_rows = c_norm[0] * c_norm[1] * bc_gain_ref[:, state:]
    bcb_s[:, :state] = jnp.broadcast_to(b_rows[:, :, None], (tokens, state, lane))
    bcb_s[:, state:] = jnp.broadcast_to(c_rows[:, :, None], (tokens, state, lane))
    arrivals[2].wait()
    arrivals[3].wait()
    pre = jnp.dot(low_s[...], w_ref[...], preferred_element_type=f32) + bias_ref[...]
    small = jnp.exp(-jnp.abs(pre))
    dt_rows = jnp.maximum(pre, 0.0) + jnp.log1p(small)
    sig_s[...] = jnp.where(pre >= 0, 1.0, small) / (1.0 + small)
    for copy in arrivals[4:]:
        copy.wait()
    x_float = x_ref[...].astype(f32)
    gy_float = gy_ref[...].astype(f32)
    dt_s[...] = dt_rows
    gy_s[...] = gy_float
    src_s[...] = dt_rows * x_float
    a_mat = -jnp.exp(alog_ref[...])
    a2_s[...] = a_mat * log2_e
    def widen(part, width):
        return jnp.concatenate([part] * (width // lane), axis=1)

    def fold(part):
        total = part[:, :lane]
        for start in range(lane, part.shape[1], lane):
            total = total + part[:, start : start + lane]
        return total

    def fold_states(part):
        total = part[:8]
        for rep in range(1, state // 8):
            total = total + part[rep * 8 : (rep + 1) * 8]
        return total

    def join_rows(early, late, level):
        mine = (lax.broadcasted_iota(jnp.int32, early.shape, 0) & level) == 0
        kept = jnp.where(mine, early, late)
        moved = jnp.where(mine, late, early)
        return kept + pltpu.roll(moved, 8 - level, 0)

    wide = min(forward_lanes, width)
    for group in range(width // wide):
        cols = slice(group * wide, (group + 1) * wide)

        def forward(block, held):
            a2 = a2_s[:, cols]
            for offset in range(forward_rows):
                t = block * forward_rows + offset
                decayed = jnp.exp2(dt_s[pl.ds(t, 1), cols] * a2) * held
                u_s[pl.ds(t, 1), :, cols] = decayed[None]
                c_acc[pl.ds(t, 1)] += fold(decayed * gy_s[pl.ds(t, 1), cols])[None]
                held = decayed + src_s[pl.ds(t, 1), cols] * widen(bcb_s[t, :state], wide)
            return held

        lax.fori_loop(0, tokens // forward_rows, forward, jnp.zeros((state, wide), f32))

    wide = min(backward_lanes, width)
    for group in range(width // wide):
        cols = slice(group * wide, (group + 1) * wide)

        def backward(step, carry):
            later, a_total = carry
            a2 = a2_s[:, cols]
            for part in range(backward_rows // 8 - 1, -1, -1):
                first_row = tokens - (step + 1) * backward_rows + part * 8
                waiting = {}
                for offset in range(7, -1, -1):
                    t = first_row + offset
                    dt_now = dt_s[pl.ds(t, 1), cols]
                    adjoint = (
                        widen(bcb_s[t, state:], wide) * gy_s[pl.ds(t, 1), cols] + later
                    )
                    through = adjoint * u_s[t, :, cols]
                    first = fold_states(adjoint * widen(bcb_s[t, :state], wide))
                    second = fold_states(through * a2)
                    level = 1
                    while level in waiting:
                        later_first, later_second = waiting.pop(level)
                        first = join_rows(first, later_first, level)
                        second = join_rows(second, later_second, level)
                        level *= 2
                    waiting[level] = (first, second)
                    b_acc[pl.ds(t, 1)] += fold(adjoint * src_s[pl.ds(t, 1), cols])[None]
                    a_total = a_total + dt_now * through
                    later = jnp.exp2(dt_now * a2) * adjoint
                rows = pl.ds(pl.multiple_of(first_row, 8), 8)
                s1_s[rows, cols], s2_s[rows, cols] = waiting[8]
            return later, a_total

        zeros = jnp.zeros((state, wide), f32)
        _, a_total = lax.fori_loop(0, tokens // backward_rows, backward, (zeros, zeros))
        misc_ref[:state, cols] = (scale / log2_e) * (a_total * a2_s[:, cols])

    s1 = s1_s[...]
    xg_ref[...] = dt_s[...] * s1 + skip_ref[...] * gy_s[...]
    dt_grad = x_ref[...].astype(f32) * s1 + s2_s[...] * (1.0 / log2_e)
    pre_float = dt_grad * sig_s[...]
    pre_grad = pre_float.astype(bf16)
    misc_ref[state : state + 1, :] = scale * jnp.sum(pre_float, axis=0, keepdims=True)
    misc_ref[state + 1 : state + 2, :] = scale * jnp.sum(
        gy_s[...] * x_ref[...].astype(f32), axis=0, keepdims=True
    )
    dt_normed = lax.dot_general(
        pre_grad, w_ref[...], contract_cols, preferred_element_type=f32
    ).astype(bf16)
    w_part_ref[...] = (
        scale
        * lax.dot_general(low_s[...], pre_grad, contract_rows, preferred_element_type=f32)
    ).astype(bf16)
    source_sum = jnp.sum(src_s[...] * gy_s[...], axis=1, keepdims=True)
    b_grad = jnp.sum(b_acc[...], axis=2)
    c_grad = jnp.sum(c_acc[...], axis=2) + b_rows * source_sum
    y_size = normed_ref.shape[0]
    own = tokens // (y_size * z_pair)
    b_grad = b_grad.astype(bf16)
    c_grad = c_grad.astype(bf16)
    bc_width = 2 * state
    for y in range(y_size):
        last = normed_ref.shape[1] - own
        normed_ref[y, last:, z_pair * bc_width :] = jnp.zeros(
            (own, lane - z_pair * bc_width), bf16
        )
        for z in range(z_pair):
            rows = slice((z * y_size + y) * own, (z * y_size + y + 1) * own)
            for piece in range(rank // lane):
                place = (piece * z_pair + z) * own
                normed_ref[y, place : place + own, :] = dt_normed[
                    rows, piece * lane : (piece + 1) * lane
                ]
            start = z * bc_width
            normed_ref[y, last:, start : start + state] = b_grad[rows]
            normed_ref[y, last:, start + state : start + bc_width] = c_grad[rows]


def join_kernel(parts_ref, out_ref):
    total = parts_ref[0].astype(f32)
    for peer in range(1, parts_ref.shape[0]):
        total = total + parts_ref[peer].astype(f32)
    out_ref[...] = total


def norm_kernel(
    y_ref, mine_ref, other_ref, proj_ref, dt_gain_ref, bc_gain_ref, out_ref, pack_s, *, state
):
    rank = dt_gain_ref.shape[1]
    z_pair, _, own, _ = proj_ref.shape
    rows = z_pair * own
    last = mine_ref.shape[0] - own
    bc_width = 2 * state
    packed = mine_ref[...] + other_ref[...]
    pieces = range(rank // lane)
    dt_grad = jnp.concatenate([packed[p * rows : (p + 1) * rows] for p in pieces], axis=1)
    bc_grad = jnp.concatenate(
        [packed[last:, z * bc_width : (z + 1) * bc_width] for z in range(z_pair)], axis=0
    )
    proj = jnp.concatenate([proj_ref[z, y_ref[0]] for z in range(z_pair)], axis=0)
    dt_norm, b_norm, c_norm = inverse_norms(proj.astype(f32), rank, state)
    dt_unit = dt_norm[0] * dt_norm[1]
    dt_cot = dt_grad * dt_gain_ref[...]
    dt_mean = jnp.mean(dt_cot * dt_unit, axis=1, keepdims=True)
    dt_back = dt_norm[1] * (dt_cot - dt_unit * dt_mean)
    for p in pieces:
        pack_s[p * rows : (p + 1) * rows, :] = dt_back[:, p * lane : (p + 1) * lane]
    pack_s[last:, :] = jnp.zeros((own, lane), f32)
    side = z_pair * bc_width
    free = lane - side
    dt_gain_part = jnp.sum(dt_grad * dt_unit, axis=0, keepdims=True)
    for piece in range(rank // free):
        pack_s[last + piece : last + piece + 1, side:] = dt_gain_part[
            :, piece * free : (piece + 1) * free
        ]
    gain_row = last + rank // free
    for index, part in enumerate((b_norm, c_norm)):
        start = index * state
        grad = bc_grad[:, start : start + state]
        unit = part[0] * part[1]
        cot = grad * bc_gain_ref[:, start : start + state]
        mean = jnp.mean(cot * unit, axis=1, keepdims=True)
        inner = jnp.where(part[2] > state_floor, mean, 0.0)
        inner = jnp.where(part[2] == state_floor, 0.5 * mean, inner)
        back = part[1] * (cot - unit * inner)
        for z in range(z_pair):
            place = z * bc_width + start
            pack_s[last:, place : place + state] = back[z * own : (z + 1) * own]
        pack_s[gain_row : gain_row + 1, side + start : side + start + state] = jnp.sum(
            grad * unit, axis=0, keepdims=True
        )
    sent = pack_s[...].astype(bf16)
    for peer in range(out_ref.shape[0]):
        out_ref[peer] = sent


def to_tokens(low_ref, low_s, z_pair, bc_width):
    y_size, packed_rows, _ = low_ref.shape
    own = low_s.shape[0] // (y_size * z_pair)
    pieces = packed_rows // (z_pair * own)
    for y in range(y_size):
        for z in range(z_pair):
            start = (z * y_size + y) * own
            for p in range(pieces):
                place = (p * z_pair + z) * own
                low_s[start : start + own, p * lane : (p + 1) * lane] = low_ref[
                    y, place : place + own, :
                ]
            low_s[start : start + own, pieces * lane : pieces * lane + bc_width] = low_ref[
                y, packed_rows - own :, z * bc_width : (z + 1) * bc_width
            ]


def grad_x_kernel(low_ref, xg_ref, w_xdt_ref, w_xbc_ref, grad_x_ref, low_s, *, z_pair):
    rank = w_xdt_ref.shape[0]
    bc_width = w_xbc_ref.shape[0]
    to_tokens(low_ref, low_s, z_pair, bc_width)
    summed = xg_ref[...] + jnp.dot(
        low_s[:, :rank], w_xdt_ref[...], preferred_element_type=f32
    )
    summed = summed + jnp.dot(
        low_s[:, rank : rank + bc_width], w_xbc_ref[...], preferred_element_type=f32
    )
    grad_x_ref[...] = summed.astype(bf16)


def project_kernel(
    core_ref,
    low_ref,
    x_ref,
    w_part_ref,
    misc_ref,
    keep_ref,
    send_ref,
    out_s,
    all_s,
    low_s,
    *,
    rank,
    bc_width,
    z_pair,
    scale,
):
    width = x_ref.shape[1]
    y_size = low_ref.shape[0]
    own = low_s.shape[0] // (y_size * z_pair)
    to_tokens(low_ref, low_s, z_pair, bc_width)
    dt_low = low_s[:, :rank]
    bc_low = low_s[:, rank : rank + bc_width]
    out_s[:, :width] = scale * lax.dot_general(
        dt_low, x_ref[...], contract_rows, preferred_element_type=f32
    )
    out_s[:, width : 2 * width] = w_part_ref[...].astype(f32)
    state = bc_width // 2
    all_s[...] = jnp.zeros_like(all_s)
    all_s[: state + 2, :] = misc_ref[: state + 2, :]
    all_s[state + 8 : state + 8 + bc_width, :] = scale * lax.dot_general(
        bc_low, x_ref[...], contract_rows, preferred_element_type=f32
    )
    gains = jnp.zeros((own, lane), f32)
    for y in range(y_size):
        gains = gains + low_ref[y, low_ref.shape[1] - own :, :].astype(f32)
    side = z_pair * bc_width
    free = lane - side
    gains = scale * gains[:, side:]
    gain_row = state + 8 + bc_width
    for piece in range(rank // free):
        all_s[gain_row : gain_row + 1, piece * free : (piece + 1) * free] = gains[
            piece : piece + 1
        ]
    piece = rank // free
    all_s[gain_row : gain_row + 1, rank : rank + bc_width] = gains[piece : piece + 1, :bc_width]
    for piece in range(width // lane):
        out_s[piece * 64 : (piece + 1) * 64, 2 * width :] = all_s[
            :, piece * lane : (piece + 1) * lane
        ]
    split_cores(core_ref, out_s, keep_ref, send_ref)


def total_kernel(parts_ref, xdt_ref, dt_ref, own_ref):
    width = xdt_ref.shape[1]
    total = parts_ref[0].astype(f32)
    for peer in range(1, parts_ref.shape[0]):
        total = total + parts_ref[peer].astype(f32)
    xdt_ref[...] = total[:, :width]
    dt_ref[...] = total[:, width : 2 * width]
    for peer in range(own_ref.shape[0]):
        own_ref[peer] = total[:, 2 * width :].astype(bf16)


def spread_kernel(
    parts_ref, xbc_ref, alog_ref, bias_ref, skip_ref, dt_gain_ref, bc_gain_ref, all_s, *, order
):
    state = alog_ref.shape[0]
    bc_width = xbc_ref.shape[0]
    rank = dt_gain_ref.shape[1]
    for block, (peer, place) in enumerate(order):
        row, piece = 16 * (block % 4), lane * (block // 4)
        all_s[row : row + 16, piece : piece + lane] = parts_ref[
            peer, :, place * lane : (place + 1) * lane
        ].astype(f32)
    alog_ref[...] = all_s[:state, :]
    bias_ref[...] = all_s[state : state + 1, :]
    skip_ref[...] = all_s[state + 1 : state + 2, :]
    xbc_ref[...] = all_s[state + 8 : state + 8 + bc_width, :]
    gain_row = state + 8 + bc_width
    dt_gain_ref[...] = all_s[gain_row : gain_row + 1, :rank]
    bc_gain_ref[...] = all_s[gain_row : gain_row + 1, rank : rank + bc_width]


def call(kernel, name, outs, scratch, limit_mib, *args, far=()):
    in_smem = pl.BlockSpec(memory_space=pltpu.SMEM)
    in_hbm = pl.BlockSpec(memory_space=pltpu.HBM)
    return pl.pallas_call(
        kernel,
        out_shape=tuple(
            pltpu.VMEM(out[0], out[1]) if len(out) > 2 else jax.ShapeDtypeStruct(*out)
            for out in outs
        ),
        in_specs=[in_smem if arg.dtype == jnp.int32 else in_vmem for arg in args]
        + [in_hbm] * len(far),
        out_specs=tuple([in_vmem] * len(outs)),
        scratch_shapes=[pltpu.VMEM(shape, dtype) for shape, dtype in scratch]
        + [pltpu.VMEM(arg.shape, arg.dtype) for arg in far]
        + ([pltpu.SemaphoreType.DMA((len(far),))] if far else []),
        compiler_params=pltpu.CompilerParams(vmem_limit_bytes=limit_mib * 2**20),
        name=name,
    )(*args, *[pltpu.with_memory_space_constraint(arg, pltpu.HBM) for arg in far])


def send_to_all(block, axis, groups=None):
    return lax.all_to_all(block, axis, 0, 0, axis_index_groups=groups)


def sum_low(parts):
    return jnp.sum(parts.astype(f32), axis=0).astype(bf16)


def body(
    x_inner, proj_dt, proj_bc, grad_y, w_xdt, w_xbc, w_dt, dt_bias, a_log, d_skip, dt_gain, bc_gain
):
    x_rows = x_inner[0]
    gy_rows = grad_y[0]
    tokens, width = x_rows.shape
    rank = proj_dt.shape[2]
    bc_width = proj_bc.shape[2]
    state = bc_width // 2
    own = proj_dt.shape[1]
    dp = lax.axis_size("dp")
    tensor = lax.axis_size("tensor")
    scale = 1.0 / math.sqrt(dp * tokens)
    bias_row = dt_bias.reshape(1, width)
    skip_row = d_skip.reshape(1, width)
    dt_gain_row = dt_gain.reshape(1, rank)
    bc_gain_row = bc_gain.reshape(1, bc_width)

    columns = rank + lane
    cores, z_size, z_pair = 2, 4, 2
    x_size = dp // (cores * z_size)
    y_size = tensor // z_pair
    per_device = rank // dp
    other_core = [(index, index ^ 1) for index in range(dp)]
    core = (lax.axis_index("dp") % cores).astype(jnp.int32).reshape(1)
    y_index = (lax.axis_index("tensor") % y_size).astype(jnp.int32).reshape(1)
    local = True
    (own_proj,) = call(
        pack_kernel,
        "pack",
        [((tensor, own, columns), bf16, local)],
        [],
        4,
        far=(proj_dt[0], proj_bc[0]),
    )
    own_proj, core = lax.optimization_barrier((own_proj, core))
    full_proj = send_to_all(own_proj, "tensor").reshape(tokens, columns)

    z_stride, x_stride = cores, cores * z_size
    along_x = [[x * x_stride + rest for x in range(x_size)] for rest in range(x_stride)]
    along_z = [
        [x * x_stride + z * z_stride + c for z in range(z_size)]
        for x in range(x_size)
        for c in range(cores)
    ]
    along_xc = [
        [x * x_stride + z * z_stride + c for x in range(x_size) for c in range(cores)]
        for z in range(z_size)
    ]
    along_y = [[z * y_size + y for y in range(y_size)] for z in range(z_pair)]

    def swap_cores(sent):
        return lax.ppermute(sent, "dp", other_core)

    def sum_over_x(both):
        blocks = both.reshape((x_size, z_size) + both.shape[1:])
        return sum_low(send_to_all(blocks, "dp", along_x))

    rows = ((tokens, width), f32)
    packed_rows = z_pair * own * (rank // lane) + own
    by_y = (y_size, packed_rows, lane)
    half = (x_size * z_size, per_device)
    normed_part, w_part, xg, misc = call(
        functools.partial(scan_kernel, scale=scale, z_pair=z_pair),
        "scan",
        [
            (by_y, bf16, local),
            ((rank, width), bf16, local),
            ((tokens, width), f32, local),
            ((state + 8, width), f32, local),
        ],
        [
            rows,
            rows,
            rows,
            rows,
            ((state, width), f32),
            ((tokens, rank), bf16),
            ((tokens, 2 * state, lane), f32),
            ((tokens, state, width), f32),
            ((tokens, state, lane), f32),
            ((tokens, state, lane), f32),
            rows,
            rows,
        ],
        42,
        full_proj,
        far=(dt_gain_row, bc_gain_row, w_dt, bias_row, x_rows, gy_rows, a_log, skip_row),
    )
    normed_parts = send_to_all(normed_part, "tensor", along_y)
    (mine,) = call(
        join_kernel, "join", [((packed_rows, lane), f32, local)], [], 4, normed_parts
    )
    other = lax.ppermute(
        mine, "tensor", [(index, (index + y_size) % tensor) for index in range(tensor)]
    )
    (own_low,) = call(
        functools.partial(norm_kernel, state=state),
        "norm",
        [(by_y, bf16, local)],
        [((packed_rows, lane), f32)],
        4,
        y_index,
        mine,
        other,
        full_proj.reshape(z_pair, y_size, own, columns),
        dt_gain_row,
        bc_gain_row,
    )
    low = send_to_all(own_low, "tensor", along_y)
    half_row = (half + (2 * width + lane,), bf16)
    kept, sent = call(
        functools.partial(
            project_kernel, rank=rank, bc_width=bc_width, z_pair=z_pair, scale=scale
        ),
        "project",
        [(half_row[0], f32, local), half_row + (local,)],
        [
            ((rank, 2 * width + lane), f32),
            ((64, width), f32),
            ((tokens, columns), bf16),
        ],
        16,
        core,
        low,
        x_rows,
        w_part,
        misc,
    )
    (grad_x,) = call(
        functools.partial(grad_x_kernel, z_pair=z_pair),
        "grad_x",
        [((tokens, width), bf16)],
        [((tokens, columns), bf16)],
        16,
        low,
        xg,
        w_xdt,
        w_xbc,
    )
    swapped, grad_x = lax.optimization_barrier((swap_cores(sent), grad_x))
    by_x = sum_over_x((kept + swapped.astype(f32)).astype(bf16))
    by_z = by_x[:, :, 2 * width :].transpose(1, 0, 2).reshape(1, per_device, z_size * lane)
    by_z = jnp.broadcast_to(by_z, (z_size, per_device, z_size * lane))
    by_z = jnp.concatenate([by_x[:, :, : 2 * width], by_z], axis=2)
    all_parts = send_to_all(by_z, "dp", along_z)
    shared = x_size * cores
    grad_w_xdt, grad_w_dt, own_total = call(
        total_kernel,
        "total",
        [
            ((per_device, width), f32),
            ((per_device, width), f32),
            ((shared, per_device, z_size * lane), bf16, local),
        ],
        [],
        4,
        all_parts,
    )
    totals = send_to_all(own_total, "dp", along_xc)
    order = tuple(
        (x * cores + c, z) for x in range(x_size) for z in range(z_size) for c in range(cores)
    )
    grad_w_xbc, grad_a_log, bias_total, skip_total, dt_gain_total, bc_gain_total = call(
        functools.partial(spread_kernel, order=order),
        "spread",
        [
            ((bc_width, width), f32),
            ((state, width), f32),
            ((1, width), f32),
            ((1, width), f32),
            ((1, rank), f32),
            ((1, bc_width), f32),
        ],
        [((64, width), f32)],
        4,
        totals,
    )
    return (
        grad_x[None],
        grad_w_xdt,
        grad_w_dt,
        grad_w_xbc,
        grad_a_log,
        bias_total.reshape(width),
        skip_total.reshape(width),
        dt_gain_total.reshape(rank),
        bc_gain_total.reshape(bc_width),
    )


def solution(mesh):
    return jax.shard_map(
        body,
        mesh=mesh,
        in_specs=(
            P("dp", None, "tensor"),
            P("dp", "tensor", None),
            P("dp", "tensor", None),
            P("dp", None, "tensor"),
            P(None, "tensor"),
            P(None, "tensor"),
            P(None, "tensor"),
            P("tensor"),
            P(None, "tensor"),
            P("tensor"),
            P(),
            P(),
        ),
        out_specs=(
            P("dp", None, "tensor"),
            P("dp", "tensor"),
            P("dp", "tensor"),
            P(None, "tensor"),
            P(None, "tensor"),
            P("tensor"),
            P("tensor"),
            P(),
            P(),
        ),
        check_vma=False,
    )
```
